32 devices in a mesh: az: 16 (over z, x, core), rad: 2 (over y).
Axes of the slice: x: 2, y: 2, z: 4, core: 2. Of those that a mesh axis runs over, the one named last changes fastest.
Arguments:
- fields: float32 [5, 8, 128, 4096], P(None, None, 'rad', 'az'), may hold values from -6 to 6
- velocity: float32 [8, 128, 4096], P(None, 'rad', 'az'), may hold values from -0.5 to 0.5
- shifts: int32 [128], P('rad'), may hold values from 0 to 4095, as said below
- block_inverse: float32 [8, 128, 64], P(None, 'rad'), may hold values from -1 to 1, as said below
- coupling: float32 [8, 2], P(None, 'rad'), may hold values from 0.2 to 0.5
Outputs:
- updated: float32 [5, 8, 128, 4096], P(None, None, 'rad', 'az')
The draws below stay inside these ranges and needn't reach their ends.
Inputs may be any that keep to these rules, and one draw needn't show every extreme that they name: `shifts`: each radius's shift; the values 0 and 4095 both occur in every draw. `block_inverse`: entries of the given block inverses.
All inputs are finite; a program needn't handle non-finite values.
Results may differ from the reference program's by a relative error of at most 0.000075.
Values sent between devices are 32-bit elements; how exact they have to be, the bound alone decides.
No kernel may reach another device: no remote copies, remote signals or barrier semaphores. Data moves between devices by JAX's collectives and lax.ppermute only.
A program may use at most 256 MiB of HBM per device.

```python
import jax
import jax.numpy as jnp
from jax import lax

NF = 5
NTH = 8
NPHI = 4096
R_DEV = 64
NR = 128
N_RAD = 2


def draw_shifts(key, part):
    key_one, key_two = jax.random.split(key)
    radius = jnp.arange(NR, dtype=jnp.int32)
    profile = (NPHI - 1) * 64 // (64 + radius * 256 // NR)
    jitter = jax.random.randint(key_one, (NR,), 0, NPHI // 8)
    drawn = (profile + jitter) % NPHI
    planted = jax.random.permutation(key_two, NR)
    drawn = drawn.at[planted[0]].set(NPHI - 1)
    drawn = drawn.at[planted[1]].set(0)
    return drawn.astype(jnp.int32)


def draw_block_inverse(key, part):
    key_one, key_two = jax.random.split(key)
    key_three = jax.random.fold_in(key, 7)
    diagonal = jax.random.uniform(key_one, (NTH, NR, 1), jnp.float32, 0.5, 0.9)
    spread = jnp.clip(jax.random.normal(key_two, (NTH, NR, R_DEV), jnp.float32), -2.5, 2.5) * (0.3 / R_DEV ** 0.5)
    far_corner = jax.random.uniform(key_three, (NTH, NR, 1), jnp.float32, 0.5, 0.8)
    radial = jnp.arange(NR, dtype=jnp.int32) % R_DEV
    column = jnp.arange(R_DEV, dtype=jnp.int32)
    identity = (radial[:, None] == column[None, :]).astype(jnp.float32)[None]
    corner_mask = ((radial[:, None] == 0) & (column[None, :] == R_DEV - 1) | (radial[:, None] == R_DEV - 1) & (column[None, :] == 0)).astype(jnp.float32)[None]
    rest = 1.0 - identity - corner_mask
    return identity * diagonal + corner_mask * far_corner + rest * spread


def block_scale(rng, shape, cuts, least, top_value):
    def one(dim, shards_of):
        steps = jax.random.uniform(jax.random.fold_in(jax.random.fold_in(rng, 6), dim), (shards_of,), jnp.float32, least / len(cuts), top_value / len(cuts))
        return jnp.repeat(jnp.exp(steps), shape[dim] // shards_of).reshape((-1,) + (1,) * (len(shape) - dim - 1))

    loudness = one(*cuts[0])
    for cut in cuts[1:]:
        loudness = loudness * one(*cut)
    return loudness


def normal_values(own_key, shape, width, most, cuts=(), held_as=jnp.bfloat16):
    values = width * jax.random.normal(own_key, shape, jnp.float32)
    if cuts:
        values = values * block_scale(own_key, shape, cuts, -0.22, 0.18)
    return jnp.clip(values, -most, most).astype(held_as)


def setup_inputs(seed: int = 0) -> dict:
    streams_of = jax.random.split(jax.random.key(seed), 6)
    return {
        "fields": normal_values(streams_of[0], (NF, NTH, NR, NPHI), 1.0, 6.0, ((2, 2), (3, 16)), jnp.float32),
        "velocity": jnp.clip(jax.random.uniform(streams_of[1], (NTH, NR, NPHI), jnp.float32, -0.5, 0.5) * block_scale(streams_of[1], (NTH, NR, NPHI), ((1, 2), (2, 16)), -0.4, 0.0), -0.5, 0.5),
        "shifts": draw_shifts(jax.random.fold_in(streams_of[5], 71), 0),
        "block_inverse": draw_block_inverse(jax.random.fold_in(streams_of[5], 71), 0),
        "coupling": jnp.clip(0.2 + 0.3 * jax.random.uniform(streams_of[4], (NTH, N_RAD), jnp.float32) ** block_scale(streams_of[4], (NTH, N_RAD), ((1, 2),), -0.2, 0.2), 0.2, 0.5),
    }


def roll_rows(values, amounts):
    return jax.vmap(lambda one_row, amount: jnp.roll(one_row, amount, axis=-1), in_axes=(2, 0), out_axes=2)(values, amounts)


def interface_solve(first_row, last_row, top_left, top_right, low_left, low_right, link_rates):
    band_count = link_rates.shape[1]
    crossings = band_count - 1
    nothing = jnp.zeros_like(first_row[:, 0])
    flat_zero = jnp.zeros_like(link_rates[:, :1])
    carry_base = nothing
    carry_slope = flat_zero
    records = []
    for crossing in range(crossings):
        if crossing > 0:
            back_link = (link_rates[:, crossing - 1] * low_left[:, crossing])[:, None]
        else:
            back_link = flat_zero
        self_link = (link_rates[:, crossing] * low_right[:, crossing])[:, None]
        fore_link = (link_rates[:, crossing] * top_left[:, crossing + 1])[:, None]
        if crossing + 1 < crossings:
            next_link = (link_rates[:, crossing + 1] * top_right[:, crossing + 1])[:, None]
        else:
            next_link = flat_zero
        steepness = back_link * carry_slope + self_link
        offset = last_row[:, crossing] + back_link * carry_base
        denominator = 1.0 - fore_link * steepness
        upper_base = (first_row[:, crossing + 1] + fore_link * offset) / denominator
        upper_slope = next_link / denominator
        carry_base = offset + steepness * upper_base
        carry_slope = steepness * upper_slope
        records.append((carry_base, carry_slope, upper_base, upper_slope))
    lower_values = [nothing] * crossings
    upper_values = [nothing] * crossings
    follow = nothing
    for crossing in reversed(range(crossings)):
        carry_base, carry_slope, upper_base, upper_slope = records[crossing]
        lower_values[crossing] = carry_base + carry_slope * follow
        upper_values[crossing] = upper_base + upper_slope * follow
        follow = upper_values[crossing]
    before = jnp.stack([nothing] + lower_values, axis=1)
    beyond = jnp.stack(upper_values + [nothing], axis=1)
    return before, beyond


def reference(fields, velocity, shifts, block_inverse, coupling):
    rotated = roll_rows(fields, shifts)
    speed = velocity[None]
    ahead_cells = jnp.roll(rotated, -1, axis=3)
    outflow = jnp.maximum(speed, 0.0) * rotated + jnp.minimum(speed, 0.0) * ahead_cells
    transported = rotated - (outflow - jnp.roll(outflow, 1, axis=3))
    energy = transported[4].reshape(NTH, N_RAD, R_DEV, NPHI)
    blocks = block_inverse.reshape(NTH, N_RAD, R_DEV, R_DEV)
    local_part = jnp.einsum('zjrl,zjlp->zjrp', blocks, energy, precision=lax.Precision.HIGHEST)
    before, beyond = interface_solve(local_part[:, :, 0, :], local_part[:, :, -1, :], blocks[:, :, 0, 0], blocks[:, :, 0, -1], blocks[:, :, -1, 0], blocks[:, :, -1, -1], coupling)
    link_prev = jnp.concatenate([jnp.zeros_like(coupling[:, :1]), coupling[:, :-1]], axis=1)
    diffused = local_part + (link_prev[:, :, None] * blocks[:, :, :, 0])[..., None] * before[:, :, None, :] + (coupling[:, :, None] * blocks[:, :, :, -1])[..., None] * beyond[:, :, None, :]
    diffused = diffused.reshape(NTH, NR, NPHI)
    return jnp.concatenate([transported[:4], diffused[None]], axis=0)
```

```python
import functools

import jax
import jax.numpy as jnp
from jax import lax
from jax.experimental import pallas as pl
from jax.experimental.pallas import tpu as pltpu
from jax.sharding import PartitionSpec as P

LANES = 128
TILE_ROWS = 8


def interface_solve(first_row, last_row, top_left, top_right, low_left, low_right, link_rates):
    band_count = link_rates.shape[1]
    crossings = band_count - 1
    nothing = jnp.zeros_like(first_row[:, 0])
    flat_zero = jnp.zeros_like(link_rates[:, :1])
    carry_base = nothing
    carry_slope = flat_zero
    records = []
    for crossing in range(crossings):
        if crossing > 0:
            back_link = (link_rates[:, crossing - 1] * low_left[:, crossing])[:, None]
        else:
            back_link = flat_zero
        self_link = (link_rates[:, crossing] * low_right[:, crossing])[:, None]
        fore_link = (link_rates[:, crossing] * top_left[:, crossing + 1])[:, None]
        if crossing + 1 < crossings:
            next_link = (link_rates[:, crossing + 1] * top_right[:, crossing + 1])[:, None]
        else:
            next_link = flat_zero
        steepness = back_link * carry_slope + self_link
        offset = last_row[:, crossing] + back_link * carry_base
        denominator = 1.0 - fore_link * steepness
        upper_base = (first_row[:, crossing + 1] + fore_link * offset) / denominator
        upper_slope = next_link / denominator
        carry_base = offset + steepness * upper_base
        carry_slope = steepness * upper_slope
        records.append((carry_base, carry_slope, upper_base, upper_slope))
    lower_values = [nothing] * crossings
    upper_values = [nothing] * crossings
    follow = nothing
    for crossing in reversed(range(crossings)):
        carry_base, carry_slope, upper_base, upper_slope = records[crossing]
        lower_values[crossing] = carry_base + carry_slope * follow
        upper_values[crossing] = upper_base + upper_slope * follow
        follow = upper_values[crossing]
    before = jnp.stack([nothing] + lower_values, axis=1)
    beyond = jnp.stack(upper_values + [nothing], axis=1)
    return (before, beyond)


def turn_kernel(shift_ref, in_ref, out_ref):
    n, nf, rows, width = in_ref.shape
    per_block = width // LANES
    tiles = n * per_block
    groups = rows // TILE_ROWS
    halo_row = nf * per_block * rows
    lane = lax.broadcasted_iota(jnp.int32, (TILE_ROWS, LANES), 1)
    for group in range(groups):
        here = pl.ds(group * TILE_ROWS, TILE_ROWS)
        shift = shift_ref[here, :]
        cells = shift & (LANES - 1)
        whole = shift >> 7
        source = (lane - cells) & (LANES - 1)
        own = lane >= cells

        def one_field(field, _, group=group, here=here, whole=whole, source=source, own=own):
            turned = []
            for tile in range(tiles):
                block, part = divmod(tile, per_block)
                values = in_ref[block, field, here, part * LANES : (part + 1) * LANES]
                turned.append(jnp.take_along_axis(values, source, axis=1, mode="promise_in_bounds"))
            circle = [jnp.where(own, turned[tile], turned[tile - 1]) for tile in range(tiles)]
            step = 1
            while step < tiles:
                wanted = (whole & step) != 0
                circle = [
                    jnp.where(wanted, circle[(tile - step) % tiles], circle[tile]) for tile in range(tiles)
                ]
                step *= 2
            for tile in range(tiles):
                block, part = divmod(tile, per_block)
                row = (field * per_block + part) * rows + group * TILE_ROWS
                out_ref[block, pl.ds(pl.multiple_of(row, TILE_ROWS), TILE_ROWS), :] = circle[tile]
            place = (field * groups + group) * 2
            edge = (lane == place) | (lane == place + 1)
            for block in range(n):
                left = circle[(block * per_block - 1) % tiles]
                right = circle[((block + 1) * per_block) % tiles]
                both = pltpu.roll(jnp.where(lane == 0, right, left), place + 1, 1)
                target = out_ref.at[block, halo_row : halo_row + TILE_ROWS, :]
                target[...] = jnp.where(edge, both, target[...])
            return 0

        if group == 0:
            for block in range(n):
                out_ref[block, halo_row : halo_row + TILE_ROWS, :] = jnp.zeros(
                    (TILE_ROWS, LANES), jnp.float32
                )
        lax.fori_loop(0, nf, one_field, 0)


def turn(shift_rows, gathered):
    n, nf, rows, width = gathered.shape
    out_rows = nf * (width // LANES) * rows + TILE_ROWS
    size = gathered.size * 4
    return pl.pallas_call(
        turn_kernel,
        out_shape=jax.ShapeDtypeStruct((n, out_rows, LANES), jnp.float32),
        in_specs=[pl.BlockSpec(memory_space=pltpu.VMEM)] * 2,
        out_specs=pl.BlockSpec(memory_space=pltpu.VMEM),
        compiler_params=pltpu.CompilerParams(vmem_limit_bytes=32 * 1024 * 1024),
        cost_estimate=pl.CostEstimate(flops=10 * gathered.size, bytes_accessed=2 * size, transcendentals=0),
    )(shift_rows, gathered)


def carry_kernel(nf, rows, recv_ref, speed_ref, back_ref, *rest):
    out_ref = rest[-1]
    pieces = recv_ref.shape[0]
    width = speed_ref.shape[-1]
    per_block = width // LANES
    groups = rows // TILE_ROWS
    halo_row = nf * per_block * rows
    lane = lax.broadcasted_iota(jnp.int32, (TILE_ROWS, LANES), 1)
    first = lane == 0
    last = lane == LANES - 1
    for piece in range(pieces):
        halo = recv_ref[piece, halo_row : halo_row + TILE_ROWS, :]
        for group in range(groups):
            at = piece * rows + group * TILE_ROWS
            fore = []
            for part in range(per_block):
                cut = (slice(at, at + TILE_ROWS), slice(part * LANES, (part + 1) * LANES))
                speed = speed_ref[(0,) + cut]
                back = back_ref[(0,) + cut]
                fore.append(
                    (
                        jnp.maximum(speed, 0.0),
                        jnp.minimum(speed, 0.0),
                        jnp.maximum(back, 0.0),
                        jnp.minimum(back, 0.0),
                    )
                )
            for field in range(nf):
                values = []
                for part in range(per_block):
                    row = (field * per_block + part) * rows + group * TILE_ROWS
                    values.append(recv_ref[piece, row : row + TILE_ROWS, :])
                place = (field * groups + group) * 2
                up = [pltpu.roll(halo, (LANES - place) % LANES, 1)]
                up += [pltpu.roll(one, 1, 1) for one in values]
                down = [pltpu.roll(one, LANES - 1, 1) for one in values]
                down.append(pltpu.roll(halo, (LANES - 2 - place) % LANES, 1))
                for part in range(per_block):
                    here = values[part]
                    behind = jnp.where(first, up[part], up[part + 1])
                    ahead = jnp.where(last, down[part + 1], down[part])
                    plus, minus, back_plus, back_minus = fore[part]
                    outflow = plus * here + minus * ahead
                    inflow = back_plus * behind + back_minus * here
                    out_ref[field, 0, at : at + TILE_ROWS, part * LANES : (part + 1) * LANES] = here - (
                        outflow - inflow
                    )
    if len(rest) == 2:
        out_ref[nf, 0] = rest[0][0]


def carry(nf, received, speed, back_speed, *energy):
    n, in_rows, _ = received.shape
    levels, radii, width = speed.shape
    rows = levels * radii // n
    pieces = n // levels
    plane = pl.BlockSpec((1, radii, width), lambda level: (level, 0, 0))
    out_fields = nf + len(energy)
    size = speed.size * 4
    return pl.pallas_call(
        functools.partial(carry_kernel, nf, rows),
        grid=(levels,),
        out_shape=jax.ShapeDtypeStruct((out_fields, levels, radii, width), jnp.float32),
        in_specs=[
            pl.BlockSpec((pieces, in_rows, LANES), lambda level: (level, 0, 0)),
            plane,
            plane,
        ]
        + [plane] * len(energy),
        out_specs=pl.BlockSpec((out_fields, 1, radii, width), lambda level: (0, level, 0, 0)),
        compiler_params=pltpu.CompilerParams(vmem_limit_bytes=32 * 1024 * 1024),
        cost_estimate=pl.CostEstimate(
            flops=10 * nf * speed.size, bytes_accessed=(2 * out_fields + 2) * size, transcendentals=0
        ),
    )(received, speed, back_speed, *energy)


def exchange(blocks):
    return lax.all_to_all(blocks, "az", split_axis=0, concat_axis=0, tiled=True)


def per_device(fields, velocity, shifts, block_inverse, coupling):
    n = lax.axis_size("az")
    nf, levels, radii, width = fields.shape
    rows = levels * radii // n
    me = lax.axis_index("az")

    energy_blocks = exchange(fields[nf - 1].reshape(n, 1, rows, width))
    rest_blocks = exchange(fields[: nf - 1].reshape(nf - 1, n, rows, width).transpose(1, 0, 2, 3))

    own_shifts = lax.dynamic_slice_in_dim(shifts, (me * rows) % radii, rows)
    shift_rows = jnp.broadcast_to(own_shifts[:, None], (rows, LANES))
    edge_speed = lax.ppermute(velocity[:, :, -1], "az", [(i, (i + 1) % n) for i in range(n)])
    back_speed = jnp.concatenate([edge_speed[:, :, None], velocity[:, :, :-1]], axis=2)

    corners = jnp.stack(
        [
            block_inverse[:, 0, 0],
            block_inverse[:, 0, -1],
            block_inverse[:, -1, 0],
            block_inverse[:, -1, -1],
            coupling[:, 0],
        ],
        axis=1,
    )
    corner_all = lax.all_gather(corners, "rad", axis=1)

    energy_turned = exchange(turn(shift_rows, energy_blocks))
    rest_turned = exchange(turn(shift_rows, rest_blocks))

    energy = carry(1, energy_turned, velocity, back_speed)[0]
    local_part = jnp.einsum("zrl,zlp->zrp", block_inverse, energy, precision=lax.Precision.HIGHEST)
    ends = lax.all_gather(jnp.stack([local_part[:, 0, :], local_part[:, -1, :]], axis=0), "rad", axis=2)
    link_all = corner_all[..., 4]
    before, beyond = interface_solve(
        ends[0],
        ends[1],
        corner_all[..., 0],
        corner_all[..., 1],
        corner_all[..., 2],
        corner_all[..., 3],
        link_all,
    )
    band_index = lax.axis_index("rad")
    before_own = lax.dynamic_index_in_dim(before, band_index, 1, keepdims=False)
    beyond_own = lax.dynamic_index_in_dim(beyond, band_index, 1, keepdims=False)
    link_prev = jnp.concatenate([jnp.zeros_like(link_all[:, :1]), link_all[:, :-1]], axis=1)
    prev_own = lax.dynamic_index_in_dim(link_prev, band_index, 1, keepdims=False)
    link_own = coupling[:, 0]
    diffused = (
        local_part
        + (prev_own[:, None] * block_inverse[:, :, 0])[:, :, None] * before_own[:, None, :]
        + (link_own[:, None] * block_inverse[:, :, -1])[:, :, None] * beyond_own[:, None, :]
    )
    return carry(nf - 1, rest_turned, velocity, back_speed, diffused)


def solution(mesh):
    placed = (
        P(None, None, "rad", "az"),
        P(None, "rad", "az"),
        P("rad"),
        P(None, "rad", None),
        P(None, "rad"),
    )
    return jax.shard_map(
        per_device,
        mesh=mesh,
        in_specs=placed,
        out_specs=P(None, None, "rad", "az"),
        check_vma=False,
    )
```

```python
import functools

import jax
import jax.numpy as jnp
from jax import lax
from jax.experimental import pallas as pl
from jax.experimental.pallas import tpu as pltpu
from jax.sharding import PartitionSpec as P

LANES = 128
TILE_ROWS = 8


def interface_solve(first_row, last_row, top_left, top_right, low_left, low_right, link_rates):
    band_count = link_rates.shape[1]
    crossings = band_count - 1
    nothing = jnp.zeros_like(first_row[:, 0])
    flat_zero = jnp.zeros_like(link_rates[:, :1])
    carry_base = nothing
    carry_slope = flat_zero
    records = []
    for crossing in range(crossings):
        if crossing > 0:
            back_link = (link_rates[:, crossing - 1] * low_left[:, crossing])[:, None]
        else:
            back_link = flat_zero
        self_link = (link_rates[:, crossing] * low_right[:, crossing])[:, None]
        fore_link = (link_rates[:, crossing] * top_left[:, crossing + 1])[:, None]
        if crossing + 1 < crossings:
            next_link = (link_rates[:, crossing + 1] * top_right[:, crossing + 1])[:, None]
        else:
            next_link = flat_zero
        steepness = back_link * carry_slope + self_link
        offset = last_row[:, crossing] + back_link * carry_base
        denominator = 1.0 - fore_link * steepness
        upper_base = (first_row[:, crossing + 1] + fore_link * offset) / denominator
        upper_slope = next_link / denominator
        carry_base = offset + steepness * upper_base
        carry_slope = steepness * upper_slope
        records.append((carry_base, carry_slope, upper_base, upper_slope))
    lower_values = [nothing] * crossings
    upper_values = [nothing] * crossings
    follow = nothing
    for crossing in reversed(range(crossings)):
        carry_base, carry_slope, upper_base, upper_slope = records[crossing]
        lower_values[crossing] = carry_base + carry_slope * follow
        upper_values[crossing] = upper_base + upper_slope * follow
        follow = upper_values[crossing]
    before = jnp.stack([nothing] + lower_values, axis=1)
    beyond = jnp.stack(upper_values + [nothing], axis=1)
    return (before, beyond)


def turn_fields(shift_ref, blocks, outs, nf):
    n = len(blocks)
    rows, width = blocks[0].shape[-2:]
    per_block = width // LANES
    tiles = n * per_block
    groups = rows // TILE_ROWS
    halo_row = nf * per_block * rows
    lane = lax.broadcasted_iota(jnp.int32, (TILE_ROWS, LANES), 1)
    for block in range(n):
        outs[block][halo_row : halo_row + TILE_ROWS, :] = jnp.zeros((TILE_ROWS, LANES), jnp.float32)
    for group in range(groups):
        here = pl.ds(group * TILE_ROWS, TILE_ROWS)
        shift = shift_ref[here, :]
        cells = shift & (LANES - 1)
        whole = shift >> 7
        source = (lane - cells) & (LANES - 1)
        own = lane >= cells

        def one_field(field, _, group=group, here=here, whole=whole, source=source, own=own):
            turned = []
            for tile in range(tiles):
                block, part = divmod(tile, per_block)
                values = blocks[block][field, here, part * LANES : (part + 1) * LANES]
                turned.append(jnp.take_along_axis(values, source, axis=1, mode="promise_in_bounds"))
            circle = [jnp.where(own, turned[tile], turned[tile - 1]) for tile in range(tiles)]
            step = 1
            while step < tiles:
                wanted = (whole & step) != 0
                circle = [
                    jnp.where(wanted, circle[(tile - step) % tiles], circle[tile]) for tile in range(tiles)
                ]
                step *= 2
            for tile in range(tiles):
                block, part = divmod(tile, per_block)
                row = (field * per_block + part) * rows + group * TILE_ROWS
                outs[block][pl.ds(pl.multiple_of(row, TILE_ROWS), TILE_ROWS), :] = circle[tile]
            place = (field * groups + group) * 2
            edge = (lane == place) | (lane == place + 1)
            for block in range(n):
                left = circle[(block * per_block - 1) % tiles]
                right = circle[((block + 1) * per_block) % tiles]
                both = pltpu.roll(jnp.where(lane == 0, right, left), place + 1, 1)
                target = outs[block].at[halo_row : halo_row + TILE_ROWS, :]
                target[...] = jnp.where(edge, both, target[...])
            return 0

        lax.fori_loop(0, nf, one_field, 0)


def turn_kernel(shift_ref, in_ref, out_ref):
    n, nf = in_ref.shape[:2]
    turn_fields(shift_ref, [in_ref.at[i] for i in range(n)], [out_ref.at[i] for i in range(n)], nf)


def turn_apart_kernel(shift_ref, *refs):
    n = len(refs) // 2
    turn_fields(shift_ref, [refs[i].reshape((1,) + refs[i].shape) for i in range(n)], refs[n:], 1)


VMEM_SPEC = pl.BlockSpec(memory_space=pltpu.VMEM)
ROOMY = pltpu.CompilerParams(vmem_limit_bytes=32 * 1024 * 1024)


def turn(shift_rows, gathered):
    n, nf, rows, width = gathered.shape
    out_rows = nf * (width // LANES) * rows + TILE_ROWS
    size = gathered.size * 4
    return pl.pallas_call(
        turn_kernel,
        out_shape=jax.ShapeDtypeStruct((n, out_rows, LANES), jnp.float32),
        in_specs=[VMEM_SPEC] * 2,
        out_specs=VMEM_SPEC,
        compiler_params=ROOMY,
        cost_estimate=pl.CostEstimate(flops=10 * gathered.size, bytes_accessed=2 * size, transcendentals=0),
    )(shift_rows, gathered)


def turn_apart(shift_rows, blocks):
    n = len(blocks)
    rows, width = blocks[0].shape
    out_rows = (width // LANES) * rows + TILE_ROWS
    size = n * rows * width
    return pl.pallas_call(
        turn_apart_kernel,
        out_shape=[jax.ShapeDtypeStruct((out_rows, LANES), jnp.float32)] * n,
        in_specs=[VMEM_SPEC] * (n + 1),
        out_specs=[VMEM_SPEC] * n,
        compiler_params=ROOMY,
        cost_estimate=pl.CostEstimate(flops=10 * size, bytes_accessed=8 * size, transcendentals=0),
    )(shift_rows, *blocks)


def split_kernel(me_ref, in_ref, *rest):
    outs, sems = rest[:-1], rest[-1]
    n = len(outs)
    copies = []
    for distance in range(n):
        owner = lax.rem(me_ref[0] + distance, n)
        copies.append(
            pltpu.make_async_copy(
                in_ref.at[in_ref.shape[0] - 1, owner], outs[distance], sems.at[distance]
            )
        )
    for copy in copies:
        copy.start()
    for copy in copies:
        copy.wait()


def split(me, blocked):
    _, n, rows, width = blocked.shape
    return pl.pallas_call(
        split_kernel,
        out_shape=[jax.ShapeDtypeStruct((rows, width), jnp.float32)] * n,
        in_specs=[pl.BlockSpec(memory_space=pltpu.SMEM), pl.BlockSpec(memory_space=pl.ANY)],
        out_specs=[VMEM_SPEC] * n,
        scratch_shapes=[pltpu.SemaphoreType.DMA((n,))],
        compiler_params=ROOMY,
        cost_estimate=pl.CostEstimate(flops=0, bytes_accessed=8 * n * rows * width, transcendentals=0),
    )(me, blocked)


def send_apart(blocks):
    n = len(blocks)
    return [blocks[0]] + [
        lax.ppermute(blocks[distance], "az", [(i, (i + distance) % n) for i in range(n)])
        for distance in range(1, n)
    ]


def carry_piece(nf, recv, speed, back, store):
    rows, width = speed.shape
    per_block = width // LANES
    groups = rows // TILE_ROWS
    halo_row = nf * per_block * rows
    lane = lax.broadcasted_iota(jnp.int32, (TILE_ROWS, LANES), 1)
    first = lane == 0
    last = lane == LANES - 1
    halo = recv[halo_row : halo_row + TILE_ROWS, :]
    for group in range(groups):
        at = slice(group * TILE_ROWS, (group + 1) * TILE_ROWS)
        rates = []
        for part in range(per_block):
            cut = (at, slice(part * LANES, (part + 1) * LANES))
            ahead_speed = speed[cut]
            back_speed = back[cut]
            rates.append(
                (
                    jnp.maximum(ahead_speed, 0.0),
                    jnp.minimum(ahead_speed, 0.0),
                    jnp.maximum(back_speed, 0.0),
                    jnp.minimum(back_speed, 0.0),
                )
            )
        for field in range(nf):
            values = []
            for part in range(per_block):
                row = (field * per_block + part) * rows + group * TILE_ROWS
                values.append(recv[row : row + TILE_ROWS, :])
            place = (field * groups + group) * 2
            up = [pltpu.roll(halo, (LANES - place) % LANES, 1)]
            up += [pltpu.roll(one, 1, 1) for one in values]
            down = [pltpu.roll(one, LANES - 1, 1) for one in values]
            down.append(pltpu.roll(halo, (LANES - 2 - place) % LANES, 1))
            for part in range(per_block):
                here = values[part]
                behind = jnp.where(first, up[part], up[part + 1])
                ahead = jnp.where(last, down[part + 1], down[part])
                plus, minus, back_plus, back_minus = rates[part]
                outflow = plus * here + minus * ahead
                inflow = back_plus * behind + back_minus * here
                store(field, group * TILE_ROWS, part * LANES, here - (outflow - inflow))


def carry_kernel(nf, rows, recv_ref, speed_ref, back_ref, energy_ref, out_ref):
    for piece in range(recv_ref.shape[0]):
        here = pl.ds(piece * rows, rows)

        def store(field, row, cell, values, piece=piece):
            row += piece * rows
            out_ref[field, 0, row : row + TILE_ROWS, cell : cell + LANES] = values

        carry_piece(nf, recv_ref.at[piece], speed_ref.at[0, here], back_ref.at[0, here], store)
    out_ref[nf, 0] = energy_ref[0]


def carry(received, speed, back_speed, energy):
    n, in_rows, _ = received.shape
    levels, radii, width = speed.shape
    rows = levels * radii // n
    nf = (in_rows - TILE_ROWS) * LANES // (rows * width)
    pieces = n // levels
    plane = pl.BlockSpec((1, radii, width), lambda level: (level, 0, 0))
    size = speed.size * 4
    return pl.pallas_call(
        functools.partial(carry_kernel, nf, rows),
        grid=(levels,),
        out_shape=jax.ShapeDtypeStruct((nf + 1, levels, radii, width), jnp.float32),
        in_specs=[pl.BlockSpec((pieces, in_rows, LANES), lambda level: (level, 0, 0)), plane, plane, plane],
        out_specs=pl.BlockSpec((nf + 1, 1, radii, width), lambda level: (0, level, 0, 0)),
        compiler_params=ROOMY,
        cost_estimate=pl.CostEstimate(
            flops=10 * nf * speed.size, bytes_accessed=(2 * nf + 4) * size, transcendentals=0
        ),
    )(received, speed, back_speed, energy)


def carry_apart_kernel(me_ref, speed_ref, back_ref, *refs):
    out_ref = refs[-1]
    n = len(refs) - 1
    rows = speed_ref.shape[1]
    for distance in range(n):
        owner = lax.rem(me_ref[0] + (n - distance), n)

        def store(field, row, cell, values, owner=owner):
            out_ref[owner, row : row + TILE_ROWS, cell : cell + LANES] = values

        carry_piece(1, refs[distance], speed_ref.at[owner], back_ref.at[owner], store)


def carry_apart(me, speed, back_speed, received):
    n = len(received)
    levels, radii, width = speed.shape
    shape = (n, levels * radii // n, width)
    return pl.pallas_call(
        carry_apart_kernel,
        out_shape=jax.ShapeDtypeStruct(shape, jnp.float32),
        in_specs=[pl.BlockSpec(memory_space=pltpu.SMEM)] + [VMEM_SPEC] * (n + 2),
        out_specs=VMEM_SPEC,
        compiler_params=ROOMY,
        cost_estimate=pl.CostEstimate(
            flops=10 * speed.size, bytes_accessed=16 * speed.size, transcendentals=0
        ),
    )(me, speed.reshape(shape), back_speed.reshape(shape), *received).reshape(speed.shape)


def exchange(blocks):
    return lax.all_to_all(blocks, "az", split_axis=0, concat_axis=0, tiled=True)


def per_device(fields, velocity, shifts, block_inverse, coupling):
    n = lax.axis_size("az")
    nf, levels, radii, width = fields.shape
    rows = levels * radii // n
    me = lax.axis_index("az")

    me_scalar = me[None].astype(jnp.int32)
    blocked = fields.reshape(nf, n, rows, width)

    energy_blocks = send_apart(split(me_scalar, blocked))
    rest_blocks = exchange(blocked[: nf - 1].transpose(1, 0, 2, 3))

    own_shifts = lax.dynamic_slice_in_dim(shifts, (me * rows) % radii, rows)
    shift_rows = jnp.broadcast_to(own_shifts[:, None], (rows, LANES))
    edge_speed = lax.ppermute(velocity[:, :, -1], "az", [(i, (i + 1) % n) for i in range(n)])
    back_speed = jnp.concatenate([edge_speed[:, :, None], velocity[:, :, :-1]], axis=2)

    corners = jnp.stack(
        [
            block_inverse[:, 0, 0],
            block_inverse[:, 0, -1],
            block_inverse[:, -1, 0],
            block_inverse[:, -1, -1],
            coupling[:, 0],
        ],
        axis=1,
    )
    corner_all = lax.all_gather(corners, "rad", axis=1)
    energy_blocks, back_speed, corner_all = lax.optimization_barrier((energy_blocks, back_speed, corner_all))

    ordered = [energy_blocks[(n - m) % n] for m in range(n)]
    energy_turned = send_apart(turn_apart(shift_rows, ordered))
    rest_turned = exchange(turn(shift_rows, rest_blocks))

    energy = carry_apart(me_scalar, velocity, back_speed, energy_turned)
    local_part = jnp.einsum("zrl,zlp->zrp", block_inverse, energy, precision=lax.Precision.HIGHEST)
    ends = lax.all_gather(jnp.stack([local_part[:, 0, :], local_part[:, -1, :]], axis=0), "rad", axis=2)
    link_all = corner_all[..., 4]
    before, beyond = interface_solve(
        ends[0],
        ends[1],
        corner_all[..., 0],
        corner_all[..., 1],
        corner_all[..., 2],
        corner_all[..., 3],
        link_all,
    )
    band_index = lax.axis_index("rad")
    before_own = lax.dynamic_index_in_dim(before, band_index, 1, keepdims=False)
    beyond_own = lax.dynamic_index_in_dim(beyond, band_index, 1, keepdims=False)
    link_prev = jnp.concatenate([jnp.zeros_like(link_all[:, :1]), link_all[:, :-1]], axis=1)
    prev_own = lax.dynamic_index_in_dim(link_prev, band_index, 1, keepdims=False)
    link_own = coupling[:, 0]
    diffused = (
        local_part
        + (prev_own[:, None] * block_inverse[:, :, 0])[:, :, None] * before_own[:, None, :]
        + (link_own[:, None] * block_inverse[:, :, -1])[:, :, None] * beyond_own[:, None, :]
    )
    return carry(rest_turned, velocity, back_speed, diffused)


def solution(mesh):
    placed = (
        P(None, None, "rad", "az"),
        P(None, "rad", "az"),
        P("rad"),
        P(None, "rad", None),
        P(None, "rad"),
    )
    return jax.shard_map(
        per_device,
        mesh=mesh,
        in_specs=placed,
        out_specs=P(None, None, "rad", "az"),
        check_vma=False,
    )
```

```python
import functools

import jax
import jax.numpy as jnp
from jax import lax
from jax.experimental import pallas as pl
from jax.experimental.pallas import tpu as pltpu
from jax.sharding import PartitionSpec as P

LANES = 128
TILE_ROWS = 8
IN_VMEM = pl.BlockSpec(memory_space=pltpu.VMEM)
IN_HBM = pl.BlockSpec(memory_space=pltpu.HBM)
IN_SMEM = pl.BlockSpec(memory_space=pltpu.SMEM)
ROOMY = pltpu.CompilerParams(vmem_limit_bytes=40 * 1024 * 1024)


def cost(flops, moved):
    return pl.CostEstimate(flops=flops, bytes_accessed=4 * moved, transcendentals=0)


def copy_each(copies):
    for copy in copies:
        copy.start()
    for copy in copies:
        copy.wait()


def pack_kernel(in_ref, out_ref, sems):
    copy_each(
        [
            pltpu.make_async_copy(in_ref.at[field], out_ref.at[:, field], sems.at[field])
            for field in range(in_ref.shape[0])
        ]
    )


def pack(blocked):
    nf, n, rows, width = blocked.shape
    return pl.pallas_call(
        pack_kernel,
        out_shape=jax.ShapeDtypeStruct((n, nf, rows, width), jnp.float32),
        in_specs=[IN_HBM],
        out_specs=IN_HBM,
        scratch_shapes=[pltpu.SemaphoreType.DMA((nf,))],
        compiler_params=ROOMY,
        cost_estimate=cost(0, 2 * blocked.size),
    )(blocked)


def turn_kernel(shift_ref, in_ref, out_ref, held, sems):
    n, nf, rows, width = in_ref.shape
    per_block = width // LANES
    tiles = n * per_block
    groups = rows // TILE_ROWS
    field_rows = per_block * rows
    halo_row = nf * field_rows
    lane = lax.broadcasted_iota(jnp.int32, (TILE_ROWS, LANES), 1)

    def field_copy(field):
        part = pl.ds(pl.multiple_of(field * field_rows, TILE_ROWS), field_rows)
        return pltpu.make_async_copy(held.at[:, part, :], out_ref.at[:, part, :], sems.at[field])

    for block in range(n):
        held[block, halo_row : halo_row + TILE_ROWS, :] = jnp.zeros((TILE_ROWS, LANES), jnp.float32)

    def one_group(index, _):
        field = index // groups
        group = index % groups
        here = pl.ds(pl.multiple_of(group * TILE_ROWS, TILE_ROWS), TILE_ROWS)
        shift = shift_ref[here, :]
        cells = shift & (LANES - 1)
        whole = shift >> 7
        source = (lane - cells) & (LANES - 1)
        own = lane >= cells
        turned = []
        for tile in range(tiles):
            block, part = divmod(tile, per_block)
            values = in_ref[block, field, here, part * LANES : (part + 1) * LANES]
            turned.append(jnp.take_along_axis(values, source, axis=1, mode="promise_in_bounds"))
        circle = [jnp.where(own, turned[tile], turned[tile - 1]) for tile in range(tiles)]
        step = 1
        while step < tiles:
            wanted = (whole & step) != 0
            circle = [jnp.where(wanted, circle[(tile - step) % tiles], circle[tile]) for tile in range(tiles)]
            step *= 2
        for tile in range(tiles):
            block, part = divmod(tile, per_block)
            row = field * field_rows + part * rows + group * TILE_ROWS
            held[block, pl.ds(pl.multiple_of(row, TILE_ROWS), TILE_ROWS), :] = circle[tile]
        place = index * 2
        edge = (lane == place) | (lane == place + 1)
        for block in range(n):
            left = circle[(block * per_block - 1) % tiles]
            right = circle[((block + 1) * per_block) % tiles]
            both = pltpu.roll(jnp.where(lane == 0, right, left), place + 1, 1)
            target = held.at[block, halo_row : halo_row + TILE_ROWS, :]
            target[...] = jnp.where(edge, both, target[...])

        @pl.when(group == groups - 1)
        def _():
            field_copy(field).start()

        return 0

    lax.fori_loop(0, nf * groups, one_group, 0)
    halo = pl.ds(halo_row, TILE_ROWS)
    halo_copy = pltpu.make_async_copy(held.at[:, halo, :], out_ref.at[:, halo, :], sems.at[nf])
    halo_copy.start()
    for field in range(nf):
        field_copy(field).wait()
    halo_copy.wait()


def turn(shift_rows, gathered):
    n, nf, rows, width = gathered.shape
    shape = (n, nf * (width // LANES) * rows + TILE_ROWS, LANES)
    return pl.pallas_call(
        turn_kernel,
        out_shape=jax.ShapeDtypeStruct(shape, jnp.float32),
        in_specs=[IN_VMEM] * 2,
        out_specs=IN_HBM,
        scratch_shapes=[pltpu.VMEM(shape, jnp.float32), pltpu.SemaphoreType.DMA((nf + 1,))],
        compiler_params=ROOMY,
        cost_estimate=cost(10 * gathered.size, 2 * gathered.size),
    )(shift_rows, gathered)


def carry_piece(fields, halo_row, recv, speed, back, store):
    rows, width = speed.shape
    per_block = width // LANES
    groups = rows // TILE_ROWS
    lane = lax.broadcasted_iota(jnp.int32, (TILE_ROWS, LANES), 1)
    first = lane == 0
    last = lane == LANES - 1
    halo = recv[halo_row : halo_row + TILE_ROWS, :]
    for group in range(groups):
        at = slice(group * TILE_ROWS, (group + 1) * TILE_ROWS)
        rates = []
        for part in range(per_block):
            cut = (at, slice(part * LANES, (part + 1) * LANES))
            ahead_speed = speed[cut]
            back_speed = back[cut]
            rates.append(
                (
                    jnp.maximum(ahead_speed, 0.0),
                    jnp.minimum(ahead_speed, 0.0),
                    jnp.maximum(back_speed, 0.0),
                    jnp.minimum(back_speed, 0.0),
                )
            )
        for field in fields:
            values = []
            for part in range(per_block):
                row = (field * per_block + part) * rows + group * TILE_ROWS
                values.append(recv[row : row + TILE_ROWS, :])
            place = (field * groups + group) * 2
            up = [pltpu.roll(halo, (LANES - place) % LANES, 1)]
            up += [pltpu.roll(one, 1, 1) for one in values]
            down = [pltpu.roll(one, LANES - 1, 1) for one in values]
            down.append(pltpu.roll(halo, (LANES - 2 - place) % LANES, 1))
            for part in range(per_block):
                here = values[part]
                behind = jnp.where(first, up[part], up[part + 1])
                ahead = jnp.where(last, down[part + 1], down[part])
                plus, minus, back_plus, back_minus = rates[part]
                outflow = plus * here + minus * ahead
                inflow = back_plus * behind + back_minus * here
                store(field, group * TILE_ROWS, part * LANES, here - (outflow - inflow))


def energy_kernel(recv_ref, speed_ref, back_ref, inverse_ref, local_ref, ends_ref, moved):
    n, in_rows, _ = recv_ref.shape
    levels, radii, width = speed_ref.shape
    pieces = n // levels
    rows = radii // pieces
    field = (in_rows - TILE_ROWS) * LANES // (rows * width) - 1

    def one_level(level, _):
        for piece in range(pieces):
            part = pl.ds(piece * rows, rows)

            def store(_, row, cell, values, piece=piece):
                row += piece * rows
                moved[row : row + TILE_ROWS, cell : cell + LANES] = values

            carry_piece(
                [field],
                in_rows - TILE_ROWS,
                recv_ref.at[level * pieces + piece],
                speed_ref.at[level, part],
                back_ref.at[level, part],
                store,
            )
        local = jnp.dot(
            inverse_ref[level],
            moved[...],
            precision=lax.Precision.HIGHEST,
            preferred_element_type=jnp.float32,
        )
        local_ref[level] = local
        ends_ref[0, pl.ds(level, 1), :] = local[:1]
        ends_ref[1, pl.ds(level, 1), :] = local[-1:]
        return 0

    lax.fori_loop(0, levels, one_level, 0)


def energy_part(received, speed, back_speed, inverse):
    levels, radii, width = speed.shape
    return pl.pallas_call(
        energy_kernel,
        out_shape=[
            jax.ShapeDtypeStruct(speed.shape, jnp.float32),
            jax.ShapeDtypeStruct((2, levels, width), jnp.float32),
        ],
        in_specs=[IN_VMEM] * 4,
        out_specs=[IN_VMEM] * 2,
        scratch_shapes=[pltpu.VMEM((radii, width), jnp.float32)],
        compiler_params=ROOMY,
        cost_estimate=cost(2 * speed.size * radii, 4 * speed.size),
    )(received, speed, back_speed, inverse)


def carry_kernel(recv_ref, speed_ref, back_ref, out_ref, held, sems):
    n, in_rows, _ = recv_ref.shape
    levels, radii, width = speed_ref.shape
    pieces = n // levels
    rows = radii // pieces
    nf = held.shape[0]

    def level_copy(level):
        return pltpu.make_async_copy(held.at[:, level], out_ref.at[pl.ds(0, nf), level], sems.at[level])

    def one_level(level, _):
        for piece in range(pieces):
            part = pl.ds(piece * rows, rows)

            def store(field, row, cell, values, piece=piece):
                row += piece * rows
                held[field, level, row : row + TILE_ROWS, cell : cell + LANES] = values

            carry_piece(
                range(nf),
                in_rows - TILE_ROWS,
                recv_ref.at[level * pieces + piece],
                speed_ref.at[level, part],
                back_ref.at[level, part],
                store,
            )
        level_copy(level).start()
        return 0

    lax.fori_loop(0, levels, one_level, 0)
    for level in range(levels):
        level_copy(level).wait()


def carry(nf, received, speed, back_speed):
    levels, radii, width = speed.shape
    return pl.pallas_call(
        carry_kernel,
        out_shape=jax.ShapeDtypeStruct((nf,) + speed.shape, jnp.float32),
        in_specs=[IN_VMEM] * 3,
        out_specs=IN_HBM,
        scratch_shapes=[
            pltpu.VMEM((nf - 1,) + speed.shape, jnp.float32),
            pltpu.SemaphoreType.DMA((levels,)),
        ],
        compiler_params=ROOMY,
        cost_estimate=cost(10 * nf * speed.size, 2 * nf * speed.size),
    )(received, speed, back_speed)


def solve_interfaces(first_row, last_row, corner):
    bands = len(first_row)
    crossings = bands - 1
    nothing = jnp.zeros_like(first_row[0])
    carry_base = nothing
    carry_slope = jnp.zeros_like(corner[0][0])
    records = []
    for crossing in range(crossings):
        link = corner[crossing][4]
        steepness = link * corner[crossing][3]
        offset = last_row[crossing]
        if crossing > 0:
            back_link = corner[crossing - 1][4] * corner[crossing][2]
            steepness = back_link * carry_slope + steepness
            offset = offset + back_link * carry_base
        fore_link = link * corner[crossing + 1][0]
        next_link = jnp.zeros_like(link)
        if crossing + 1 < crossings:
            next_link = corner[crossing + 1][4] * corner[crossing + 1][1]
        denominator = 1.0 - fore_link * steepness
        upper_base = (first_row[crossing + 1] + fore_link * offset) / denominator
        upper_slope = next_link / denominator
        carry_base = offset + steepness * upper_base
        carry_slope = steepness * upper_slope
        records.append((carry_base, carry_slope, upper_base, upper_slope))
    lower_values = [nothing] * crossings
    upper_values = [nothing] * crossings
    follow = nothing
    for crossing in reversed(range(crossings)):
        carry_base, carry_slope, upper_base, upper_slope = records[crossing]
        lower_values[crossing] = carry_base + carry_slope * follow
        upper_values[crossing] = upper_base + upper_slope * follow
        follow = upper_values[crossing]
    return [nothing] + lower_values, upper_values + [nothing]


def diffuse_kernel(band_ref, corner_ref, local_ref, inverse_ref, *refs):
    end_refs, (_, out_ref, held, sems) = refs[:-4], refs[-4:]
    levels, radii, _ = local_ref.shape
    bands = corner_ref.shape[1] // 5
    band = band_ref[0]
    if len(end_refs) == 2:
        own, other = end_refs
        ends = [
            [jnp.where(band == j, own[side], other[side]) for j in range(bands)] for side in range(2)
        ]
    else:
        ends = [[end_refs[0][j, side] for j in range(bands)] for side in range(2)]
    corner = [[corner_ref[:, j * 5 + c : j * 5 + c + 1] for c in range(5)] for j in range(bands)]
    all_before, all_beyond = solve_interfaces(ends[0], ends[1], corner)
    before = beyond = jnp.zeros_like(ends[0][0])
    below = above = jnp.zeros_like(corner[0][4])
    for j in range(bands):
        mine = band == j
        before = jnp.where(mine, all_before[j], before)
        beyond = jnp.where(mine, all_beyond[j], beyond)
        above = jnp.where(mine, corner[j][4], above)
        if j > 0:
            below = jnp.where(mine, corner[j - 1][4], below)
    copies = []
    for level in range(levels):
        row = slice(level, level + 1)
        held[level] = (
            local_ref[level]
            + (below[row] * inverse_ref[level, :, :1]) * before[row]
            + (above[row] * inverse_ref[level, :, radii - 1 :]) * beyond[row]
        )
        copies.append(
            pltpu.make_async_copy(held.at[level], out_ref.at[out_ref.shape[0] - 1, level], sems.at[level])
        )
        copies[-1].start()
    for copy in copies:
        copy.wait()


def diffuse(band, corners, local_part, inverse, ends, result):
    levels = local_part.shape[0]
    return pl.pallas_call(
        diffuse_kernel,
        out_shape=jax.ShapeDtypeStruct(result.shape, jnp.float32),
        in_specs=[IN_SMEM] + [IN_VMEM] * (3 + len(ends)) + [IN_HBM],
        out_specs=IN_HBM,
        scratch_shapes=[pltpu.VMEM(local_part.shape, jnp.float32), pltpu.SemaphoreType.DMA((levels,))],
        input_output_aliases={4 + len(ends): 0},
        compiler_params=ROOMY,
        cost_estimate=cost(4 * local_part.size, 2 * local_part.size),
    )(band, corners, local_part, inverse, *ends, result)


def exchange(blocks):
    return lax.all_to_all(blocks, "az", split_axis=0, concat_axis=0, tiled=True)


def per_device(fields, velocity, shifts, block_inverse, coupling):
    n = lax.axis_size("az")
    bands = lax.axis_size("rad")
    nf, levels, radii, width = fields.shape
    rows = levels * radii // n
    me = lax.axis_index("az")
    band = lax.axis_index("rad")

    gathered = exchange(pack(fields.reshape(nf, n, rows, width)))

    own_shifts = lax.dynamic_slice_in_dim(shifts, (me * rows) % radii, rows)
    shift_rows = jnp.broadcast_to(own_shifts[:, None], (rows, LANES))
    edge_speed = lax.ppermute(velocity[:, :, -1], "az", [(i, (i + 1) % n) for i in range(n)])
    back_speed = jnp.concatenate([edge_speed[:, :, None], velocity[:, :, :-1]], axis=2)
    corners = jnp.stack(
        [
            block_inverse[:, 0, 0],
            block_inverse[:, 0, -1],
            block_inverse[:, -1, 0],
            block_inverse[:, -1, -1],
            coupling[:, 0],
        ],
        axis=1,
    )
    all_corners = lax.all_gather(corners, "rad", axis=1, tiled=True)
    gathered, back_speed, all_corners = lax.optimization_barrier((gathered, back_speed, all_corners))

    received = exchange(turn(shift_rows, gathered))

    local_part, ends = energy_part(received, velocity, back_speed, block_inverse)
    if bands == 2:
        all_ends = [ends, lax.ppermute(ends, "rad", [(0, 1), (1, 0)])]
    else:
        all_ends = [lax.all_gather(ends, "rad", axis=0)]
    result = carry(nf, received, velocity, back_speed)
    band_scalar = band[None].astype(jnp.int32)
    return diffuse(band_scalar, all_corners, local_part, block_inverse, all_ends, result)


def solution(mesh):
    placed = (
        P(None, None, "rad", "az"),
        P(None, "rad", "az"),
        P("rad"),
        P(None, "rad", None),
        P(None, "rad"),
    )
    return jax.shard_map(
        per_device,
        mesh=mesh,
        in_specs=placed,
        out_specs=P(None, None, "rad", "az"),
        check_vma=False,
    )
```

```python
import functools

import jax
import jax.numpy as jnp
from jax import lax
from jax.experimental import pallas as pl
from jax.experimental.pallas import tpu as pltpu
from jax.sharding import PartitionSpec as P

LANES = 128
TILE_ROWS = 8
IN_VMEM = pl.BlockSpec(memory_space=pltpu.VMEM)
IN_HBM = pl.BlockSpec(memory_space=pltpu.HBM)
IN_ANY = pl.BlockSpec(memory_space=pl.ANY)
IN_SMEM = pl.BlockSpec(memory_space=pltpu.SMEM)
ROOMY = pltpu.CompilerParams(vmem_limit_bytes=20 * 1024 * 1024)


def cost(flops, moved):
    return pl.CostEstimate(flops=flops, bytes_accessed=4 * moved, transcendentals=0)


def partner(me, step):
    return lax.bitwise_xor(me, jnp.int32(step))


def split_kernel(me_ref, in_ref, *rest):
    outs, sems = rest[:-1], rest[-1]
    copies = [
        pltpu.make_async_copy(in_ref.at[:, partner(me_ref[0], step)], out, sems.at[step])
        for step, out in enumerate(outs)
    ]
    for copy in copies:
        copy.start()
    for copy in copies:
        copy.wait()


def split(me, blocked):
    nf, n, rows, width = blocked.shape
    return pl.pallas_call(
        split_kernel,
        out_shape=[jax.ShapeDtypeStruct((nf, rows, width), jnp.float32)] * n,
        in_specs=[IN_SMEM, IN_HBM],
        out_specs=[IN_HBM] * n,
        scratch_shapes=[pltpu.SemaphoreType.DMA((n,))],
        compiler_params=pltpu.CompilerParams(vmem_limit_bytes=56 * 1024 * 1024),
        cost_estimate=cost(0, 2 * blocked.size),
    )(me, blocked)


def turn_kernel(me_ref, shift_ref, *refs):
    circles, held, in_sems, out_sems = refs[-4:]
    n, nf, rows, width = circles.shape
    pieces, outs = refs[:n], refs[n : 2 * n]
    me = me_ref[0]
    per_block = width // LANES
    tiles = n * per_block
    groups = rows // TILE_ROWS
    field_rows = per_block * rows
    halo_row = nf * field_rows
    lane = lax.broadcasted_iota(jnp.int32, (TILE_ROWS, LANES), 1)

    cuts = [pl.ds(0, 1), pl.ds(1, nf - 1)]
    arrivals = [
        [
            pltpu.make_async_copy(
                pieces[step].at[cut], circles.at[partner(me, step), cut], in_sems.at[half, step]
            )
            for step in range(n)
        ]
        for half, cut in enumerate(cuts)
    ]
    cuts = [pl.ds(0, halo_row - field_rows), pl.ds(halo_row - field_rows, field_rows + TILE_ROWS)]
    leavings = [
        [
            pltpu.make_async_copy(
                held.at[partner(me, step), cut, :], outs[step].at[cut, :], out_sems.at[half, step]
            )
            for step in range(n)
        ]
        for half, cut in enumerate(cuts)
    ]
    for half in arrivals:
        for copy in half:
            copy.start()
    for block in range(n):
        held[block, halo_row : halo_row + TILE_ROWS, :] = jnp.zeros((TILE_ROWS, LANES), jnp.float32)

    def one_group(index, _):
        field = index // groups
        group = index % groups
        here = pl.ds(pl.multiple_of(group * TILE_ROWS, TILE_ROWS), TILE_ROWS)
        shift = shift_ref[here, :]
        cells = shift & (LANES - 1)
        whole = shift >> 7
        source = (lane - cells) & (LANES - 1)
        own = lane >= cells
        turned = []
        for tile in range(tiles):
            block, part = divmod(tile, per_block)
            values = circles[block, field, here, part * LANES : (part + 1) * LANES]
            turned.append(jnp.take_along_axis(values, source, axis=1, mode="promise_in_bounds"))
        circle = [jnp.where(own, turned[tile], turned[tile - 1]) for tile in range(tiles)]
        step = 1
        while step < tiles:
            wanted = (whole & step) != 0
            circle = [jnp.where(wanted, circle[(tile - step) % tiles], circle[tile]) for tile in range(tiles)]
            step *= 2
        for tile in range(tiles):
            block, part = divmod(tile, per_block)
            row = field * field_rows + part * rows + group * TILE_ROWS
            held[block, pl.ds(pl.multiple_of(row, TILE_ROWS), TILE_ROWS), :] = circle[tile]
        place = index * 2
        edge = (lane == place) | (lane == place + 1)
        for block in range(n):
            left = circle[(block * per_block - 1) % tiles]
            right = circle[((block + 1) * per_block) % tiles]
            both = pltpu.roll(jnp.where(lane == 0, right, left), place + 1, 1)
            target = held.at[block, halo_row : halo_row + TILE_ROWS, :]
            target[...] = jnp.where(edge, both, target[...])
        return 0

    for copy in arrivals[0]:
        copy.wait()
    lax.fori_loop(0, groups, one_group, 0)
    for copy in arrivals[1]:
        copy.wait()
    lax.fori_loop(groups, (nf - 1) * groups, one_group, 0)
    for copy in leavings[0]:
        copy.start()
    lax.fori_loop((nf - 1) * groups, nf * groups, one_group, 0)
    for copy in leavings[1]:
        copy.start()
    for half in leavings:
        for copy in half:
            copy.wait()


def turn(me, shift_rows, pieces):
    n = len(pieces)
    nf, rows, width = pieces[0].shape
    shape = (nf * (width // LANES) * rows + TILE_ROWS, LANES)
    size = n * nf * rows * width
    return pl.pallas_call(
        turn_kernel,
        out_shape=[jax.ShapeDtypeStruct(shape, jnp.float32)] * n,
        in_specs=[IN_SMEM, IN_VMEM] + [IN_ANY] * n,
        out_specs=[IN_ANY] * n,
        scratch_shapes=[
            pltpu.VMEM((n, nf, rows, width), jnp.float32),
            pltpu.VMEM((n,) + shape, jnp.float32),
            pltpu.SemaphoreType.DMA((2, n)),
            pltpu.SemaphoreType.DMA((2, n)),
        ],
        compiler_params=ROOMY,
        cost_estimate=cost(10 * size, 2 * size),
    )(me, shift_rows, *pieces)


def carry_piece(fields, halo_row, recv, speed, back, store):
    rows, width = speed.shape
    per_block = width // LANES
    groups = rows // TILE_ROWS
    lane = lax.broadcasted_iota(jnp.int32, (TILE_ROWS, LANES), 1)
    first = lane == 0
    last = lane == LANES - 1
    halo = recv[halo_row : halo_row + TILE_ROWS, :]
    for group in range(groups):
        at = slice(group * TILE_ROWS, (group + 1) * TILE_ROWS)
        rates = []
        for part in range(per_block):
            cut = (at, slice(part * LANES, (part + 1) * LANES))
            ahead_speed = speed[cut]
            back_speed = back[cut]
            rates.append(
                (
                    jnp.maximum(ahead_speed, 0.0),
                    jnp.minimum(ahead_speed, 0.0),
                    jnp.maximum(back_speed, 0.0),
                    jnp.minimum(back_speed, 0.0),
                )
            )
        for field in fields:
            values = []
            for part in range(per_block):
                row = (field * per_block + part) * rows + group * TILE_ROWS
                values.append(recv[row : row + TILE_ROWS, :])
            place = (field * groups + group) * 2
            up = [pltpu.roll(halo, (LANES - place) % LANES, 1)]
            up += [pltpu.roll(one, 1, 1) for one in values]
            down = [pltpu.roll(one, LANES - 1, 1) for one in values]
            down.append(pltpu.roll(halo, (LANES - 2 - place) % LANES, 1))
            for part in range(per_block):
                here = values[part]
                behind = jnp.where(first, up[part], up[part + 1])
                ahead = jnp.where(last, down[part + 1], down[part])
                plus, minus, back_plus, back_minus = rates[part]
                outflow = plus * here + minus * ahead
                inflow = back_plus * behind + back_minus * here
                store(field, group * TILE_ROWS, part * LANES, here - (outflow - inflow))


def energy_kernel(me_ref, speed_ref, back_ref, inverse_ref, *refs):
    local_ref, ends_ref, recv_ref, moved, sems = refs[-5:]
    n, in_rows, _ = recv_ref.shape
    pieces = refs[:n]
    levels, radii, width = speed_ref.shape
    per_level = n // levels
    rows = radii // per_level
    halo_row = in_rows - TILE_ROWS
    field_rows = rows * width // LANES
    field = halo_row // field_rows - 1

    cuts = [pl.ds(halo_row - field_rows, field_rows + TILE_ROWS), pl.ds(0, halo_row - field_rows)]
    copies = [
        [
            pltpu.make_async_copy(
                pieces[step].at[cut, :], recv_ref.at[partner(me_ref[0], step), cut, :], sems.at[half, step]
            )
            for step in range(n)
        ]
        for half, cut in enumerate(cuts)
    ]
    for half in copies:
        for copy in half:
            copy.start()
    for copy in copies[0]:
        copy.wait()

    def one_level(level, _):
        for piece in range(per_level):
            part = pl.ds(piece * rows, rows)

            def store(_, row, cell, values, piece=piece):
                row += piece * rows
                moved[row : row + TILE_ROWS, cell : cell + LANES] = values

            carry_piece(
                [field],
                halo_row,
                recv_ref.at[level * per_level + piece],
                speed_ref.at[level, part],
                back_ref.at[level, part],
                store,
            )
        local = jnp.dot(
            inverse_ref[level],
            moved[...],
            precision=lax.Precision.HIGHEST,
            preferred_element_type=jnp.float32,
        )
        local_ref[level] = local
        ends_ref[0, pl.ds(level, 1), :] = local[:1]
        ends_ref[1, pl.ds(level, 1), :] = local[-1:]
        return 0

    lax.fori_loop(0, levels, one_level, 0)
    for copy in copies[1]:
        copy.wait()


def energy_part(me, pieces, speed, back_speed, inverse):
    n = len(pieces)
    levels, radii, width = speed.shape
    return pl.pallas_call(
        energy_kernel,
        out_shape=[
            jax.ShapeDtypeStruct(speed.shape, jnp.float32),
            jax.ShapeDtypeStruct((2, levels, width), jnp.float32),
            jax.ShapeDtypeStruct((n,) + pieces[0].shape, jnp.float32),
        ],
        in_specs=[IN_SMEM] + [IN_VMEM] * 3 + [IN_ANY] * n,
        out_specs=[IN_VMEM] * 3,
        scratch_shapes=[pltpu.VMEM((radii, width), jnp.float32), pltpu.SemaphoreType.DMA((2, n))],
        compiler_params=ROOMY,
        cost_estimate=cost(2 * speed.size * radii, 4 * speed.size),
    )(me, speed, back_speed, inverse, *pieces)


def carry_kernel(recv_ref, speed_ref, back_ref, out_ref, held, sems):
    n, in_rows, _ = recv_ref.shape
    levels, radii, width = speed_ref.shape
    pieces = n // levels
    rows = radii // pieces
    nf = held.shape[0]

    def level_copy(level):
        return pltpu.make_async_copy(held.at[:, level], out_ref.at[pl.ds(0, nf), level], sems.at[level])

    def one_level(level, _):
        for piece in range(pieces):
            part = pl.ds(piece * rows, rows)

            def store(field, row, cell, values, piece=piece):
                row += piece * rows
                held[field, level, row : row + TILE_ROWS, cell : cell + LANES] = values

            carry_piece(
                range(nf),
                in_rows - TILE_ROWS,
                recv_ref.at[level * pieces + piece],
                speed_ref.at[level, part],
                back_ref.at[level, part],
                store,
            )
        level_copy(level).start()
        return 0

    lax.fori_loop(0, levels, one_level, 0)
    for level in range(levels):
        level_copy(level).wait()


def carry(nf, received, speed, back_speed):
    levels, radii, width = speed.shape
    return pl.pallas_call(
        carry_kernel,
        out_shape=jax.ShapeDtypeStruct((nf,) + speed.shape, jnp.float32),
        in_specs=[IN_VMEM] * 3,
        out_specs=IN_HBM,
        scratch_shapes=[
            pltpu.VMEM((nf - 1,) + speed.shape, jnp.float32),
            pltpu.SemaphoreType.DMA((levels,)),
        ],
        compiler_params=ROOMY,
        cost_estimate=cost(10 * nf * speed.size, 2 * nf * speed.size),
    )(received, speed, back_speed)


def solve_interfaces(first_row, last_row, corner):
    bands = len(first_row)
    crossings = bands - 1
    nothing = jnp.zeros_like(first_row[0])
    carry_base = nothing
    carry_slope = jnp.zeros_like(corner[0][0])
    records = []
    for crossing in range(crossings):
        link = corner[crossing][4]
        steepness = link * corner[crossing][3]
        offset = last_row[crossing]
        if crossing > 0:
            back_link = corner[crossing - 1][4] * corner[crossing][2]
            steepness = back_link * carry_slope + steepness
            offset = offset + back_link * carry_base
        fore_link = link * corner[crossing + 1][0]
        next_link = jnp.zeros_like(link)
        if crossing + 1 < crossings:
            next_link = corner[crossing + 1][4] * corner[crossing + 1][1]
        denominator = 1.0 - fore_link * steepness
        upper_base = (first_row[crossing + 1] + fore_link * offset) / denominator
        upper_slope = next_link / denominator
        carry_base = offset + steepness * upper_base
        carry_slope = steepness * upper_slope
        records.append((carry_base, carry_slope, upper_base, upper_slope))
    lower_values = [nothing] * crossings
    upper_values = [nothing] * crossings
    follow = nothing
    for crossing in reversed(range(crossings)):
        carry_base, carry_slope, upper_base, upper_slope = records[crossing]
        lower_values[crossing] = carry_base + carry_slope * follow
        upper_values[crossing] = upper_base + upper_slope * follow
        follow = upper_values[crossing]
    return [nothing] + lower_values, upper_values + [nothing]


def diffuse_kernel(band_ref, corner_ref, local_ref, inverse_ref, *refs):
    end_refs, (_, out_ref, held, sems) = refs[:-4], refs[-4:]
    levels, radii, _ = local_ref.shape
    bands = corner_ref.shape[1] // 5
    band = band_ref[0]
    if len(end_refs) == 2:
        own, other = end_refs
        ends = [
            [jnp.where(band == j, own[side], other[side]) for j in range(bands)] for side in range(2)
        ]
    else:
        ends = [[end_refs[0][j, side] for j in range(bands)] for side in range(2)]
    corner = [[corner_ref[:, j * 5 + c : j * 5 + c + 1] for c in range(5)] for j in range(bands)]
    all_before, all_beyond = solve_interfaces(ends[0], ends[1], corner)
    before = beyond = jnp.zeros_like(ends[0][0])
    below = above = jnp.zeros_like(corner[0][4])
    for j in range(bands):
        mine = band == j
        before = jnp.where(mine, all_before[j], before)
        beyond = jnp.where(mine, all_beyond[j], beyond)
        above = jnp.where(mine, corner[j][4], above)
        if j > 0:
            below = jnp.where(mine, corner[j - 1][4], below)
    copies = []
    for level in range(levels):
        row = slice(level, level + 1)
        held[level] = (
            local_ref[level]
            + (below[row] * inverse_ref[level, :, :1]) * before[row]
            + (above[row] * inverse_ref[level, :, radii - 1 :]) * beyond[row]
        )
        copies.append(
            pltpu.make_async_copy(held.at[level], out_ref.at[out_ref.shape[0] - 1, level], sems.at[level])
        )
        copies[-1].start()
    for copy in copies:
        copy.wait()


def diffuse(band, corners, local_part, inverse, ends, result):
    levels = local_part.shape[0]
    return pl.pallas_call(
        diffuse_kernel,
        out_shape=jax.ShapeDtypeStruct(result.shape, jnp.float32),
        in_specs=[IN_SMEM] + [IN_VMEM] * (3 + len(ends)) + [IN_HBM],
        out_specs=IN_HBM,
        scratch_shapes=[pltpu.VMEM(local_part.shape, jnp.float32), pltpu.SemaphoreType.DMA((levels,))],
        input_output_aliases={4 + len(ends): 0},
        compiler_params=ROOMY,
        cost_estimate=cost(4 * local_part.size, 2 * local_part.size),
    )(band, corners, local_part, inverse, *ends, result)


def exchange(pieces):
    n = len(pieces)
    order = [step for pair in zip(range(n // 2, n), range(n // 2)) for step in pair if step > 0]
    swapped = {0: pieces[0]}
    for step in order:
        swapped[step] = lax.ppermute(pieces[step], "az", [(i, i ^ step) for i in range(n)])
    return [swapped[step] for step in range(n)]


def per_device(fields, velocity, shifts, block_inverse, coupling):
    n = lax.axis_size("az")
    bands = lax.axis_size("rad")
    nf, levels, radii, width = fields.shape
    rows = levels * radii // n
    me = lax.axis_index("az")
    band = lax.axis_index("rad")

    me_scalar = me[None].astype(jnp.int32)

    gathered = exchange(split(me_scalar, fields.reshape(nf, n, rows, width)))

    own_shifts = lax.dynamic_slice_in_dim(shifts, (me * rows) % radii, rows)
    shift_rows = jnp.broadcast_to(own_shifts[:, None], (rows, LANES))
    edge_speed = lax.ppermute(velocity[:, :, -1], "az", [(i, (i + 1) % n) for i in range(n)])
    back_speed = jnp.concatenate([edge_speed[:, :, None], velocity[:, :, :-1]], axis=2)
    corners = jnp.stack(
        [
            block_inverse[:, 0, 0],
            block_inverse[:, 0, -1],
            block_inverse[:, -1, 0],
            block_inverse[:, -1, -1],
            coupling[:, 0],
        ],
        axis=1,
    )
    all_corners = lax.all_gather(corners, "rad", axis=1, tiled=True)
    gathered, back_speed, all_corners = lax.optimization_barrier((gathered, back_speed, all_corners))

    pieces = exchange(turn(me_scalar, shift_rows, gathered))

    local_part, ends, received = energy_part(me_scalar, pieces, velocity, back_speed, block_inverse)
    if bands == 2:
        all_ends = [ends, lax.ppermute(ends, "rad", [(0, 1), (1, 0)])]
    else:
        all_ends = [lax.all_gather(ends, "rad", axis=0)]
    result = carry(nf, received, velocity, back_speed)
    band_scalar = band[None].astype(jnp.int32)
    return diffuse(band_scalar, all_corners, local_part, block_inverse, all_ends, result)


def solution(mesh):
    placed = (
        P(None, None, "rad", "az"),
        P(None, "rad", "az"),
        P("rad"),
        P(None, "rad", None),
        P(None, "rad"),
    )
    return jax.shard_map(
        per_device,
        mesh=mesh,
        in_specs=placed,
        out_specs=P(None, None, "rad", "az"),
        check_vma=False,
    )
```

```python
import functools

import jax
import jax.numpy as jnp
from jax import lax
from jax.experimental import pallas as pl
from jax.experimental.pallas import tpu as pltpu
from jax.sharding import PartitionSpec as P

LANES = 128
TILE_ROWS = 8
IN_VMEM = pl.BlockSpec(memory_space=pltpu.VMEM)
IN_HBM = pl.BlockSpec(memory_space=pltpu.HBM)
IN_SMEM = pl.BlockSpec(memory_space=pltpu.SMEM)
ROOMY = pltpu.CompilerParams(vmem_limit_bytes=24 * 1024 * 1024)


def cost(flops, moved):
    return pl.CostEstimate(flops=flops, bytes_accessed=4 * moved, transcendentals=0)


def pack_kernel(in_ref, out_ref, held, in_sems, out_sems):
    nf, n = in_ref.shape[:2]
    half = n // 2
    arrivals, leavings = [], []
    for piece in range(2 * nf):
        field, part = piece // 2, pl.ds((piece % 2) * half, half)
        arrivals.append(
            pltpu.make_async_copy(in_ref.at[field, part], held.at[field, part], in_sems.at[piece])
        )
        leavings.append(
            pltpu.make_async_copy(held.at[field, part], out_ref.at[part, field], out_sems.at[piece])
        )
    for copy in arrivals:
        copy.start()
    for arrival, leaving in zip(arrivals, leavings):
        arrival.wait()
        leaving.start()
    for copy in leavings:
        copy.wait()


def pack(blocked):
    nf, n, rows, width = blocked.shape
    return pl.pallas_call(
        pack_kernel,
        out_shape=jax.ShapeDtypeStruct((n, nf, rows, width), jnp.float32),
        in_specs=[IN_HBM],
        out_specs=IN_HBM,
        scratch_shapes=[
            pltpu.VMEM(blocked.shape, jnp.float32),
            pltpu.SemaphoreType.DMA((2 * nf,)),
            pltpu.SemaphoreType.DMA((2 * nf,)),
        ],
        compiler_params=pltpu.CompilerParams(vmem_limit_bytes=58 * 1024 * 1024),
        cost_estimate=cost(0, 2 * blocked.size),
    )(blocked)


def turn_kernel(shift_ref, in_ref, out_ref):
    n, nf, rows, width = in_ref.shape
    per_block = width // LANES
    tiles = n * per_block
    groups = rows // TILE_ROWS
    field_rows = per_block * rows
    halo_row = nf * field_rows
    lane = lax.broadcasted_iota(jnp.int32, (TILE_ROWS, LANES), 1)

    for block in range(n):
        out_ref[block, halo_row : halo_row + TILE_ROWS, :] = jnp.zeros((TILE_ROWS, LANES), jnp.float32)

    def one_group(index, _):
        field = index // groups
        group = index % groups
        here = pl.ds(pl.multiple_of(group * TILE_ROWS, TILE_ROWS), TILE_ROWS)
        shift = shift_ref[here, :]
        cells = shift & (LANES - 1)
        whole = shift >> 7
        source = (lane - cells) & (LANES - 1)
        own = lane >= cells
        turned = []
        for tile in range(tiles):
            block, part = divmod(tile, per_block)
            values = in_ref[block, field, here, part * LANES : (part + 1) * LANES]
            turned.append(jnp.take_along_axis(values, source, axis=1, mode="promise_in_bounds"))
        circle = [jnp.where(own, turned[tile], turned[tile - 1]) for tile in range(tiles)]
        step = 1
        while step < tiles:
            wanted = (whole & step) != 0
            circle = [jnp.where(wanted, circle[(tile - step) % tiles], circle[tile]) for tile in range(tiles)]
            step *= 2
        for tile in range(tiles):
            block, part = divmod(tile, per_block)
            row = field * field_rows + part * rows + group * TILE_ROWS
            out_ref[block, pl.ds(pl.multiple_of(row, TILE_ROWS), TILE_ROWS), :] = circle[tile]
        place = index * 2
        edge = (lane == place) | (lane == place + 1)
        for block in range(n):
            left = circle[(block * per_block - 1) % tiles]
            right = circle[((block + 1) * per_block) % tiles]
            both = pltpu.roll(jnp.where(lane == 0, right, left), place + 1, 1)
            target = out_ref.at[block, halo_row : halo_row + TILE_ROWS, :]
            target[...] = jnp.where(edge, both, target[...])

        return 0

    lax.fori_loop(0, nf * groups, one_group, 0)


def turn(shift_rows, gathered):
    n, nf, rows, width = gathered.shape
    shape = (n, nf * (width // LANES) * rows + TILE_ROWS, LANES)
    return pl.pallas_call(
        turn_kernel,
        out_shape=jax.ShapeDtypeStruct(shape, jnp.float32),
        in_specs=[IN_VMEM] * 2,
        out_specs=IN_VMEM,
        compiler_params=ROOMY,
        cost_estimate=cost(10 * gathered.size, 2 * gathered.size),
    )(shift_rows, gathered)


def carry_piece(fields, halo_row, recv, speed, back, store):
    rows, width = speed.shape
    per_block = width // LANES
    groups = rows // TILE_ROWS
    lane = lax.broadcasted_iota(jnp.int32, (TILE_ROWS, LANES), 1)
    first = lane == 0
    last = lane == LANES - 1
    halo = recv[halo_row : halo_row + TILE_ROWS, :]
    for group in range(groups):
        at = slice(group * TILE_ROWS, (group + 1) * TILE_ROWS)
        rates = []
        for part in range(per_block):
            cut = (at, slice(part * LANES, (part + 1) * LANES))
            ahead_speed = speed[cut]
            back_speed = back[cut]
            rates.append(
                (
                    jnp.maximum(ahead_speed, 0.0),
                    jnp.minimum(ahead_speed, 0.0),
                    jnp.maximum(back_speed, 0.0),
                    jnp.minimum(back_speed, 0.0),
                )
            )
        for field in fields:
            values = []
            for part in range(per_block):
                row = (field * per_block + part) * rows + group * TILE_ROWS
                values.append(recv[row : row + TILE_ROWS, :])
            place = (field * groups + group) * 2
            up = [pltpu.roll(halo, (LANES - place) % LANES, 1)]
            up += [pltpu.roll(one, 1, 1) for one in values]
            down = [pltpu.roll(one, LANES - 1, 1) for one in values]
            down.append(pltpu.roll(halo, (LANES - 2 - place) % LANES, 1))
            for part in range(per_block):
                here = values[part]
                behind = jnp.where(first, up[part], up[part + 1])
                ahead = jnp.where(last, down[part + 1], down[part])
                plus, minus, back_plus, back_minus = rates[part]
                outflow = plus * here + minus * ahead
                inflow = back_plus * behind + back_minus * here
                store(field, group * TILE_ROWS, part * LANES, here - (outflow - inflow))


def energy_kernel(recv_ref, speed_ref, back_ref, inverse_ref, local_ref, ends_ref, moved):
    n, in_rows, _ = recv_ref.shape
    levels, radii, width = speed_ref.shape
    pieces = n // levels
    rows = radii // pieces
    field = (in_rows - TILE_ROWS) * LANES // (rows * width) - 1

    def one_level(level):
        for piece in range(pieces):
            part = pl.ds(piece * rows, rows)

            def store(_, row, cell, values, piece=piece):
                row += piece * rows
                moved[level, row : row + TILE_ROWS, cell : cell + LANES] = values

            carry_piece(
                [field],
                in_rows - TILE_ROWS,
                recv_ref.at[level * pieces + piece],
                speed_ref.at[level, part],
                back_ref.at[level, part],
                store,
            )
        local = jnp.dot(
            inverse_ref[level],
            moved[level],
            precision=lax.Precision.HIGHEST,
            preferred_element_type=jnp.float32,
        )
        local_ref[level] = local
        ends_ref[0, level : level + 1, :] = local[:1]
        ends_ref[1, level : level + 1, :] = local[-1:]

    for level in range(levels):
        one_level(level)


def energy_part(received, speed, back_speed, inverse):
    levels, radii, width = speed.shape
    return pl.pallas_call(
        energy_kernel,
        out_shape=[
            jax.ShapeDtypeStruct(speed.shape, jnp.float32),
            jax.ShapeDtypeStruct((2, levels, width), jnp.float32),
        ],
        in_specs=[IN_VMEM] * 4,
        out_specs=[IN_VMEM] * 2,
        scratch_shapes=[pltpu.VMEM(speed.shape, jnp.float32)],
        compiler_params=ROOMY,
        cost_estimate=cost(2 * speed.size * radii, 4 * speed.size),
    )(received, speed, back_speed, inverse)


def carry_kernel(recv_ref, speed_ref, back_ref, out_ref, held, sems):
    n, in_rows, _ = recv_ref.shape
    levels, radii, width = speed_ref.shape
    pieces = n // levels
    rows = radii // pieces
    nf = held.shape[0]

    def level_copy(level):
        return pltpu.make_async_copy(held.at[:, level], out_ref.at[pl.ds(0, nf), level], sems.at[level])

    def one_level(level, _):
        for piece in range(pieces):
            part = pl.ds(piece * rows, rows)

            def store(field, row, cell, values, piece=piece):
                row += piece * rows
                held[field, level, row : row + TILE_ROWS, cell : cell + LANES] = values

            carry_piece(
                range(nf),
                in_rows - TILE_ROWS,
                recv_ref.at[level * pieces + piece],
                speed_ref.at[level, part],
                back_ref.at[level, part],
                store,
            )
        level_copy(level).start()
        return 0

    lax.fori_loop(0, levels, one_level, 0)
    for level in range(levels):
        level_copy(level).wait()


def carry(nf, received, speed, back_speed):
    levels, radii, width = speed.shape
    return pl.pallas_call(
        carry_kernel,
        out_shape=jax.ShapeDtypeStruct((nf,) + speed.shape, jnp.float32),
        in_specs=[IN_VMEM] * 3,
        out_specs=IN_HBM,
        scratch_shapes=[
            pltpu.VMEM((nf - 1,) + speed.shape, jnp.float32),
            pltpu.SemaphoreType.DMA((levels,)),
        ],
        compiler_params=ROOMY,
        cost_estimate=cost(10 * nf * speed.size, 2 * nf * speed.size),
    )(received, speed, back_speed)


def solve_interfaces(first_row, last_row, corner):
    bands = len(first_row)
    crossings = bands - 1
    nothing = jnp.zeros_like(first_row[0])
    carry_base = nothing
    carry_slope = jnp.zeros_like(corner[0][0])
    records = []
    for crossing in range(crossings):
        link = corner[crossing][4]
        steepness = link * corner[crossing][3]
        offset = last_row[crossing]
        if crossing > 0:
            back_link = corner[crossing - 1][4] * corner[crossing][2]
            steepness = back_link * carry_slope + steepness
            offset = offset + back_link * carry_base
        fore_link = link * corner[crossing + 1][0]
        next_link = jnp.zeros_like(link)
        if crossing + 1 < crossings:
            next_link = corner[crossing + 1][4] * corner[crossing + 1][1]
        denominator = 1.0 - fore_link * steepness
        upper_base = (first_row[crossing + 1] + fore_link * offset) / denominator
        upper_slope = next_link / denominator
        carry_base = offset + steepness * upper_base
        carry_slope = steepness * upper_slope
        records.append((carry_base, carry_slope, upper_base, upper_slope))
    lower_values = [nothing] * crossings
    upper_values = [nothing] * crossings
    follow = nothing
    for crossing in reversed(range(crossings)):
        carry_base, carry_slope, upper_base, upper_slope = records[crossing]
        lower_values[crossing] = carry_base + carry_slope * follow
        upper_values[crossing] = upper_base + upper_slope * follow
        follow = upper_values[crossing]
    return [nothing] + lower_values, upper_values + [nothing]


def diffuse_kernel(band_ref, corner_ref, local_ref, inverse_ref, *refs):
    end_refs, (_, out_ref, held, sems) = refs[:-4], refs[-4:]
    levels, radii, _ = local_ref.shape
    bands = corner_ref.shape[1] // 5
    band = band_ref[0]
    if len(end_refs) == 2:
        own, other = end_refs
        ends = [
            [jnp.where(band == j, own[side], other[side]) for j in range(bands)] for side in range(2)
        ]
    else:
        ends = [[end_refs[0][j, side] for j in range(bands)] for side in range(2)]
    corner = [[corner_ref[:, j * 5 + c : j * 5 + c + 1] for c in range(5)] for j in range(bands)]
    all_before, all_beyond = solve_interfaces(ends[0], ends[1], corner)
    before = beyond = jnp.zeros_like(ends[0][0])
    below = above = jnp.zeros_like(corner[0][4])
    for j in range(bands):
        mine = band == j
        before = jnp.where(mine, all_before[j], before)
        beyond = jnp.where(mine, all_beyond[j], beyond)
        above = jnp.where(mine, corner[j][4], above)
        if j > 0:
            below = jnp.where(mine, corner[j - 1][4], below)
    copies = []
    for level in range(levels):
        row = slice(level, level + 1)
        held[level] = (
            local_ref[level]
            + (below[row] * inverse_ref[level, :, :1]) * before[row]
            + (above[row] * inverse_ref[level, :, radii - 1 :]) * beyond[row]
        )
        copies.append(
            pltpu.make_async_copy(held.at[level], out_ref.at[out_ref.shape[0] - 1, level], sems.at[level])
        )
        copies[-1].start()
    for copy in copies:
        copy.wait()


def diffuse(band, corners, local_part, inverse, ends, result):
    levels = local_part.shape[0]
    return pl.pallas_call(
        diffuse_kernel,
        out_shape=jax.ShapeDtypeStruct(result.shape, jnp.float32),
        in_specs=[IN_SMEM] + [IN_VMEM] * (3 + len(ends)) + [IN_HBM],
        out_specs=IN_HBM,
        scratch_shapes=[pltpu.VMEM(local_part.shape, jnp.float32), pltpu.SemaphoreType.DMA((levels,))],
        input_output_aliases={4 + len(ends): 0},
        compiler_params=ROOMY,
        cost_estimate=cost(4 * local_part.size, 2 * local_part.size),
    )(band, corners, local_part, inverse, *ends, result)


def exchange(blocks):
    return lax.all_to_all(blocks, "az", split_axis=0, concat_axis=0, tiled=True)


def per_device(fields, velocity, shifts, block_inverse, coupling):
    n = lax.axis_size("az")
    bands = lax.axis_size("rad")
    nf, levels, radii, width = fields.shape
    rows = levels * radii // n
    me = lax.axis_index("az")
    band = lax.axis_index("rad")

    gathered = exchange(pack(fields.reshape(nf, n, rows, width)))

    own_shifts = lax.dynamic_slice_in_dim(shifts, (me * rows) % radii, rows)
    shift_rows = jnp.broadcast_to(own_shifts[:, None], (rows, LANES))
    edge_speed = lax.ppermute(velocity[:, :, -1], "az", [(i, (i + 1) % n) for i in range(n)])
    back_speed = jnp.concatenate([edge_speed[:, :, None], velocity[:, :, :-1]], axis=2)
    corners = jnp.stack(
        [
            block_inverse[:, 0, 0],
            block_inverse[:, 0, -1],
            block_inverse[:, -1, 0],
            block_inverse[:, -1, -1],
            coupling[:, 0],
        ],
        axis=1,
    )
    all_corners = lax.all_gather(corners, "rad", axis=1, tiled=True)
    band_scalar = band[None].astype(jnp.int32)
    gathered, back_speed, all_corners, band_scalar, shift_rows = lax.optimization_barrier(
        (gathered, back_speed, all_corners, band_scalar, shift_rows)
    )

    received = exchange(turn(shift_rows, gathered))

    local_part, ends = energy_part(received, velocity, back_speed, block_inverse)
    if bands == 2:
        all_ends = [ends, lax.ppermute(ends, "rad", [(0, 1), (1, 0)])]
    else:
        all_ends = [lax.all_gather(ends, "rad", axis=0)]
    result = carry(nf, received, velocity, back_speed)
    return diffuse(band_scalar, all_corners, local_part, block_inverse, all_ends, result)


def solution(mesh):
    placed = (
        P(None, None, "rad", "az"),
        P(None, "rad", "az"),
        P("rad"),
        P(None, "rad", None),
        P(None, "rad"),
    )
    return jax.shard_map(
        per_device,
        mesh=mesh,
        in_specs=placed,
        out_specs=P(None, None, "rad", "az"),
        check_vma=False,
    )
```

```python
import functools

import jax
import jax.numpy as jnp
from jax import lax
from jax.experimental import pallas as pl
from jax.experimental.pallas import tpu as pltpu
from jax.sharding import PartitionSpec as P

LANES = 128
TILE_ROWS = 8
IN_VMEM = pl.BlockSpec(memory_space=pltpu.VMEM)
IN_HBM = pl.BlockSpec(memory_space=pltpu.HBM)
IN_SMEM = pl.BlockSpec(memory_space=pltpu.SMEM)
ROOMY = pltpu.CompilerParams(vmem_limit_bytes=24 * 1024 * 1024)


def cost(flops, moved):
    return pl.CostEstimate(flops=flops, bytes_accessed=4 * moved, transcendentals=0)


def pack_kernel(in_ref, out_ref, held, in_sems, out_sems):
    nf, n = in_ref.shape[:2]
    cuts = in_sems.shape[0] // nf
    size = n // cuts
    arrivals, leavings = [], []
    for piece in range(cuts * nf):
        field, part = piece // cuts, pl.ds((piece % cuts) * size, size)
        arrivals.append(
            pltpu.make_async_copy(in_ref.at[field, part], held.at[field, part], in_sems.at[piece])
        )
        leavings.append(
            pltpu.make_async_copy(held.at[field, part], out_ref.at[part, field], out_sems.at[piece])
        )
    for copy in arrivals:
        copy.start()
    for arrival, leaving in zip(arrivals, leavings):
        arrival.wait()
        leaving.start()
    for copy in leavings:
        copy.wait()


def pack(blocked):
    nf, n, rows, width = blocked.shape
    return pl.pallas_call(
        pack_kernel,
        out_shape=jax.ShapeDtypeStruct((n, nf, rows, width), jnp.float32),
        in_specs=[IN_HBM],
        out_specs=IN_HBM,
        scratch_shapes=[
            pltpu.VMEM(blocked.shape, jnp.float32),
            pltpu.SemaphoreType.DMA((4 * nf,)),
            pltpu.SemaphoreType.DMA((4 * nf,)),
        ],
        compiler_params=pltpu.CompilerParams(vmem_limit_bytes=58 * 1024 * 1024),
        cost_estimate=cost(0, 2 * blocked.size),
    )(blocked)


def turn_kernel(shift_ref, in_ref, out_ref):
    n, nf, rows, width = in_ref.shape
    per_block = width // LANES
    tiles = n * per_block
    groups = rows // TILE_ROWS
    field_rows = per_block * rows
    halo_row = nf * field_rows
    lane = lax.broadcasted_iota(jnp.int32, (TILE_ROWS, LANES), 1)

    for block in range(n):
        out_ref[block, halo_row : halo_row + TILE_ROWS, :] = jnp.zeros((TILE_ROWS, LANES), jnp.float32)

    def one_group(index, _):
        field = index // groups
        group = index % groups
        here = pl.ds(pl.multiple_of(group * TILE_ROWS, TILE_ROWS), TILE_ROWS)
        shift = shift_ref[here, :]
        cells = shift & (LANES - 1)
        whole = shift >> 7
        source = (lane - cells) & (LANES - 1)
        own = lane >= cells
        turned = []
        for tile in range(tiles):
            block, part = divmod(tile, per_block)
            values = in_ref[block, field, here, part * LANES : (part + 1) * LANES]
            turned.append(jnp.take_along_axis(values, source, axis=1, mode="promise_in_bounds"))
        circle = [jnp.where(own, turned[tile], turned[tile - 1]) for tile in range(tiles)]
        step = 1
        while step < tiles:
            wanted = (whole & step) != 0
            circle = [jnp.where(wanted, circle[(tile - step) % tiles], circle[tile]) for tile in range(tiles)]
            step *= 2
        for tile in range(tiles):
            block, part = divmod(tile, per_block)
            row = field * field_rows + part * rows + group * TILE_ROWS
            out_ref[block, pl.ds(pl.multiple_of(row, TILE_ROWS), TILE_ROWS), :] = circle[tile]
        place = index * 2
        edge = (lane == place) | (lane == place + 1)
        for block in range(n):
            left = circle[(block * per_block - 1) % tiles]
            right = circle[((block + 1) * per_block) % tiles]
            both = pltpu.roll(jnp.where(lane == 0, right, left), place + 1, 1)
            target = out_ref.at[block, halo_row : halo_row + TILE_ROWS, :]
            target[...] = jnp.where(edge, both, target[...])

        return 0

    lax.fori_loop(0, nf * groups, one_group, 0, unroll=groups)


def turn(shift_rows, gathered):
    n, nf, rows, width = gathered.shape
    shape = (n, nf * (width // LANES) * rows + TILE_ROWS, LANES)
    return pl.pallas_call(
        turn_kernel,
        out_shape=jax.ShapeDtypeStruct(shape, jnp.float32),
        in_specs=[IN_VMEM] * 2,
        out_specs=IN_VMEM,
        compiler_params=ROOMY,
        cost_estimate=cost(10 * gathered.size, 2 * gathered.size),
    )(shift_rows, gathered)


def carry_piece(fields, halo_row, recv, speed, back, store):
    rows, width = speed.shape
    per_block = width // LANES
    groups = rows // TILE_ROWS
    lane = lax.broadcasted_iota(jnp.int32, (TILE_ROWS, LANES), 1)
    first = lane == 0
    last = lane == LANES - 1
    halo = recv[halo_row : halo_row + TILE_ROWS, :]
    for group in range(groups):
        at = slice(group * TILE_ROWS, (group + 1) * TILE_ROWS)
        rates = []
        for part in range(per_block):
            cut = (at, slice(part * LANES, (part + 1) * LANES))
            ahead_speed = speed[cut]
            back_speed = back[cut]
            rates.append(
                (
                    jnp.maximum(ahead_speed, 0.0),
                    jnp.minimum(ahead_speed, 0.0),
                    jnp.maximum(back_speed, 0.0),
                    jnp.minimum(back_speed, 0.0),
                )
            )
        for field in fields:
            values = []
            for part in range(per_block):
                row = (field * per_block + part) * rows + group * TILE_ROWS
                values.append(recv[row : row + TILE_ROWS, :])
            place = (field * groups + group) * 2
            edges = pltpu.roll(halo, (2 * LANES - 1 - place) % LANES, 1)
            circle = [edges] + values + [edges]
            for part in range(per_block):
                before, here, after = circle[part : part + 3]
                behind = pltpu.roll(jnp.where(last, before, here), 1, 1)
                ahead = pltpu.roll(jnp.where(first, after, here), LANES - 1, 1)
                plus, minus, back_plus, back_minus = rates[part]
                outflow = plus * here + minus * ahead
                inflow = back_plus * behind + back_minus * here
                store(field, group * TILE_ROWS, part * LANES, here - (outflow - inflow))


def energy_kernel(recv_ref, speed_ref, back_ref, inverse_ref, local_ref, ends_ref, moved):
    n, in_rows, _ = recv_ref.shape
    levels, radii, width = speed_ref.shape
    pieces = n // levels
    rows = radii // pieces
    field = (in_rows - TILE_ROWS) * LANES // (rows * width) - 1

    def one_level(level):
        for piece in range(pieces):
            part = pl.ds(piece * rows, rows)

            def store(_, row, cell, values, piece=piece):
                row += piece * rows
                moved[level, row : row + TILE_ROWS, cell : cell + LANES] = values

            carry_piece(
                [field],
                in_rows - TILE_ROWS,
                recv_ref.at[level * pieces + piece],
                speed_ref.at[level, part],
                back_ref.at[level, part],
                store,
            )
        local = jnp.dot(
            inverse_ref[level],
            moved[level],
            precision=lax.Precision.HIGHEST,
            preferred_element_type=jnp.float32,
        )
        local_ref[level] = local
        ends_ref[0, level : level + 1, :] = local[:1]
        ends_ref[1, level : level + 1, :] = local[-1:]

    for level in range(levels):
        one_level(level)


def energy_part(received, speed, back_speed, inverse):
    levels, radii, width = speed.shape
    return pl.pallas_call(
        energy_kernel,
        out_shape=[
            jax.ShapeDtypeStruct(speed.shape, jnp.float32),
            jax.ShapeDtypeStruct((2, levels, width), jnp.float32),
        ],
        in_specs=[IN_VMEM] * 4,
        out_specs=[IN_VMEM] * 2,
        scratch_shapes=[pltpu.VMEM(speed.shape, jnp.float32)],
        compiler_params=ROOMY,
        cost_estimate=cost(2 * speed.size * radii, 4 * speed.size),
    )(received, speed, back_speed, inverse)


def carry_kernel(recv_ref, speed_ref, back_ref, out_ref, held, sems):
    n, in_rows, _ = recv_ref.shape
    levels, radii, width = speed_ref.shape
    pieces = n // levels
    rows = radii // pieces
    nf = held.shape[0]

    def level_copy(level):
        return pltpu.make_async_copy(held.at[:, level], out_ref.at[pl.ds(0, nf), level], sems.at[level])

    def one_level(level, _):
        for piece in range(pieces):
            part = pl.ds(piece * rows, rows)

            def store(field, row, cell, values, piece=piece):
                row += piece * rows
                held[field, level, row : row + TILE_ROWS, cell : cell + LANES] = values

            carry_piece(
                range(nf),
                in_rows - TILE_ROWS,
                recv_ref.at[level * pieces + piece],
                speed_ref.at[level, part],
                back_ref.at[level, part],
                store,
            )
        level_copy(level).start()
        return 0

    lax.fori_loop(0, levels, one_level, 0)
    for level in range(levels):
        level_copy(level).wait()


def carry(nf, received, speed, back_speed):
    levels, radii, width = speed.shape
    return pl.pallas_call(
        carry_kernel,
        out_shape=jax.ShapeDtypeStruct((nf,) + speed.shape, jnp.float32),
        in_specs=[IN_VMEM] * 3,
        out_specs=IN_HBM,
        scratch_shapes=[
            pltpu.VMEM((nf - 1,) + speed.shape, jnp.float32),
            pltpu.SemaphoreType.DMA((levels,)),
        ],
        compiler_params=ROOMY,
        cost_estimate=cost(10 * nf * speed.size, 2 * nf * speed.size),
    )(received, speed, back_speed)


def solve_interfaces(first_row, last_row, corner):
    bands = len(first_row)
    crossings = bands - 1
    nothing = jnp.zeros_like(first_row[0])
    carry_base = nothing
    carry_slope = jnp.zeros_like(corner[0][0])
    records = []
    for crossing in range(crossings):
        link = corner[crossing][4]
        steepness = link * corner[crossing][3]
        offset = last_row[crossing]
        if crossing > 0:
            back_link = corner[crossing - 1][4] * corner[crossing][2]
            steepness = back_link * carry_slope + steepness
            offset = offset + back_link * carry_base
        fore_link = link * corner[crossing + 1][0]
        next_link = jnp.zeros_like(link)
        if crossing + 1 < crossings:
            next_link = corner[crossing + 1][4] * corner[crossing + 1][1]
        denominator = 1.0 - fore_link * steepness
        upper_base = (first_row[crossing + 1] + fore_link * offset) / denominator
        upper_slope = next_link / denominator
        carry_base = offset + steepness * upper_base
        carry_slope = steepness * upper_slope
        records.append((carry_base, carry_slope, upper_base, upper_slope))
    lower_values = [nothing] * crossings
    upper_values = [nothing] * crossings
    follow = nothing
    for crossing in reversed(range(crossings)):
        carry_base, carry_slope, upper_base, upper_slope = records[crossing]
        lower_values[crossing] = carry_base + carry_slope * follow
        upper_values[crossing] = upper_base + upper_slope * follow
        follow = upper_values[crossing]
    return [nothing] + lower_values, upper_values + [nothing]


def diffuse_kernel(band_ref, corner_ref, local_ref, low_ref, high_ref, *refs):
    end_refs, (_, out_ref, held, sems) = refs[:-4], refs[-4:]
    levels, _, width = local_ref.shape
    bands = corner_ref.shape[1] // 5
    band = band_ref[0]
    if len(end_refs) == 2:
        own, other = end_refs
        ends = [
            [jnp.where(band == j, own[side], other[side]) for j in range(bands)] for side in range(2)
        ]
    else:
        ends = [[end_refs[0][j, side] for j in range(bands)] for side in range(2)]
    corner = [[corner_ref[:, j * 5 + c : j * 5 + c + 1] for c in range(5)] for j in range(bands)]
    all_before, all_beyond = solve_interfaces(ends[0], ends[1], corner)
    before = beyond = jnp.zeros_like(ends[0][0])
    for j in range(bands):
        before = jnp.where(band == j, all_before[j], before)
        beyond = jnp.where(band == j, all_beyond[j], beyond)
    copies = []
    for level in range(levels):
        for cell in range(0, width, LANES):
            cut = slice(cell, cell + LANES)
            held[level, :, cut] = (
                local_ref[level, :, cut]
                + low_ref[level] * before[level : level + 1, cut]
                + high_ref[level] * beyond[level : level + 1, cut]
            )
        copies.append(
            pltpu.make_async_copy(held.at[level], out_ref.at[out_ref.shape[0] - 1, level], sems.at[level])
        )
        copies[-1].start()
    for copy in copies:
        copy.wait()


def diffuse(band, corners, local_part, low, high, ends, result):
    levels = local_part.shape[0]
    return pl.pallas_call(
        diffuse_kernel,
        out_shape=jax.ShapeDtypeStruct(result.shape, jnp.float32),
        in_specs=[IN_SMEM] + [IN_VMEM] * (4 + len(ends)) + [IN_HBM],
        out_specs=IN_HBM,
        scratch_shapes=[pltpu.VMEM(local_part.shape, jnp.float32), pltpu.SemaphoreType.DMA((levels,))],
        input_output_aliases={5 + len(ends): 0},
        compiler_params=ROOMY,
        cost_estimate=cost(4 * local_part.size, 2 * local_part.size),
    )(band, corners, local_part, low, high, *ends, result)


def exchange(blocks):
    return lax.all_to_all(blocks, "az", split_axis=0, concat_axis=0, tiled=True)


def per_device(fields, velocity, shifts, block_inverse, coupling):
    n = lax.axis_size("az")
    bands = lax.axis_size("rad")
    nf, levels, radii, width = fields.shape
    rows = levels * radii // n
    me = lax.axis_index("az")
    band = lax.axis_index("rad")

    gathered = exchange(pack(fields.reshape(nf, n, rows, width)))

    own_shifts = lax.dynamic_slice_in_dim(shifts, (me * rows) % radii, rows)
    shift_rows = jnp.broadcast_to(own_shifts[:, None], (rows, LANES))
    edge_speed = lax.ppermute(velocity[:, :, -1], "az", [(i, (i + 1) % n) for i in range(n)])
    back_speed = jnp.concatenate([edge_speed[:, :, None], velocity[:, :, :-1]], axis=2)
    corners = jnp.stack(
        [
            block_inverse[:, 0, 0],
            block_inverse[:, 0, -1],
            block_inverse[:, -1, 0],
            block_inverse[:, -1, -1],
            coupling[:, 0],
        ],
        axis=1,
    )
    all_corners = lax.all_gather(corners, "rad", axis=1, tiled=True)
    links = all_corners.reshape(levels, bands, 5)[:, :, 4]
    links_below = jnp.concatenate([jnp.zeros_like(links[:, :1]), links[:, :-1]], axis=1)
    link_below = lax.dynamic_index_in_dim(links_below, band, 1, keepdims=True)
    low = jnp.broadcast_to((link_below * block_inverse[:, :, 0])[:, :, None], (levels, radii, LANES))
    high = jnp.broadcast_to((coupling * block_inverse[:, :, -1])[:, :, None], (levels, radii, LANES))
    band_scalar = band[None].astype(jnp.int32)
    gathered, back_speed, all_corners, low, high, band_scalar, shift_rows = lax.optimization_barrier(
        (gathered, back_speed, all_corners, low, high, band_scalar, shift_rows)
    )

    received = exchange(turn(shift_rows, gathered))

    local_part, ends = energy_part(received, velocity, back_speed, block_inverse)
    if bands == 2:
        all_ends = [ends, lax.ppermute(ends, "rad", [(0, 1), (1, 0)])]
    else:
        all_ends = [lax.all_gather(ends, "rad", axis=0)]
    result = carry(nf, received, velocity, back_speed)
    return diffuse(band_scalar, all_corners, local_part, low, high, all_ends, result)


def solution(mesh):
    placed = (
        P(None, None, "rad", "az"),
        P(None, "rad", "az"),
        P("rad"),
        P(None, "rad", None),
        P(None, "rad"),
    )
    return jax.shard_map(
        per_device,
        mesh=mesh,
        in_specs=placed,
        out_specs=P(None, None, "rad", "az"),
        check_vma=False,
    )
```

```python
import functools

import jax
import jax.numpy as jnp
from jax import lax
from jax.experimental import pallas as pl
from jax.experimental.pallas import tpu as pltpu
from jax.sharding import PartitionSpec as P

LANES = 128
TILE_ROWS = 8
IN_VMEM = pl.BlockSpec(memory_space=pltpu.VMEM)
IN_HBM = pl.BlockSpec(memory_space=pltpu.HBM)
IN_SMEM = pl.BlockSpec(memory_space=pltpu.SMEM)
ROOMY = pltpu.CompilerParams(vmem_limit_bytes=24 * 1024 * 1024)


def cost(flops, moved):
    return pl.CostEstimate(flops=flops, bytes_accessed=4 * moved, transcendentals=0)


def turn_kernel(shift_ref, in_ref, out_ref):
    n, rows, width = in_ref.shape
    per_block = width // LANES
    tiles = n * per_block
    groups = rows // TILE_ROWS
    halo_row = per_block * rows
    lane = lax.broadcasted_iota(jnp.int32, (TILE_ROWS, LANES), 1)
    for block in range(n):
        out_ref[block, halo_row : halo_row + TILE_ROWS, :] = jnp.zeros((TILE_ROWS, LANES), jnp.float32)

    def one_group(group, _):
        here = pl.ds(pl.multiple_of(group * TILE_ROWS, TILE_ROWS), TILE_ROWS)
        shift = shift_ref[here, :]
        cells = shift & (LANES - 1)
        whole = shift >> 7
        source = (lane - cells) & (LANES - 1)
        own = lane >= cells
        turned = []
        for tile in range(tiles):
            block, part = divmod(tile, per_block)
            values = in_ref[block, here, part * LANES : (part + 1) * LANES]
            turned.append(jnp.take_along_axis(values, source, axis=1, mode="promise_in_bounds"))
        circle = [jnp.where(own, turned[tile], turned[tile - 1]) for tile in range(tiles)]
        step = 1
        while step < tiles:
            wanted = (whole & step) != 0
            circle = [jnp.where(wanted, circle[(tile - step) % tiles], circle[tile]) for tile in range(tiles)]
            step *= 2
        for tile in range(tiles):
            block, part = divmod(tile, per_block)
            row = pl.multiple_of((group * per_block + part) * TILE_ROWS, TILE_ROWS)
            out_ref[block, pl.ds(row, TILE_ROWS), :] = circle[tile]
        place = group * 2
        edge = (lane == place) | (lane == place + 1)
        for block in range(n):
            left = circle[(block * per_block - 1) % tiles]
            right = circle[((block + 1) * per_block) % tiles]
            both = pltpu.roll(jnp.where(lane == 0, right, left), place + 1, 1)
            target = out_ref.at[block, halo_row : halo_row + TILE_ROWS, :]
            target[...] = jnp.where(edge, both, target[...])
        return 0

    lax.fori_loop(0, groups, one_group, 0, unroll=4 if groups % 4 == 0 else 2 if groups % 2 == 0 else 1)


def turn(shift_rows, gathered):
    n, rows, width = gathered.shape
    shape = (n, (width // LANES) * rows + TILE_ROWS, LANES)
    return pl.pallas_call(
        turn_kernel,
        out_shape=jax.ShapeDtypeStruct(shape, jnp.float32),
        in_specs=[IN_VMEM] * 2,
        out_specs=IN_VMEM,
        compiler_params=ROOMY,
        cost_estimate=cost(10 * gathered.size, 2 * gathered.size),
    )(shift_rows, gathered)


def spread_kernel(low_ref, high_ref, low_out, high_out):
    low_out[...] = jnp.broadcast_to(low_ref[...], low_out.shape)
    high_out[...] = jnp.broadcast_to(high_ref[...], high_out.shape)


def spread(low, high):
    shape = low.shape[:-1] + (LANES,)
    return pl.pallas_call(
        spread_kernel,
        out_shape=[jax.ShapeDtypeStruct(shape, jnp.float32)] * 2,
        in_specs=[IN_VMEM] * 2,
        out_specs=[IN_VMEM] * 2,
        compiler_params=ROOMY,
        cost_estimate=cost(low.size, 2 * low.size * LANES),
    )(low, high)


def carry_level(fields, level, recv_ref, speed_ref, back_ref, store):
    levels, radii, width = speed_ref.shape
    per_block = width // LANES
    in_rows = recv_ref.shape[1]
    halo_row = in_rows - TILE_ROWS
    groups = halo_row // (per_block * TILE_ROWS)
    lane = lax.broadcasted_iota(jnp.int32, (TILE_ROWS, LANES), 1)
    first = lane == 0
    last = lane == LANES - 1
    for row in range(0, radii, TILE_ROWS):
        rates = []
        for part in range(per_block):
            cut = (level, slice(row, row + TILE_ROWS), slice(part * LANES, (part + 1) * LANES))
            speed = speed_ref[cut]
            back = back_ref[cut]
            rates.append(
                (
                    jnp.maximum(speed, 0.0),
                    jnp.minimum(speed, 0.0),
                    jnp.maximum(back, 0.0),
                    jnp.minimum(back, 0.0),
                )
            )
        for field in fields:
            piece, group = divmod(((field * levels + level) * radii + row) // TILE_ROWS, groups)
            halo = recv_ref[piece, halo_row : halo_row + TILE_ROWS, :]
            values = []
            for part in range(per_block):
                at = (group * per_block + part) * TILE_ROWS
                values.append(recv_ref[piece, at : at + TILE_ROWS, :])
            up = [pltpu.roll(halo, (LANES - 2 * group) % LANES, 1)]
            up += [pltpu.roll(one, 1, 1) for one in values]
            down = [pltpu.roll(one, LANES - 1, 1) for one in values]
            down.append(pltpu.roll(halo, (LANES - 2 - 2 * group) % LANES, 1))
            for part in range(per_block):
                here = values[part]
                behind = jnp.where(first, up[part], up[part + 1])
                ahead = jnp.where(last, down[part + 1], down[part])
                plus, minus, back_plus, back_minus = rates[part]
                outflow = plus * here + minus * ahead
                inflow = back_plus * behind + back_minus * here
                store(field, row, part * LANES, here - (outflow - inflow))


def energy_kernel(field, recv_ref, speed_ref, back_ref, inverse_ref, local_ref, ends_ref, moved):
    for level in range(speed_ref.shape[0]):

        def store(_, row, cell, values, level=level):
            moved[level, row : row + TILE_ROWS, cell : cell + LANES] = values

        carry_level([field], level, recv_ref, speed_ref, back_ref, store)
        local = jnp.dot(
            inverse_ref[level],
            moved[level],
            precision=lax.Precision.HIGHEST,
            preferred_element_type=jnp.float32,
        )
        local_ref[level] = local
        ends_ref[0, level : level + 1, :] = local[:1]
        ends_ref[1, level : level + 1, :] = local[-1:]


def energy_part(field, received, speed, back_speed, inverse):
    levels, radii, width = speed.shape
    return pl.pallas_call(
        functools.partial(energy_kernel, field),
        out_shape=[
            jax.ShapeDtypeStruct(speed.shape, jnp.float32),
            jax.ShapeDtypeStruct((2, levels, width), jnp.float32),
        ],
        in_specs=[IN_VMEM] * 4,
        out_specs=[IN_VMEM] * 2,
        scratch_shapes=[pltpu.VMEM(speed.shape, jnp.float32)],
        compiler_params=ROOMY,
        cost_estimate=cost(2 * speed.size * radii, 4 * speed.size),
    )(received, speed, back_speed, inverse)


def carry_kernel(recv_ref, speed_ref, back_ref, out_ref, held, sems):
    nf, levels = held.shape[:2]
    copies = []
    for level in range(levels):

        def store(field, row, cell, values, level=level):
            held[field, level, row : row + TILE_ROWS, cell : cell + LANES] = values

        carry_level(range(nf), level, recv_ref, speed_ref, back_ref, store)
        copies.append(
            pltpu.make_async_copy(held.at[:, level], out_ref.at[pl.ds(0, nf), level], sems.at[level])
        )
        copies[-1].start()
    for copy in copies:
        copy.wait()


def carry(nf, received, speed, back_speed):
    levels, radii, width = speed.shape
    return pl.pallas_call(
        carry_kernel,
        out_shape=jax.ShapeDtypeStruct((nf,) + speed.shape, jnp.float32),
        in_specs=[IN_VMEM] * 3,
        out_specs=IN_HBM,
        scratch_shapes=[
            pltpu.VMEM((nf - 1,) + speed.shape, jnp.float32),
            pltpu.SemaphoreType.DMA((levels,)),
        ],
        compiler_params=ROOMY,
        cost_estimate=cost(10 * nf * speed.size, 2 * nf * speed.size),
    )(received, speed, back_speed)


def solve_interfaces(first_row, last_row, corner):
    bands = len(first_row)
    crossings = bands - 1
    nothing = jnp.zeros_like(first_row[0])
    carry_base = nothing
    carry_slope = jnp.zeros_like(corner[0][0])
    records = []
    for crossing in range(crossings):
        link = corner[crossing][4]
        steepness = link * corner[crossing][3]
        offset = last_row[crossing]
        if crossing > 0:
            back_link = corner[crossing - 1][4] * corner[crossing][2]
            steepness = back_link * carry_slope + steepness
            offset = offset + back_link * carry_base
        fore_link = link * corner[crossing + 1][0]
        next_link = jnp.zeros_like(link)
        if crossing + 1 < crossings:
            next_link = corner[crossing + 1][4] * corner[crossing + 1][1]
        denominator = 1.0 - fore_link * steepness
        upper_base = (first_row[crossing + 1] + fore_link * offset) / denominator
        upper_slope = next_link / denominator
        carry_base = offset + steepness * upper_base
        carry_slope = steepness * upper_slope
        records.append((carry_base, carry_slope, upper_base, upper_slope))
    lower_values = [nothing] * crossings
    upper_values = [nothing] * crossings
    follow = nothing
    for crossing in reversed(range(crossings)):
        carry_base, carry_slope, upper_base, upper_slope = records[crossing]
        lower_values[crossing] = carry_base + carry_slope * follow
        upper_values[crossing] = upper_base + upper_slope * follow
        follow = upper_values[crossing]
    return [nothing] + lower_values, upper_values + [nothing]


def diffuse_kernel(band_ref, corner_ref, local_ref, low_ref, high_ref, *refs):
    end_refs, (_, out_ref, held, sems) = refs[:-4], refs[-4:]
    levels, _, width = local_ref.shape
    bands = corner_ref.shape[1] // 5
    band = band_ref[0]
    if len(end_refs) == 2:
        own, other = end_refs
        ends = [
            [jnp.where(band == j, own[side], other[side]) for j in range(bands)] for side in range(2)
        ]
    else:
        ends = [[end_refs[0][j, side] for j in range(bands)] for side in range(2)]
    corner = [[corner_ref[:, j * 5 + c : j * 5 + c + 1] for c in range(5)] for j in range(bands)]
    all_before, all_beyond = solve_interfaces(ends[0], ends[1], corner)
    before = beyond = jnp.zeros_like(ends[0][0])
    for j in range(bands):
        before = jnp.where(band == j, all_before[j], before)
        beyond = jnp.where(band == j, all_beyond[j], beyond)
    copies = []
    for level in range(levels):
        for cell in range(0, width, LANES):
            cut = slice(cell, cell + LANES)
            held[level, :, cut] = (
                local_ref[level, :, cut]
                + low_ref[level] * before[level : level + 1, cut]
                + high_ref[level] * beyond[level : level + 1, cut]
            )
        copies.append(
            pltpu.make_async_copy(held.at[level], out_ref.at[out_ref.shape[0] - 1, level], sems.at[level])
        )
        copies[-1].start()
    for copy in copies:
        copy.wait()


def diffuse(band, corners, local_part, low, high, ends, result):
    levels = local_part.shape[0]
    return pl.pallas_call(
        diffuse_kernel,
        out_shape=jax.ShapeDtypeStruct(result.shape, jnp.float32),
        in_specs=[IN_SMEM] + [IN_VMEM] * (4 + len(ends)) + [IN_HBM],
        out_specs=IN_HBM,
        scratch_shapes=[pltpu.VMEM(local_part.shape, jnp.float32), pltpu.SemaphoreType.DMA((levels,))],
        input_output_aliases={5 + len(ends): 0},
        compiler_params=ROOMY,
        cost_estimate=cost(4 * local_part.size, 2 * local_part.size),
    )(band, corners, local_part, low, high, *ends, result)


def exchange(blocks):
    return lax.all_to_all(blocks, "az", split_axis=0, concat_axis=0, tiled=True)


def per_device(fields, velocity, shifts, block_inverse, coupling):
    n = lax.axis_size("az")
    bands = lax.axis_size("rad")
    nf, levels, radii, width = fields.shape
    rows = nf * levels * radii // n
    me = lax.axis_index("az")
    band = lax.axis_index("rad")

    gathered = exchange(fields.reshape(n, rows, width))

    all_shifts = jnp.tile(shifts, rows // radii + 2)
    own_shifts = lax.dynamic_slice_in_dim(all_shifts, (me * rows) % radii, rows)
    shift_rows = jnp.broadcast_to(own_shifts[:, None], (rows, LANES))
    edge_speed = lax.ppermute(velocity[:, :, -1], "az", [(i, (i + 1) % n) for i in range(n)])
    back_speed = jnp.concatenate([edge_speed[:, :, None], velocity[:, :, :-1]], axis=2)
    corners = jnp.stack(
        [
            block_inverse[:, 0, 0],
            block_inverse[:, 0, -1],
            block_inverse[:, -1, 0],
            block_inverse[:, -1, -1],
            coupling[:, 0],
        ],
        axis=1,
    )
    all_corners = lax.all_gather(corners, "rad", axis=1, tiled=True)
    links = all_corners.reshape(levels, bands, 5)[:, :, 4]
    links_below = jnp.concatenate([jnp.zeros_like(links[:, :1]), links[:, :-1]], axis=1)
    link_below = lax.dynamic_index_in_dim(links_below, band, 1, keepdims=True)
    low, high = spread(
        (link_below * block_inverse[:, :, 0])[:, :, None], (coupling * block_inverse[:, :, -1])[:, :, None]
    )
    band_scalar = band[None].astype(jnp.int32)
    gathered, back_speed, all_corners, low, high, band_scalar, shift_rows = lax.optimization_barrier(
        (gathered, back_speed, all_corners, low, high, band_scalar, shift_rows)
    )

    received = exchange(turn(shift_rows, gathered))

    local_part, ends = energy_part(nf - 1, received, velocity, back_speed, block_inverse)
    if bands == 2:
        all_ends = [ends, lax.ppermute(ends, "rad", [(0, 1), (1, 0)])]
    else:
        all_ends = [lax.all_gather(ends, "rad", axis=0)]
    result = carry(nf, received, velocity, back_speed)
    return diffuse(band_scalar, all_corners, local_part, low, high, all_ends, result)


def solution(mesh):
    placed = (
        P(None, None, "rad", "az"),
        P(None, "rad", "az"),
        P("rad"),
        P(None, "rad", None),
        P(None, "rad"),
    )
    return jax.shard_map(
        per_device,
        mesh=mesh,
        in_specs=placed,
        out_specs=P(None, None, "rad", "az"),
        check_vma=False,
    )
```

```python
import functools

import jax
import jax.numpy as jnp
from jax import lax
from jax.experimental import pallas as pl
from jax.experimental.pallas import tpu as pltpu
from jax.sharding import PartitionSpec as P

LANES = 128
TILE_ROWS = 8
IN_VMEM = pl.BlockSpec(memory_space=pltpu.VMEM)
IN_HBM = pl.BlockSpec(memory_space=pltpu.HBM)
IN_SMEM = pl.BlockSpec(memory_space=pltpu.SMEM)
ROOMY = pltpu.CompilerParams(vmem_limit_bytes=24 * 1024 * 1024)


def cost(flops, moved):
    return pl.CostEstimate(flops=flops, bytes_accessed=4 * moved, transcendentals=0)


def group_order(n):
    return [(place % 2) * (n // 2) + place // 2 for place in range(n)]


def turn_kernel(shift_ref, in_ref, out_ref):
    n, rows, width = in_ref.shape
    order = group_order(n)
    places = [order.index(block) for block in range(n)]
    per_block = width // LANES
    tiles = n * per_block
    groups = rows // TILE_ROWS
    halo_row = per_block * rows
    lane = lax.broadcasted_iota(jnp.int32, (TILE_ROWS, LANES), 1)
    for block in range(n):
        out_ref[block, halo_row : halo_row + TILE_ROWS, :] = jnp.zeros((TILE_ROWS, LANES), jnp.float32)

    def one_group(group, _):
        here = pl.ds(pl.multiple_of(group * TILE_ROWS, TILE_ROWS), TILE_ROWS)
        shift = shift_ref[here, :]
        cells = shift & (LANES - 1)
        whole = shift >> 7
        source = (lane - cells) & (LANES - 1)
        own = lane >= cells
        turned = []
        for tile in range(tiles):
            block, part = divmod(tile, per_block)
            values = in_ref[places[block], here, part * LANES : (part + 1) * LANES]
            turned.append(jnp.take_along_axis(values, source, axis=1, mode="promise_in_bounds"))
        circle = [jnp.where(own, turned[tile], turned[tile - 1]) for tile in range(tiles)]
        step = 1
        while step < tiles:
            wanted = (whole & step) != 0
            circle = [jnp.where(wanted, circle[(tile - step) % tiles], circle[tile]) for tile in range(tiles)]
            step *= 2
        for tile in range(tiles):
            block, part = divmod(tile, per_block)
            row = pl.multiple_of((group * per_block + part) * TILE_ROWS, TILE_ROWS)
            out_ref[places[block], pl.ds(row, TILE_ROWS), :] = circle[tile]
        place = group * 2
        edge = (lane == place) | (lane == place + 1)
        for block in range(n):
            left = circle[(block * per_block - 1) % tiles]
            right = circle[((block + 1) * per_block) % tiles]
            both = pltpu.roll(jnp.where(lane == 0, right, left), place + 1, 1)
            target = out_ref.at[places[block], halo_row : halo_row + TILE_ROWS, :]
            target[...] = jnp.where(edge, both, target[...])
        return 0

    lax.fori_loop(0, groups, one_group, 0, unroll=4 if groups % 4 == 0 else 2 if groups % 2 == 0 else 1)


def turn(shift_rows, gathered):
    n, rows, width = gathered.shape
    shape = (n, (width // LANES) * rows + TILE_ROWS, LANES)
    return pl.pallas_call(
        turn_kernel,
        out_shape=jax.ShapeDtypeStruct(shape, jnp.float32),
        in_specs=[IN_VMEM] * 2,
        out_specs=IN_VMEM,
        compiler_params=ROOMY,
        cost_estimate=cost(10 * gathered.size, 2 * gathered.size),
    )(shift_rows, gathered)


def spread_kernel(low_ref, high_ref, low_out, high_out):
    low_out[...] = jnp.broadcast_to(low_ref[...], low_out.shape)
    high_out[...] = jnp.broadcast_to(high_ref[...], high_out.shape)


def spread(low, high):
    shape = low.shape[:-1] + (LANES,)
    return pl.pallas_call(
        spread_kernel,
        out_shape=[jax.ShapeDtypeStruct(shape, jnp.float32)] * 2,
        in_specs=[IN_VMEM] * 2,
        out_specs=[IN_VMEM] * 2,
        compiler_params=ROOMY,
        cost_estimate=cost(low.size, 2 * low.size * LANES),
    )(low, high)


def carry_level(fields, level, recv_ref, speed_ref, back_ref, store):
    levels, radii, width = speed_ref.shape
    per_block = width // LANES
    in_rows = recv_ref.shape[1]
    halo_row = in_rows - TILE_ROWS
    groups = halo_row // (per_block * TILE_ROWS)
    lane = lax.broadcasted_iota(jnp.int32, (TILE_ROWS, LANES), 1)
    first = lane == 0
    last = lane == LANES - 1
    for row in range(0, radii, TILE_ROWS):
        rates = []
        for part in range(per_block):
            cut = (level, slice(row, row + TILE_ROWS), slice(part * LANES, (part + 1) * LANES))
            speed = speed_ref[cut]
            back = back_ref[cut]
            rates.append(
                (
                    jnp.maximum(speed, 0.0),
                    jnp.minimum(speed, 0.0),
                    jnp.maximum(back, 0.0),
                    jnp.minimum(back, 0.0),
                )
            )
        for field in fields:
            piece, group = divmod(((field * levels + level) * radii + row) // TILE_ROWS, groups)
            halo = recv_ref[piece, halo_row : halo_row + TILE_ROWS, :]
            values = []
            for part in range(per_block):
                at = (group * per_block + part) * TILE_ROWS
                values.append(recv_ref[piece, at : at + TILE_ROWS, :])
            up = [pltpu.roll(halo, (LANES - 2 * group) % LANES, 1)]
            up += [pltpu.roll(one, 1, 1) for one in values]
            down = [pltpu.roll(one, LANES - 1, 1) for one in values]
            down.append(pltpu.roll(halo, (LANES - 2 - 2 * group) % LANES, 1))
            for part in range(per_block):
                here = values[part]
                behind = jnp.where(first, up[part], up[part + 1])
                ahead = jnp.where(last, down[part + 1], down[part])
                plus, minus, back_plus, back_minus = rates[part]
                outflow = plus * here + minus * ahead
                inflow = back_plus * behind + back_minus * here
                store(field, row, part * LANES, here - (outflow - inflow))


def energy_kernel(field, recv_ref, speed_ref, back_ref, inverse_ref, local_ref, ends_ref, moved):
    for level in range(speed_ref.shape[0]):

        def store(_, row, cell, values, level=level):
            moved[level, row : row + TILE_ROWS, cell : cell + LANES] = values

        carry_level([field], level, recv_ref, speed_ref, back_ref, store)
        local = jnp.dot(
            inverse_ref[level],
            moved[level],
            precision=lax.Precision.HIGHEST,
            preferred_element_type=jnp.float32,
        )
        local_ref[level] = local
        ends_ref[0, level : level + 1, :] = local[:1]
        ends_ref[1, level : level + 1, :] = local[-1:]


def energy_part(field, received, speed, back_speed, inverse):
    levels, radii, width = speed.shape
    return pl.pallas_call(
        functools.partial(energy_kernel, field),
        out_shape=[
            jax.ShapeDtypeStruct(speed.shape, jnp.float32),
            jax.ShapeDtypeStruct((2, levels, width), jnp.float32),
        ],
        in_specs=[IN_VMEM] * 4,
        out_specs=[IN_VMEM] * 2,
        scratch_shapes=[pltpu.VMEM(speed.shape, jnp.float32)],
        compiler_params=ROOMY,
        cost_estimate=cost(2 * speed.size * radii, 4 * speed.size),
    )(received, speed, back_speed, inverse)


def carry_kernel(recv_ref, speed_ref, back_ref, out_ref, held, sems):
    nf, levels = held.shape[:2]
    copies = []
    for level in range(levels):

        def store(field, row, cell, values, level=level):
            held[field, level, row : row + TILE_ROWS, cell : cell + LANES] = values

        carry_level(range(nf), level, recv_ref, speed_ref, back_ref, store)
        copies.append(
            pltpu.make_async_copy(held.at[:, level], out_ref.at[pl.ds(0, nf), level], sems.at[level])
        )
        copies[-1].start()
    for copy in copies:
        copy.wait()


def carry(nf, received, speed, back_speed):
    levels, radii, width = speed.shape
    return pl.pallas_call(
        carry_kernel,
        out_shape=jax.ShapeDtypeStruct((nf,) + speed.shape, jnp.float32),
        in_specs=[IN_VMEM] * 3,
        out_specs=IN_HBM,
        scratch_shapes=[
            pltpu.VMEM((nf - 1,) + speed.shape, jnp.float32),
            pltpu.SemaphoreType.DMA((levels,)),
        ],
        compiler_params=ROOMY,
        cost_estimate=cost(10 * nf * speed.size, 2 * nf * speed.size),
    )(received, speed, back_speed)


def solve_interfaces(first_row, last_row, corner):
    bands = len(first_row)
    crossings = bands - 1
    nothing = jnp.zeros_like(first_row[0])
    carry_base = nothing
    carry_slope = jnp.zeros_like(corner[0][0])
    records = []
    for crossing in range(crossings):
        link = corner[crossing][4]
        steepness = link * corner[crossing][3]
        offset = last_row[crossing]
        if crossing > 0:
            back_link = corner[crossing - 1][4] * corner[crossing][2]
            steepness = back_link * carry_slope + steepness
            offset = offset + back_link * carry_base
        fore_link = link * corner[crossing + 1][0]
        next_link = jnp.zeros_like(link)
        if crossing + 1 < crossings:
            next_link = corner[crossing + 1][4] * corner[crossing + 1][1]
        denominator = 1.0 - fore_link * steepness
        upper_base = (first_row[crossing + 1] + fore_link * offset) / denominator
        upper_slope = next_link / denominator
        carry_base = offset + steepness * upper_base
        carry_slope = steepness * upper_slope
        records.append((carry_base, carry_slope, upper_base, upper_slope))
    lower_values = [nothing] * crossings
    upper_values = [nothing] * crossings
    follow = nothing
    for crossing in reversed(range(crossings)):
        carry_base, carry_slope, upper_base, upper_slope = records[crossing]
        lower_values[crossing] = carry_base + carry_slope * follow
        upper_values[crossing] = upper_base + upper_slope * follow
        follow = upper_values[crossing]
    return [nothing] + lower_values, upper_values + [nothing]


def diffuse_kernel(band_ref, corner_ref, local_ref, low_ref, high_ref, *refs):
    end_refs, (_, out_ref, held, sems) = refs[:-4], refs[-4:]
    levels, _, width = local_ref.shape
    bands = corner_ref.shape[1] // 5
    band = band_ref[0]
    if len(end_refs) == 2:
        own, other = end_refs
        ends = [
            [jnp.where(band == j, own[side], other[side]) for j in range(bands)] for side in range(2)
        ]
    else:
        ends = [[end_refs[0][j, side] for j in range(bands)] for side in range(2)]
    corner = [[corner_ref[:, j * 5 + c : j * 5 + c + 1] for c in range(5)] for j in range(bands)]
    all_before, all_beyond = solve_interfaces(ends[0], ends[1], corner)
    before = beyond = jnp.zeros_like(ends[0][0])
    for j in range(bands):
        before = jnp.where(band == j, all_before[j], before)
        beyond = jnp.where(band == j, all_beyond[j], beyond)
    copies = []
    for level in range(levels):
        for cell in range(0, width, LANES):
            cut = slice(cell, cell + LANES)
            held[level, :, cut] = (
                local_ref[level, :, cut]
                + low_ref[level] * before[level : level + 1, cut]
                + high_ref[level] * beyond[level : level + 1, cut]
            )
        copies.append(
            pltpu.make_async_copy(held.at[level], out_ref.at[out_ref.shape[0] - 1, level], sems.at[level])
        )
        copies[-1].start()
    for copy in copies:
        copy.wait()


def diffuse(band, corners, local_part, low, high, ends, result):
    levels = local_part.shape[0]
    return pl.pallas_call(
        diffuse_kernel,
        out_shape=jax.ShapeDtypeStruct(result.shape, jnp.float32),
        in_specs=[IN_SMEM] + [IN_VMEM] * (4 + len(ends)) + [IN_HBM],
        out_specs=IN_HBM,
        scratch_shapes=[pltpu.VMEM(local_part.shape, jnp.float32), pltpu.SemaphoreType.DMA((levels,))],
        input_output_aliases={5 + len(ends): 0},
        compiler_params=ROOMY,
        cost_estimate=cost(4 * local_part.size, 2 * local_part.size),
    )(band, corners, local_part, low, high, *ends, result)


def exchange(blocks):
    order = group_order(blocks.shape[0])
    return lax.all_to_all(blocks, "az", split_axis=0, concat_axis=0, tiled=True, axis_index_groups=[order])


def per_device(fields, velocity, shifts, block_inverse, coupling):
    n = lax.axis_size("az")
    bands = lax.axis_size("rad")
    nf, levels, radii, width = fields.shape
    rows = nf * levels * radii // n
    order = group_order(n)
    places = jnp.array([order.index(block) for block in range(n)], jnp.int32)
    place = places[lax.axis_index("az")]
    band = lax.axis_index("rad")

    gathered = exchange(fields.reshape(n, rows, width))

    all_shifts = jnp.tile(shifts, rows // radii + 2)
    own_shifts = lax.dynamic_slice_in_dim(all_shifts, (place * rows) % radii, rows)
    shift_rows = jnp.broadcast_to(own_shifts[:, None], (rows, LANES))
    edge_speed = lax.ppermute(velocity[:, :, -1], "az", [(i, (i + 1) % n) for i in range(n)])
    back_speed = jnp.concatenate([edge_speed[:, :, None], velocity[:, :, :-1]], axis=2)
    corners = jnp.stack(
        [
            block_inverse[:, 0, 0],
            block_inverse[:, 0, -1],
            block_inverse[:, -1, 0],
            block_inverse[:, -1, -1],
            coupling[:, 0],
        ],
        axis=1,
    )
    all_corners = lax.all_gather(corners, "rad", axis=1, tiled=True)
    links = all_corners.reshape(levels, bands, 5)[:, :, 4]
    links_below = jnp.concatenate([jnp.zeros_like(links[:, :1]), links[:, :-1]], axis=1)
    link_below = lax.dynamic_index_in_dim(links_below, band, 1, keepdims=True)
    low, high = spread(
        (link_below * block_inverse[:, :, 0])[:, :, None], (coupling * block_inverse[:, :, -1])[:, :, None]
    )
    band_scalar = band[None].astype(jnp.int32)
    gathered, back_speed, all_corners, low, high, band_scalar, shift_rows = lax.optimization_barrier(
        (gathered, back_speed, all_corners, low, high, band_scalar, shift_rows)
    )

    received = exchange(turn(shift_rows, gathered))

    local_part, ends = energy_part(nf - 1, received, velocity, back_speed, block_inverse)
    if bands == 2:
        all_ends = [ends, lax.ppermute(ends, "rad", [(0, 1), (1, 0)])]
    else:
        all_ends = [lax.all_gather(ends, "rad", axis=0)]
    result = carry(nf, received, velocity, back_speed)
    return diffuse(band_scalar, all_corners, local_part, low, high, all_ends, result)


def solution(mesh):
    placed = (
        P(None, None, "rad", "az"),
        P(None, "rad", "az"),
        P("rad"),
        P(None, "rad", None),
        P(None, "rad"),
    )
    return jax.shard_map(
        per_device,
        mesh=mesh,
        in_specs=placed,
        out_specs=P(None, None, "rad", "az"),
        check_vma=False,
    )
```

```python
import functools

import jax
import jax.numpy as jnp
from jax import lax
from jax.experimental import pallas as pl
from jax.experimental.pallas import tpu as pltpu
from jax.sharding import PartitionSpec as P

LANES = 128
TILE_ROWS = 8
IN_VMEM = pl.BlockSpec(memory_space=pltpu.VMEM)
IN_HBM = pl.BlockSpec(memory_space=pltpu.HBM)
IN_SMEM = pl.BlockSpec(memory_space=pltpu.SMEM)
ROOMY = pltpu.CompilerParams(vmem_limit_bytes=24 * 1024 * 1024)


def cost(flops, moved):
    return pl.CostEstimate(flops=flops, bytes_accessed=4 * moved, transcendentals=0)


def turn_kernel(shift_ref, in_ref, out_ref):
    n, rows, width = in_ref.shape
    per_block = width // LANES
    tiles = n * per_block
    groups = rows // TILE_ROWS
    halo_row = per_block * rows
    lane = lax.broadcasted_iota(jnp.int32, (TILE_ROWS, LANES), 1)
    for block in range(n):
        out_ref[block, halo_row : halo_row + TILE_ROWS, :] = jnp.zeros((TILE_ROWS, LANES), jnp.float32)

    def one_group(group, _):
        here = pl.ds(pl.multiple_of(group * TILE_ROWS, TILE_ROWS), TILE_ROWS)
        shift = shift_ref[here, :]
        cells = shift & (LANES - 1)
        whole = shift >> 7
        source = (lane - cells) & (LANES - 1)
        own = lane >= cells
        turned = []
        for tile in range(tiles):
            block, part = divmod(tile, per_block)
            values = in_ref[block, here, part * LANES : (part + 1) * LANES]
            turned.append(jnp.take_along_axis(values, source, axis=1, mode="promise_in_bounds"))
        circle = [jnp.where(own, turned[tile], turned[tile - 1]) for tile in range(tiles)]
        step = 1
        while step < tiles:
            wanted = (whole & step) != 0
            circle = [jnp.where(wanted, circle[(tile - step) % tiles], circle[tile]) for tile in range(tiles)]
            step *= 2
        for tile in range(tiles):
            block, part = divmod(tile, per_block)
            row = pl.multiple_of((group * per_block + part) * TILE_ROWS, TILE_ROWS)
            out_ref[block, pl.ds(row, TILE_ROWS), :] = circle[tile]
        place = group * 2
        edge = (lane == place) | (lane == place + 1)
        for block in range(n):
            left = circle[(block * per_block - 1) % tiles]
            right = circle[((block + 1) * per_block) % tiles]
            both = pltpu.roll(jnp.where(lane == 0, right, left), place + 1, 1)
            target = out_ref.at[block, halo_row : halo_row + TILE_ROWS, :]
            target[...] = jnp.where(edge, both, target[...])
        return 0

    lax.fori_loop(0, groups, one_group, 0, unroll=4 if groups % 4 == 0 else 2 if groups % 2 == 0 else 1)


def turn(shift_rows, gathered):
    n, rows, width = gathered.shape
    shape = (n, (width // LANES) * rows + TILE_ROWS, LANES)
    return pl.pallas_call(
        turn_kernel,
        out_shape=jax.ShapeDtypeStruct(shape, jnp.float32),
        in_specs=[IN_VMEM] * 2,
        out_specs=IN_VMEM,
        compiler_params=ROOMY,
        cost_estimate=cost(10 * gathered.size, 2 * gathered.size),
    )(shift_rows, gathered)


def spread_kernel(low_ref, high_ref, low_out, high_out):
    low_out[...] = jnp.broadcast_to(low_ref[...], low_out.shape)
    high_out[...] = jnp.broadcast_to(high_ref[...], high_out.shape)


def spread(low, high):
    shape = low.shape[:-1] + (LANES,)
    return pl.pallas_call(
        spread_kernel,
        out_shape=[jax.ShapeDtypeStruct(shape, jnp.float32)] * 2,
        in_specs=[IN_VMEM] * 2,
        out_specs=[IN_VMEM] * 2,
        compiler_params=ROOMY,
        cost_estimate=cost(low.size, 2 * low.size * LANES),
    )(low, high)


def speed_parts(level, row, speed_ref, back_ref):
    rates = []
    for cell in range(0, speed_ref.shape[2], LANES):
        cut = (level, slice(row, row + TILE_ROWS), slice(cell, cell + LANES))
        speed = speed_ref[cut]
        back = back_ref[cut]
        rates.append(
            (
                jnp.maximum(speed, 0.0),
                jnp.minimum(speed, 0.0),
                jnp.maximum(back, 0.0),
                jnp.minimum(back, 0.0),
            )
        )
    return rates


def transport(values, left, right, rates):
    lane = lax.broadcasted_iota(jnp.int32, (TILE_ROWS, LANES), 1)
    up = [left] + [pltpu.roll(one, 1, 1) for one in values]
    down = [pltpu.roll(one, LANES - 1, 1) for one in values] + [right]
    moved = []
    for part, (plus, minus, back_plus, back_minus) in enumerate(rates):
        here = values[part]
        behind = jnp.where(lane == 0, up[part], up[part + 1])
        ahead = jnp.where(lane == LANES - 1, down[part + 1], down[part])
        outflow = plus * here + minus * ahead
        inflow = back_plus * behind + back_minus * here
        moved.append(here - (outflow - inflow))
    return moved


def energy_kernel(me_ref, shift_ref, circle_ref, speed_ref, back_ref, inverse_ref, local_ref, ends_ref, moved):
    n, _, radii, width = circle_ref.shape
    per_block = width // LANES
    tiles = n * per_block
    lane = lax.broadcasted_iota(jnp.int32, (TILE_ROWS, LANES), 1)
    for row in range(0, radii, TILE_ROWS):
        here = slice(row, row + TILE_ROWS)
        start = (me_ref[0] * width - shift_ref[here, :]) & (tiles * LANES - 1)
        offset = start & (LANES - 1)
        base = ((start >> 7) - 1) & (tiles - 1)
        found = []
        for tile in range(tiles):
            block, part = divmod(tile, per_block)
            found.append(circle_ref[block, 0, here, part * LANES : (part + 1) * LANES])
        step = tiles // 2
        while step > 0:
            count = min(len(found), step + per_block + 1)
            high = (base & step) != 0
            found = [
                jnp.where(high, found[(tile + step) % len(found)], found[tile]) for tile in range(count)
            ]
            step //= 2
        source = (lane + offset) & (LANES - 1)
        found = [jnp.take_along_axis(one, source, axis=1, mode="promise_in_bounds") for one in found]
        fits = lane < LANES - offset
        window = [jnp.where(fits, found[k], found[k + 1]) for k in range(per_block + 1)]
        left = pltpu.roll(window[0], 1, 1)
        right = pltpu.roll(found[per_block + 1], LANES - 1, 1)
        results = transport(window[1:], left, right, speed_parts(0, row, speed_ref, back_ref))
        for part, values in enumerate(results):
            moved[here, part * LANES : (part + 1) * LANES] = values
    local = jnp.dot(
        inverse_ref[0], moved[...], precision=lax.Precision.HIGHEST, preferred_element_type=jnp.float32
    )
    local_ref[0] = local
    level = pl.ds(pl.program_id(0), 1)
    ends_ref[0, level, :] = local[:1]
    ends_ref[1, level, :] = local[-1:]


def energy_part(me, shift_rows, circles, speed, back_speed, inverse):
    levels, radii, width = speed.shape
    n = circles.shape[0]
    plane = pl.BlockSpec((1, radii, width), lambda level: (level, 0, 0))
    return pl.pallas_call(
        energy_kernel,
        grid=(levels,),
        out_shape=[
            jax.ShapeDtypeStruct(speed.shape, jnp.float32),
            jax.ShapeDtypeStruct((2, levels, width), jnp.float32),
        ],
        in_specs=[
            IN_SMEM,
            pl.BlockSpec((radii, LANES), lambda level: (0, 0)),
            pl.BlockSpec((n, 1, radii, width), lambda level: (0, level, 0, 0)),
            plane,
            plane,
            pl.BlockSpec((1, radii, radii), lambda level: (level, 0, 0)),
        ],
        out_specs=[plane, pl.BlockSpec((2, levels, width), lambda level: (0, 0, 0))],
        scratch_shapes=[pltpu.VMEM((radii, width), jnp.float32)],
        compiler_params=ROOMY,
        cost_estimate=cost(2 * speed.size * radii, (n + 4) * speed.size),
    )(me, shift_rows, circles, speed, back_speed, inverse)


def carry_kernel(recv_ref, speed_ref, back_ref, energy_ref, out_ref, held, sems):
    nf, levels, radii, width = held.shape
    per_block = width // LANES
    halo_row = recv_ref.shape[1] - TILE_ROWS
    groups = halo_row // (per_block * TILE_ROWS)
    copies = [pltpu.make_async_copy(energy_ref, out_ref.at[nf], sems.at[levels])]
    copies[0].start()
    for level in range(levels):
        for row in range(0, radii, TILE_ROWS):
            rates = speed_parts(level, row, speed_ref, back_ref)
            for field in range(nf):
                piece, group = divmod(((field * levels + level) * radii + row) // TILE_ROWS, groups)
                halo = recv_ref[piece, halo_row : halo_row + TILE_ROWS, :]
                values = []
                for part in range(per_block):
                    at = (group * per_block + part) * TILE_ROWS
                    values.append(recv_ref[piece, at : at + TILE_ROWS, :])
                left = pltpu.roll(halo, (LANES - 2 * group) % LANES, 1)
                right = pltpu.roll(halo, (LANES - 2 - 2 * group) % LANES, 1)
                for part, result in enumerate(transport(values, left, right, rates)):
                    held[field, level, row : row + TILE_ROWS, part * LANES : (part + 1) * LANES] = result
        copies.append(
            pltpu.make_async_copy(held.at[:, level], out_ref.at[pl.ds(0, nf), level], sems.at[level])
        )
        copies[-1].start()
    for copy in copies:
        copy.wait()


def carry(received, speed, back_speed, energy):
    n, in_rows, _ = received.shape
    levels, radii, width = speed.shape
    nf = n * (in_rows - TILE_ROWS) * LANES // speed.size
    return pl.pallas_call(
        carry_kernel,
        out_shape=jax.ShapeDtypeStruct((nf + 1,) + speed.shape, jnp.float32),
        in_specs=[IN_VMEM] * 4,
        out_specs=IN_HBM,
        scratch_shapes=[
            pltpu.VMEM((nf,) + speed.shape, jnp.float32),
            pltpu.SemaphoreType.DMA((levels + 1,)),
        ],
        compiler_params=ROOMY,
        cost_estimate=cost(10 * nf * speed.size, 2 * nf * speed.size),
    )(received, speed, back_speed, energy)


def solve_interfaces(first_row, last_row, corner):
    bands = len(first_row)
    crossings = bands - 1
    nothing = jnp.zeros_like(first_row[0])
    carry_base = nothing
    carry_slope = jnp.zeros_like(corner[0][0])
    records = []
    for crossing in range(crossings):
        link = corner[crossing][4]
        steepness = link * corner[crossing][3]
        offset = last_row[crossing]
        if crossing > 0:
            back_link = corner[crossing - 1][4] * corner[crossing][2]
            steepness = back_link * carry_slope + steepness
            offset = offset + back_link * carry_base
        fore_link = link * corner[crossing + 1][0]
        next_link = jnp.zeros_like(link)
        if crossing + 1 < crossings:
            next_link = corner[crossing + 1][4] * corner[crossing + 1][1]
        denominator = 1.0 - fore_link * steepness
        upper_base = (first_row[crossing + 1] + fore_link * offset) / denominator
        upper_slope = next_link / denominator
        carry_base = offset + steepness * upper_base
        carry_slope = steepness * upper_slope
        records.append((carry_base, carry_slope, upper_base, upper_slope))
    lower_values = [nothing] * crossings
    upper_values = [nothing] * crossings
    follow = nothing
    for crossing in reversed(range(crossings)):
        carry_base, carry_slope, upper_base, upper_slope = records[crossing]
        lower_values[crossing] = carry_base + carry_slope * follow
        upper_values[crossing] = upper_base + upper_slope * follow
        follow = upper_values[crossing]
    return [nothing] + lower_values, upper_values + [nothing]


def diffuse_kernel(band_ref, corner_ref, local_ref, low_ref, high_ref, *refs):
    end_refs, out_ref = refs[:-1], refs[-1]
    levels, _, width = local_ref.shape
    bands = corner_ref.shape[1] // 5
    band = band_ref[0]
    if len(end_refs) == 2:
        own, other = end_refs
        ends = [
            [jnp.where(band == j, own[side], other[side]) for j in range(bands)] for side in range(2)
        ]
    else:
        ends = [[end_refs[0][j, side] for j in range(bands)] for side in range(2)]
    corner = [[corner_ref[:, j * 5 + c : j * 5 + c + 1] for c in range(5)] for j in range(bands)]
    all_before, all_beyond = solve_interfaces(ends[0], ends[1], corner)
    before = beyond = jnp.zeros_like(ends[0][0])
    for j in range(bands):
        before = jnp.where(band == j, all_before[j], before)
        beyond = jnp.where(band == j, all_beyond[j], beyond)
    for level in range(levels):
        for cell in range(0, width, LANES):
            cut = slice(cell, cell + LANES)
            out_ref[level, :, cut] = (
                local_ref[level, :, cut]
                + low_ref[level] * before[level : level + 1, cut]
                + high_ref[level] * beyond[level : level + 1, cut]
            )


def diffuse(band, corners, local_part, low, high, ends):
    return pl.pallas_call(
        diffuse_kernel,
        out_shape=jax.ShapeDtypeStruct(local_part.shape, jnp.float32),
        in_specs=[IN_SMEM] + [IN_VMEM] * (4 + len(ends)),
        out_specs=IN_VMEM,
        compiler_params=ROOMY,
        cost_estimate=cost(4 * local_part.size, 2 * local_part.size),
    )(band, corners, local_part, low, high, *ends)


def exchange(blocks):
    return lax.all_to_all(blocks, "az", split_axis=0, concat_axis=0, tiled=True)


def per_device(fields, velocity, shifts, block_inverse, coupling):
    n = lax.axis_size("az")
    bands = lax.axis_size("rad")
    nf, levels, radii, width = fields.shape
    rows = (nf - 1) * levels * radii // n
    me = lax.axis_index("az")
    band = lax.axis_index("rad")

    circles = lax.all_gather(fields[nf - 1], "az", axis=0)
    gathered = exchange(fields[: nf - 1].reshape(n, rows, width))

    all_shifts = jnp.tile(shifts, rows // radii + 2)
    own_shifts = lax.dynamic_slice_in_dim(all_shifts, (me * rows) % radii, rows)
    shift_rows = jnp.broadcast_to(own_shifts[:, None], (rows, LANES))
    edge_speed = lax.ppermute(velocity[:, :, -1], "az", [(i, (i + 1) % n) for i in range(n)])
    back_speed = jnp.concatenate([edge_speed[:, :, None], velocity[:, :, :-1]], axis=2)
    corners = jnp.stack(
        [
            block_inverse[:, 0, 0],
            block_inverse[:, 0, -1],
            block_inverse[:, -1, 0],
            block_inverse[:, -1, -1],
            coupling[:, 0],
        ],
        axis=1,
    )
    all_corners = lax.all_gather(corners, "rad", axis=1, tiled=True)
    links = all_corners.reshape(levels, bands, 5)[:, :, 4]
    links_below = jnp.concatenate([jnp.zeros_like(links[:, :1]), links[:, :-1]], axis=1)
    link_below = lax.dynamic_index_in_dim(links_below, band, 1, keepdims=True)
    low, high = spread(
        (link_below * block_inverse[:, :, 0])[:, :, None], (coupling * block_inverse[:, :, -1])[:, :, None]
    )
    band_scalar = band[None].astype(jnp.int32)
    me_scalar = me[None].astype(jnp.int32)
    all_shift_rows = jnp.broadcast_to(shifts[:, None], (radii, LANES))
    gathered, back_speed, all_corners, low, high, band_scalar, me_scalar, shift_rows, all_shift_rows = (
        lax.optimization_barrier(
            (
                gathered,
                back_speed,
                all_corners,
                low,
                high,
                band_scalar,
                me_scalar,
                shift_rows,
                all_shift_rows,
            )
        )
    )

    turned = turn(shift_rows, gathered)
    turned, circles = lax.optimization_barrier((turned, circles))
    received = exchange(turned)

    local_part, ends = energy_part(me_scalar, all_shift_rows, circles, velocity, back_speed, block_inverse)
    if bands == 2:
        all_ends = [ends, lax.ppermute(ends, "rad", [(0, 1), (1, 0)])]
    else:
        all_ends = [lax.all_gather(ends, "rad", axis=0)]
    energy = diffuse(band_scalar, all_corners, local_part, low, high, all_ends)
    return carry(received, velocity, back_speed, energy)


def solution(mesh):
    placed = (
        P(None, None, "rad", "az"),
        P(None, "rad", "az"),
        P("rad"),
        P(None, "rad", None),
        P(None, "rad"),
    )
    return jax.shard_map(
        per_device,
        mesh=mesh,
        in_specs=placed,
        out_specs=P(None, None, "rad", "az"),
        check_vma=False,
    )
```

```python
import functools

import jax
import jax.numpy as jnp
from jax import lax
from jax.experimental import pallas as pl
from jax.experimental.pallas import tpu as pltpu
from jax.sharding import PartitionSpec as P

LANES = 128
TILE_ROWS = 8
IN_VMEM = pl.BlockSpec(memory_space=pltpu.VMEM)
IN_HBM = pl.BlockSpec(memory_space=pltpu.HBM)
IN_SMEM = pl.BlockSpec(memory_space=pltpu.SMEM)
ROOMY = pltpu.CompilerParams(vmem_limit_bytes=24 * 1024 * 1024)


def cost(flops, moved):
    return pl.CostEstimate(flops=flops, bytes_accessed=4 * moved, transcendentals=0)


def turn_kernel(shift_ref, in_ref, out_ref):
    n, rows, width = in_ref.shape
    per_block = width // LANES
    tiles = n * per_block
    groups = rows // TILE_ROWS
    halo_row = per_block * rows
    lane = lax.broadcasted_iota(jnp.int32, (TILE_ROWS, LANES), 1)
    for block in range(n):
        out_ref[block, halo_row : halo_row + TILE_ROWS, :] = jnp.zeros((TILE_ROWS, LANES), jnp.float32)

    def one_group(group):
        here = pl.ds(group * TILE_ROWS, TILE_ROWS)
        shift = shift_ref[here, :]
        cells = shift & (LANES - 1)
        whole = shift >> 7
        source = (lane - cells) & (LANES - 1)
        own = lane >= cells
        turned = []
        for tile in range(tiles):
            block, part = divmod(tile, per_block)
            values = in_ref[block, here, part * LANES : (part + 1) * LANES]
            turned.append(jnp.take_along_axis(values, source, axis=1, mode="promise_in_bounds"))
        circle = [jnp.where(own, turned[tile], turned[tile - 1]) for tile in range(tiles)]
        step = 1
        while step < tiles:
            wanted = (whole & step) != 0
            circle = [jnp.where(wanted, circle[(tile - step) % tiles], circle[tile]) for tile in range(tiles)]
            step *= 2
        for tile in range(tiles):
            block, part = divmod(tile, per_block)
            row = (group * per_block + part) * TILE_ROWS
            out_ref[block, pl.ds(row, TILE_ROWS), :] = circle[tile]
        place = group * 2
        edge = (lane == place) | (lane == place + 1)
        for block in range(n):
            left = circle[(block * per_block - 1) % tiles]
            right = circle[((block + 1) * per_block) % tiles]
            both = pltpu.roll(jnp.where(lane == 0, right, left), place + 1, 1)
            target = out_ref.at[block, halo_row : halo_row + TILE_ROWS, :]
            target[...] = jnp.where(edge, both, target[...])

    for group in range(groups):
        one_group(group)


def turn(shift_rows, gathered):
    n, rows, width = gathered.shape
    shape = (n, (width // LANES) * rows + TILE_ROWS, LANES)
    return pl.pallas_call(
        turn_kernel,
        out_shape=jax.ShapeDtypeStruct(shape, jnp.float32),
        in_specs=[IN_VMEM] * 2,
        out_specs=IN_VMEM,
        compiler_params=ROOMY,
        cost_estimate=cost(10 * gathered.size, 2 * gathered.size),
    )(shift_rows, gathered)


def spread_kernel(low_ref, high_ref, low_out, high_out):
    low_out[...] = jnp.broadcast_to(low_ref[...], low_out.shape)
    high_out[...] = jnp.broadcast_to(high_ref[...], high_out.shape)


def spread(low, high):
    shape = low.shape[:-1] + (LANES,)
    return pl.pallas_call(
        spread_kernel,
        out_shape=[jax.ShapeDtypeStruct(shape, jnp.float32)] * 2,
        in_specs=[IN_VMEM] * 2,
        out_specs=[IN_VMEM] * 2,
        compiler_params=ROOMY,
        cost_estimate=cost(low.size, 2 * low.size * LANES),
    )(low, high)


def carry_level(fields, level, recv_ref, speed_ref, back_ref, store):
    levels, radii, width = speed_ref.shape
    per_block = width // LANES
    in_rows = recv_ref.shape[1]
    halo_row = in_rows - TILE_ROWS
    groups = halo_row // (per_block * TILE_ROWS)
    lane = lax.broadcasted_iota(jnp.int32, (TILE_ROWS, LANES), 1)
    first = lane == 0
    last = lane == LANES - 1
    for row in range(0, radii, TILE_ROWS):
        cuts = [
            (level, slice(row, row + TILE_ROWS), slice(part * LANES, (part + 1) * LANES))
            for part in range(per_block)
        ]
        rates = [(jnp.maximum(speed_ref[cut], 0.0), jnp.minimum(speed_ref[cut], 0.0)) for cut in cuts]
        back_plus = jnp.maximum(back_ref[cuts[0]], 0.0)
        back_minus = jnp.minimum(back_ref[cuts[0]], 0.0)
        for field in fields:
            piece, group = divmod(((field * levels + level) * radii + row) // TILE_ROWS, groups)
            halo = recv_ref[piece, halo_row : halo_row + TILE_ROWS, :]
            values = []
            for part in range(per_block):
                at = (group * per_block + part) * TILE_ROWS
                values.append(recv_ref[piece, at : at + TILE_ROWS, :])
            edge = pltpu.roll(halo, (LANES - 2 * group) % LANES, 1)
            inflow = [back_plus * edge + back_minus * values[0]]
            down = [pltpu.roll(one, LANES - 1, 1) for one in values]
            down.append(pltpu.roll(halo, (LANES - 2 - 2 * group) % LANES, 1))
            outflow = []
            for part, (plus, minus) in enumerate(rates):
                ahead = jnp.where(last, down[part + 1], down[part])
                outflow.append(plus * values[part] + minus * ahead)
                inflow.append(pltpu.roll(outflow[part], 1, 1))
            for part in range(per_block):
                behind = jnp.where(first, inflow[part], inflow[part + 1])
                store(field, row, part * LANES, values[part] - (outflow[part] - behind))


def energy_kernel(field, recv_ref, speed_ref, back_ref, inverse_ref, local_ref, ends_ref, moved):
    for level in range(speed_ref.shape[0]):

        def store(_, row, cell, values, level=level):
            moved[level, row : row + TILE_ROWS, cell : cell + LANES] = values

        carry_level([field], level, recv_ref, speed_ref, back_ref, store)
        local = jnp.dot(
            inverse_ref[level],
            moved[level],
            precision=lax.Precision.HIGHEST,
            preferred_element_type=jnp.float32,
        )
        local_ref[level] = local
        ends_ref[0, level : level + 1, :] = local[:1]
        ends_ref[1, level : level + 1, :] = local[-1:]


def energy_part(field, received, speed, back_speed, inverse):
    levels, radii, width = speed.shape
    return pl.pallas_call(
        functools.partial(energy_kernel, field),
        out_shape=[
            jax.ShapeDtypeStruct(speed.shape, jnp.float32),
            jax.ShapeDtypeStruct((2, levels, width), jnp.float32),
        ],
        in_specs=[IN_VMEM] * 4,
        out_specs=[IN_VMEM] * 2,
        scratch_shapes=[pltpu.VMEM(speed.shape, jnp.float32)],
        compiler_params=ROOMY,
        cost_estimate=cost(2 * speed.size * radii, 4 * speed.size),
    )(received, speed, back_speed, inverse)


def carry_kernel(recv_ref, speed_ref, back_ref, out_ref, held, sems):
    nf, levels = held.shape[:2]
    copies = []
    for level in range(levels):

        def store(field, row, cell, values, level=level):
            held[field, level, row : row + TILE_ROWS, cell : cell + LANES] = values

        carry_level(range(nf), level, recv_ref, speed_ref, back_ref, store)
        copies.append(
            pltpu.make_async_copy(held.at[:, level], out_ref.at[pl.ds(0, nf), level], sems.at[level])
        )
        copies[-1].start()
    for copy in copies:
        copy.wait()


def carry(nf, received, speed, back_speed):
    levels, radii, width = speed.shape
    return pl.pallas_call(
        carry_kernel,
        out_shape=jax.ShapeDtypeStruct((nf,) + speed.shape, jnp.float32),
        in_specs=[IN_VMEM] * 3,
        out_specs=IN_HBM,
        scratch_shapes=[
            pltpu.VMEM((nf - 1,) + speed.shape, jnp.float32),
            pltpu.SemaphoreType.DMA((levels,)),
        ],
        compiler_params=ROOMY,
        cost_estimate=cost(10 * nf * speed.size, 2 * nf * speed.size),
    )(received, speed, back_speed)


def solve_interfaces(first_row, last_row, corner):
    bands = len(first_row)
    crossings = bands - 1
    nothing = jnp.zeros_like(first_row[0])
    carry_base = nothing
    carry_slope = jnp.zeros_like(corner[0][0])
    records = []
    for crossing in range(crossings):
        link = corner[crossing][4]
        steepness = link * corner[crossing][3]
        offset = last_row[crossing]
        if crossing > 0:
            back_link = corner[crossing - 1][4] * corner[crossing][2]
            steepness = back_link * carry_slope + steepness
            offset = offset + back_link * carry_base
        fore_link = link * corner[crossing + 1][0]
        next_link = jnp.zeros_like(link)
        if crossing + 1 < crossings:
            next_link = corner[crossing + 1][4] * corner[crossing + 1][1]
        denominator = 1.0 - fore_link * steepness
        upper_base = (first_row[crossing + 1] + fore_link * offset) / denominator
        upper_slope = next_link / denominator
        carry_base = offset + steepness * upper_base
        carry_slope = steepness * upper_slope
        records.append((carry_base, carry_slope, upper_base, upper_slope))
    lower_values = [nothing] * crossings
    upper_values = [nothing] * crossings
    follow = nothing
    for crossing in reversed(range(crossings)):
        carry_base, carry_slope, upper_base, upper_slope = records[crossing]
        lower_values[crossing] = carry_base + carry_slope * follow
        upper_values[crossing] = upper_base + upper_slope * follow
        follow = upper_values[crossing]
    return [nothing] + lower_values, upper_values + [nothing]


def diffuse_kernel(band_ref, corner_ref, local_ref, low_ref, high_ref, *refs):
    end_refs, (_, out_ref, held, sems) = refs[:-4], refs[-4:]
    levels, _, width = local_ref.shape
    bands = corner_ref.shape[1] // 5
    band = band_ref[0]
    if len(end_refs) == 2:
        own, other = end_refs
        ends = [
            [jnp.where(band == j, own[side], other[side]) for j in range(bands)] for side in range(2)
        ]
    else:
        ends = [[end_refs[0][j, side] for j in range(bands)] for side in range(2)]
    corner = [[corner_ref[:, j * 5 + c : j * 5 + c + 1] for c in range(5)] for j in range(bands)]
    all_before, all_beyond = solve_interfaces(ends[0], ends[1], corner)
    before = beyond = jnp.zeros_like(ends[0][0])
    for j in range(bands):
        before = jnp.where(band == j, all_before[j], before)
        beyond = jnp.where(band == j, all_beyond[j], beyond)
    copies = []
    for level in range(levels):
        for cell in range(0, width, LANES):
            cut = slice(cell, cell + LANES)
            held[level, :, cut] = (
                local_ref[level, :, cut]
                + low_ref[level] * before[level : level + 1, cut]
                + high_ref[level] * beyond[level : level + 1, cut]
            )
        copies.append(
            pltpu.make_async_copy(held.at[level], out_ref.at[out_ref.shape[0] - 1, level], sems.at[level])
        )
        copies[-1].start()
    for copy in copies:
        copy.wait()


def diffuse(band, corners, local_part, low, high, ends, result):
    levels = local_part.shape[0]
    return pl.pallas_call(
        diffuse_kernel,
        out_shape=jax.ShapeDtypeStruct(result.shape, jnp.float32),
        in_specs=[IN_SMEM] + [IN_VMEM] * (4 + len(ends)) + [IN_HBM],
        out_specs=IN_HBM,
        scratch_shapes=[pltpu.VMEM(local_part.shape, jnp.float32), pltpu.SemaphoreType.DMA((levels,))],
        input_output_aliases={5 + len(ends): 0},
        compiler_params=ROOMY,
        cost_estimate=cost(4 * local_part.size, 2 * local_part.size),
    )(band, corners, local_part, low, high, *ends, result)


def exchange(blocks):
    return lax.all_to_all(blocks, "az", split_axis=0, concat_axis=0, tiled=True)


def per_device(fields, velocity, shifts, block_inverse, coupling):
    n = lax.axis_size("az")
    bands = lax.axis_size("rad")
    nf, levels, radii, width = fields.shape
    rows = nf * levels * radii // n
    me = lax.axis_index("az")
    band = lax.axis_index("rad")

    gathered = exchange(fields.reshape(n, rows, width))

    all_shifts = jnp.tile(shifts, rows // radii + 2)
    own_shifts = lax.dynamic_slice_in_dim(all_shifts, (me * rows) % radii, rows)
    shift_rows = jnp.broadcast_to(own_shifts[:, None], (rows, LANES))
    edge_speed = lax.ppermute(velocity[:, :, -1], "az", [(i, (i + 1) % n) for i in range(n)])
    back_speed = jnp.concatenate([edge_speed[:, :, None], velocity[:, :, :-1]], axis=2)
    corners = jnp.stack(
        [
            block_inverse[:, 0, 0],
            block_inverse[:, 0, -1],
            block_inverse[:, -1, 0],
            block_inverse[:, -1, -1],
            coupling[:, 0],
        ],
        axis=1,
    )
    all_corners = lax.all_gather(corners, "rad", axis=1, tiled=True)
    links = all_corners.reshape(levels, bands, 5)[:, :, 4]
    links_below = jnp.concatenate([jnp.zeros_like(links[:, :1]), links[:, :-1]], axis=1)
    link_below = lax.dynamic_index_in_dim(links_below, band, 1, keepdims=True)
    low, high = spread(
        (link_below * block_inverse[:, :, 0])[:, :, None], (coupling * block_inverse[:, :, -1])[:, :, None]
    )
    band_scalar = band[None].astype(jnp.int32)
    gathered, back_speed, all_corners, low, high, band_scalar, shift_rows = lax.optimization_barrier(
        (gathered, back_speed, all_corners, low, high, band_scalar, shift_rows)
    )

    received = exchange(turn(shift_rows, gathered))

    local_part, ends = energy_part(nf - 1, received, velocity, back_speed, block_inverse)
    if bands == 2:
        all_ends = [ends, lax.ppermute(ends, "rad", [(0, 1), (1, 0)])]
    else:
        all_ends = [lax.all_gather(ends, "rad", axis=0)]
    result = carry(nf, received, velocity, back_speed)
    return diffuse(band_scalar, all_corners, local_part, low, high, all_ends, result)


def solution(mesh):
    placed = (
        P(None, None, "rad", "az"),
        P(None, "rad", "az"),
        P("rad"),
        P(None, "rad", None),
        P(None, "rad"),
    )
    return jax.shard_map(
        per_device,
        mesh=mesh,
        in_specs=placed,
        out_specs=P(None, None, "rad", "az"),
        check_vma=False,
    )
```

```python
import functools

import jax
import jax.numpy as jnp
from jax import lax
from jax.experimental import pallas as pl
from jax.experimental.pallas import tpu as pltpu
from jax.sharding import PartitionSpec as P

LANES = 128
TILE_ROWS = 8
IN_VMEM = pl.BlockSpec(memory_space=pltpu.VMEM)
IN_HBM = pl.BlockSpec(memory_space=pltpu.HBM)
IN_SMEM = pl.BlockSpec(memory_space=pltpu.SMEM)
ROOMY = pltpu.CompilerParams(vmem_limit_bytes=24 * 1024 * 1024)


def cost(flops, moved):
    return pl.CostEstimate(flops=flops, bytes_accessed=4 * moved, transcendentals=0)


def place_of(device, n):
    return (device + n - n // 4) % n


def turn_kernel(shift_ref, in_ref, out_ref):
    n, rows, width = in_ref.shape
    places = [place_of(block, n) for block in range(n)]
    per_block = width // LANES
    tiles = n * per_block
    groups = rows // TILE_ROWS
    halo_row = per_block * rows
    lane = lax.broadcasted_iota(jnp.int32, (TILE_ROWS, LANES), 1)
    for block in range(n):
        out_ref[block, halo_row : halo_row + TILE_ROWS, :] = jnp.zeros((TILE_ROWS, LANES), jnp.float32)

    def one_group(group):
        here = pl.ds(group * TILE_ROWS, TILE_ROWS)
        shift = shift_ref[here, :]
        cells = shift & (LANES - 1)
        whole = shift >> 7
        source = (lane - cells) & (LANES - 1)
        own = lane >= cells
        turned = []
        for tile in range(tiles):
            block, part = divmod(tile, per_block)
            values = in_ref[places[block], here, part * LANES : (part + 1) * LANES]
            turned.append(jnp.take_along_axis(values, source, axis=1, mode="promise_in_bounds"))
        circle = [jnp.where(own, turned[tile], turned[tile - 1]) for tile in range(tiles)]
        step = 1
        while step < tiles:
            wanted = (whole & step) != 0
            circle = [jnp.where(wanted, circle[(tile - step) % tiles], circle[tile]) for tile in range(tiles)]
            step *= 2
        for tile in range(tiles):
            block, part = divmod(tile, per_block)
            row = (group * per_block + part) * TILE_ROWS
            out_ref[places[block], pl.ds(row, TILE_ROWS), :] = circle[tile]
        place = group * 2
        edge = (lane == place) | (lane == place + 1)
        for block in range(n):
            left = circle[(block * per_block - 1) % tiles]
            right = circle[((block + 1) * per_block) % tiles]
            both = pltpu.roll(jnp.where(lane == 0, right, left), place + 1, 1)
            target = out_ref.at[places[block], halo_row : halo_row + TILE_ROWS, :]
            target[...] = jnp.where(edge, both, target[...])

    for group in range(groups):
        one_group(group)


def turn(shift_rows, gathered):
    n, rows, width = gathered.shape
    shape = (n, (width // LANES) * rows + TILE_ROWS, LANES)
    return pl.pallas_call(
        turn_kernel,
        out_shape=jax.ShapeDtypeStruct(shape, jnp.float32),
        in_specs=[IN_VMEM] * 2,
        out_specs=IN_VMEM,
        compiler_params=ROOMY,
        cost_estimate=cost(10 * gathered.size, 2 * gathered.size),
    )(shift_rows, gathered)


def spread_kernel(low_ref, high_ref, low_out, high_out):
    low_out[...] = jnp.broadcast_to(low_ref[...], low_out.shape)
    high_out[...] = jnp.broadcast_to(high_ref[...], high_out.shape)


def spread(low, high):
    shape = low.shape[:-1] + (LANES,)
    return pl.pallas_call(
        spread_kernel,
        out_shape=[jax.ShapeDtypeStruct(shape, jnp.float32)] * 2,
        in_specs=[IN_VMEM] * 2,
        out_specs=[IN_VMEM] * 2,
        compiler_params=ROOMY,
        cost_estimate=cost(low.size, 2 * low.size * LANES),
    )(low, high)


def carry_level(fields, level, recv_ref, speed_ref, back_ref, known, store):
    levels, radii, width = speed_ref.shape
    per_block = width // LANES
    in_rows = recv_ref.shape[1]
    halo_row = in_rows - TILE_ROWS
    groups = halo_row // (per_block * TILE_ROWS)
    lane = lax.broadcasted_iota(jnp.int32, (TILE_ROWS, LANES), 1)
    first = lane == 0
    last = lane == LANES - 1

    def edges(piece, group):
        key = (piece, group)
        if key not in known:
            known[key] = pltpu.roll(recv_ref[piece, halo_row:in_rows, :], (LANES - 2 * group) % LANES, 1)
        return known[key]

    for row in range(0, radii, TILE_ROWS):
        rates = []
        for part in range(per_block):
            cut = (level, slice(row, row + TILE_ROWS), slice(part * LANES, (part + 1) * LANES))
            speed = speed_ref[cut]
            back = back_ref[cut]
            rates.append(
                (
                    jnp.maximum(speed, 0.0),
                    jnp.minimum(speed, 0.0),
                    jnp.maximum(back, 0.0),
                    jnp.minimum(back, 0.0),
                )
            )
        for field in fields:
            piece, group = divmod(((field * levels + level) * radii + row) // TILE_ROWS, groups)
            values = []
            for part in range(per_block):
                at = (group * per_block + part) * TILE_ROWS
                values.append(recv_ref[piece, at : at + TILE_ROWS, :])
            up = [edges(piece, group)]
            up += [pltpu.roll(one, 1, 1) for one in values]
            down = [pltpu.roll(one, LANES - 1, 1) for one in values]
            down.append(edges(piece, group + 1))
            for part in range(per_block):
                here = values[part]
                behind = jnp.where(first, up[part], up[part + 1])
                ahead = jnp.where(last, down[part + 1], down[part])
                plus, minus, back_plus, back_minus = rates[part]
                outflow = plus * here + minus * ahead
                inflow = back_plus * behind + back_minus * here
                store(field, row, part * LANES, here - (outflow - inflow))


def energy_kernel(field, recv_ref, speed_ref, back_ref, inverse_ref, local_ref, ends_ref, moved):
    known = {}
    for level in range(speed_ref.shape[0]):

        def store(_, row, cell, values, level=level):
            moved[level, row : row + TILE_ROWS, cell : cell + LANES] = values

        carry_level([field], level, recv_ref, speed_ref, back_ref, known, store)
        local = jnp.dot(
            inverse_ref[level],
            moved[level],
            precision=lax.Precision.HIGHEST,
            preferred_element_type=jnp.float32,
        )
        local_ref[level] = local
        ends_ref[0, level : level + 1, :] = local[:1]
        ends_ref[1, level : level + 1, :] = local[-1:]


def energy_part(field, received, speed, back_speed, inverse):
    levels, radii, width = speed.shape
    return pl.pallas_call(
        functools.partial(energy_kernel, field),
        out_shape=[
            jax.ShapeDtypeStruct(speed.shape, jnp.float32),
            jax.ShapeDtypeStruct((2, levels, width), jnp.float32),
        ],
        in_specs=[IN_VMEM] * 4,
        out_specs=[IN_VMEM] * 2,
        scratch_shapes=[pltpu.VMEM(speed.shape, jnp.float32)],
        compiler_params=ROOMY,
        cost_estimate=cost(2 * speed.size * radii, 4 * speed.size),
    )(received, speed, back_speed, inverse)


def carry_kernel(recv_ref, speed_ref, back_ref, out_ref, held, sems):
    nf, levels = held.shape[:2]
    copies = []
    known = {}
    for level in range(levels):

        def store(field, row, cell, values, level=level):
            held[field, level, row : row + TILE_ROWS, cell : cell + LANES] = values

        carry_level(range(nf), level, recv_ref, speed_ref, back_ref, known, store)
        copies.append(
            pltpu.make_async_copy(held.at[:, level], out_ref.at[pl.ds(0, nf), level], sems.at[level])
        )
        copies[-1].start()
    for copy in copies:
        copy.wait()


def carry(nf, count, received, speed, back_speed):
    levels, radii, width = speed.shape
    return pl.pallas_call(
        carry_kernel,
        out_shape=jax.ShapeDtypeStruct((nf,) + speed.shape, jnp.float32),
        in_specs=[IN_VMEM] * 3,
        out_specs=IN_HBM,
        scratch_shapes=[
            pltpu.VMEM((count,) + speed.shape, jnp.float32),
            pltpu.SemaphoreType.DMA((levels,)),
        ],
        compiler_params=ROOMY,
        cost_estimate=cost(10 * count * speed.size, 2 * count * speed.size),
    )(received, speed, back_speed)


def solve_interfaces(first_row, last_row, corner):
    bands = len(first_row)
    crossings = bands - 1
    nothing = jnp.zeros_like(first_row[0])
    carry_base = nothing
    carry_slope = jnp.zeros_like(corner[0][0])
    records = []
    for crossing in range(crossings):
        link = corner[crossing][4]
        steepness = link * corner[crossing][3]
        offset = last_row[crossing]
        if crossing > 0:
            back_link = corner[crossing - 1][4] * corner[crossing][2]
            steepness = back_link * carry_slope + steepness
            offset = offset + back_link * carry_base
        fore_link = link * corner[crossing + 1][0]
        next_link = jnp.zeros_like(link)
        if crossing + 1 < crossings:
            next_link = corner[crossing + 1][4] * corner[crossing + 1][1]
        denominator = 1.0 - fore_link * steepness
        upper_base = (first_row[crossing + 1] + fore_link * offset) / denominator
        upper_slope = next_link / denominator
        carry_base = offset + steepness * upper_base
        carry_slope = steepness * upper_slope
        records.append((carry_base, carry_slope, upper_base, upper_slope))
    lower_values = [nothing] * crossings
    upper_values = [nothing] * crossings
    follow = nothing
    for crossing in reversed(range(crossings)):
        carry_base, carry_slope, upper_base, upper_slope = records[crossing]
        lower_values[crossing] = carry_base + carry_slope * follow
        upper_values[crossing] = upper_base + upper_slope * follow
        follow = upper_values[crossing]
    return [nothing] + lower_values, upper_values + [nothing]


def finish_kernel(band_ref, corner_ref, local_ref, low_ref, high_ref, recv_ref, speed_ref, back_ref, *refs):
    end_refs, (_, out_ref, held, sems) = refs[:-4], refs[-4:]
    nf = out_ref.shape[0]
    begin = nf - held.shape[0]
    levels, _, width = local_ref.shape
    bands = corner_ref.shape[1] // 5
    band = band_ref[0]
    if len(end_refs) == 2:
        own, other = end_refs
        ends = [
            [jnp.where(band == j, own[side], other[side]) for j in range(bands)] for side in range(2)
        ]
    else:
        ends = [[end_refs[0][j, side] for j in range(bands)] for side in range(2)]
    corner = [[corner_ref[:, j * 5 + c : j * 5 + c + 1] for c in range(5)] for j in range(bands)]
    all_before, all_beyond = solve_interfaces(ends[0], ends[1], corner)
    before = beyond = jnp.zeros_like(ends[0][0])
    for j in range(bands):
        before = jnp.where(band == j, all_before[j], before)
        beyond = jnp.where(band == j, all_beyond[j], beyond)
    copies = []
    known = {}
    for level in range(levels):

        def store(field, row, cell, values, level=level):
            held[field - begin, level, row : row + TILE_ROWS, cell : cell + LANES] = values

        for cell in range(0, width, LANES):
            cut = slice(cell, cell + LANES)
            held[nf - 1 - begin, level, :, cut] = (
                local_ref[level, :, cut]
                + low_ref[level] * before[level : level + 1, cut]
                + high_ref[level] * beyond[level : level + 1, cut]
            )
        carry_level(range(begin, nf - 1), level, recv_ref, speed_ref, back_ref, known, store)
        copies.append(
            pltpu.make_async_copy(
                held.at[:, level], out_ref.at[pl.ds(begin, nf - begin), level], sems.at[level]
            )
        )
        copies[-1].start()
    for copy in copies:
        copy.wait()


def finish(count, band, corners, local_part, low, high, received, speed, back_speed, ends, result):
    levels = local_part.shape[0]
    return pl.pallas_call(
        finish_kernel,
        out_shape=jax.ShapeDtypeStruct(result.shape, jnp.float32),
        in_specs=[IN_SMEM] + [IN_VMEM] * (7 + len(ends)) + [IN_HBM],
        out_specs=IN_HBM,
        scratch_shapes=[
            pltpu.VMEM((count,) + local_part.shape, jnp.float32),
            pltpu.SemaphoreType.DMA((levels,)),
        ],
        input_output_aliases={8 + len(ends): 0},
        compiler_params=ROOMY,
        cost_estimate=cost(10 * count * local_part.size, 2 * count * local_part.size),
    )(band, corners, local_part, low, high, received, speed, back_speed, *ends, result)


def exchange(blocks):
    n = blocks.shape[0]
    order = sorted(range(n), key=lambda device: place_of(device, n))
    return lax.all_to_all(blocks, "az", split_axis=0, concat_axis=0, tiled=True, axis_index_groups=[order])


def per_device(fields, velocity, shifts, block_inverse, coupling):
    n = lax.axis_size("az")
    bands = lax.axis_size("rad")
    nf, levels, radii, width = fields.shape
    rows = nf * levels * radii // n
    me = lax.axis_index("az")
    band = lax.axis_index("rad")

    gathered = exchange(fields.reshape(n, rows, width))

    all_shifts = jnp.tile(shifts, rows // radii + 2)
    own_shifts = lax.dynamic_slice_in_dim(all_shifts, (place_of(me, n) * rows) % radii, rows)
    shift_rows = jnp.broadcast_to(own_shifts[:, None], (rows, LANES))
    edge_speed = lax.ppermute(velocity[:, :, -1], "az", [(i, (i + 1) % n) for i in range(n)])
    back_speed = jnp.concatenate([edge_speed[:, :, None], velocity[:, :, :-1]], axis=2)
    corners = jnp.stack(
        [
            block_inverse[:, 0, 0],
            block_inverse[:, 0, -1],
            block_inverse[:, -1, 0],
            block_inverse[:, -1, -1],
            coupling[:, 0],
        ],
        axis=1,
    )
    all_corners = lax.all_gather(corners, "rad", axis=1, tiled=True)
    links = all_corners.reshape(levels, bands, 5)[:, :, 4]
    links_below = jnp.concatenate([jnp.zeros_like(links[:, :1]), links[:, :-1]], axis=1)
    link_below = lax.dynamic_index_in_dim(links_below, band, 1, keepdims=True)
    low, high = spread(
        (link_below * block_inverse[:, :, 0])[:, :, None], (coupling * block_inverse[:, :, -1])[:, :, None]
    )
    band_scalar = band[None].astype(jnp.int32)
    gathered, back_speed, all_corners, low, high, band_scalar, shift_rows = lax.optimization_barrier(
        (gathered, back_speed, all_corners, low, high, band_scalar, shift_rows)
    )

    received = exchange(turn(shift_rows, gathered))

    local_part, ends = energy_part(nf - 1, received, velocity, back_speed, block_inverse)
    if bands == 2:
        all_ends = [ends, lax.ppermute(ends, "rad", [(0, 1), (1, 0)])]
    else:
        all_ends = [lax.all_gather(ends, "rad", axis=0)]
    first = nf // 2
    result = carry(nf, first, received, velocity, back_speed)
    return finish(
        nf - first,
        band_scalar,
        all_corners,
        local_part,
        low,
        high,
        received,
        velocity,
        back_speed,
        all_ends,
        result,
    )


def solution(mesh):
    placed = (
        P(None, None, "rad", "az"),
        P(None, "rad", "az"),
        P("rad"),
        P(None, "rad", None),
        P(None, "rad"),
    )
    return jax.shard_map(
        per_device,
        mesh=mesh,
        in_specs=placed,
        out_specs=P(None, None, "rad", "az"),
        check_vma=False,
    )
```

```python
import functools

import jax
import jax.numpy as jnp
from jax import lax
from jax.experimental import pallas as pl
from jax.experimental.pallas import tpu as pltpu
from jax.sharding import PartitionSpec as P

LANES = 128
TILE_ROWS = 8
IN_VMEM = pl.BlockSpec(memory_space=pltpu.VMEM)
IN_HBM = pl.BlockSpec(memory_space=pltpu.HBM)
IN_SMEM = pl.BlockSpec(memory_space=pltpu.SMEM)
ROOMY = pltpu.CompilerParams(vmem_limit_bytes=24 * 1024 * 1024)


def cost(flops, moved):
    return pl.CostEstimate(flops=flops, bytes_accessed=4 * moved, transcendentals=0)


def place_of(device, n):
    return (device + n - n // 4) % n


def turn_kernel(shift_ref, in_ref, out_ref):
    n, rows, width = in_ref.shape
    places = [place_of(block, n) for block in range(n)]
    per_block = width // LANES
    tiles = n * per_block
    groups = rows // TILE_ROWS
    halo_row = per_block * rows
    lane = lax.broadcasted_iota(jnp.int32, (TILE_ROWS, LANES), 1)
    for block in range(n):
        out_ref[block, halo_row : halo_row + TILE_ROWS, :] = jnp.zeros((TILE_ROWS, LANES), jnp.float32)

    def one_group(group):
        here = pl.ds(group * TILE_ROWS, TILE_ROWS)
        shift = shift_ref[here, :]
        cells = shift & (LANES - 1)
        whole = shift >> 7
        source = (lane - cells) & (LANES - 1)
        own = lane >= cells
        turned = []
        for tile in range(tiles):
            block, part = divmod(tile, per_block)
            values = in_ref[places[block], here, part * LANES : (part + 1) * LANES]
            turned.append(jnp.take_along_axis(values, source, axis=1, mode="promise_in_bounds"))
        circle = [jnp.where(own, turned[tile], turned[tile - 1]) for tile in range(tiles)]
        step = 1
        while step < tiles:
            wanted = (whole & step) != 0
            circle = [jnp.where(wanted, circle[(tile - step) % tiles], circle[tile]) for tile in range(tiles)]
            step *= 2
        for tile in range(tiles):
            block, part = divmod(tile, per_block)
            row = (group * per_block + part) * TILE_ROWS
            out_ref[places[block], pl.ds(row, TILE_ROWS), :] = circle[tile]
        place = group * 2
        edge = (lane == place) | (lane == place + 1)
        for block in range(n):
            left = circle[(block * per_block - 1) % tiles]
            right = circle[((block + 1) * per_block) % tiles]
            both = pltpu.roll(jnp.where(lane == 0, right, left), place + 1, 1)
            target = out_ref.at[places[block], halo_row : halo_row + TILE_ROWS, :]
            target[...] = jnp.where(edge, both, target[...])

    for group in range(groups):
        one_group(group)


def turn(shift_rows, gathered):
    n, rows, width = gathered.shape
    shape = (n, (width // LANES) * rows + TILE_ROWS, LANES)
    return pl.pallas_call(
        turn_kernel,
        out_shape=jax.ShapeDtypeStruct(shape, jnp.float32),
        in_specs=[IN_VMEM] * 2,
        out_specs=IN_VMEM,
        compiler_params=ROOMY,
        cost_estimate=cost(10 * gathered.size, 2 * gathered.size),
    )(shift_rows, gathered)


def spread_kernel(low_ref, high_ref, low_out, high_out):
    low_out[...] = jnp.broadcast_to(low_ref[...], low_out.shape)
    high_out[...] = jnp.broadcast_to(high_ref[...], high_out.shape)


def spread(low, high):
    shape = low.shape[:-1] + (LANES,)
    return pl.pallas_call(
        spread_kernel,
        out_shape=[jax.ShapeDtypeStruct(shape, jnp.float32)] * 2,
        in_specs=[IN_VMEM] * 2,
        out_specs=[IN_VMEM] * 2,
        compiler_params=ROOMY,
        cost_estimate=cost(low.size, 2 * low.size * LANES),
    )(low, high)


def carry_level(fields, level, recv_ref, speed_ref, back_ref, known, store):
    levels, radii, width = speed_ref.shape
    per_block = width // LANES
    in_rows = recv_ref.shape[1]
    halo_row = in_rows - TILE_ROWS
    groups = halo_row // (per_block * TILE_ROWS)
    lane = lax.broadcasted_iota(jnp.int32, (TILE_ROWS, LANES), 1)
    first = lane == 0
    last = lane == LANES - 1

    def edges(piece, group):
        key = (piece, group)
        if key not in known:
            known[key] = pltpu.roll(recv_ref[piece, halo_row:in_rows, :], (LANES - 2 * group) % LANES, 1)
        return known[key]

    for row in range(0, radii, TILE_ROWS):
        rates = []
        for part in range(per_block):
            cut = (level, slice(row, row + TILE_ROWS), slice(part * LANES, (part + 1) * LANES))
            speed = speed_ref[cut]
            back = back_ref[cut]
            rates.append(
                (
                    jnp.maximum(speed, 0.0),
                    jnp.minimum(speed, 0.0),
                    jnp.maximum(back, 0.0),
                    jnp.minimum(back, 0.0),
                )
            )
        for field in fields:
            piece, group = divmod(((field * levels + level) * radii + row) // TILE_ROWS, groups)
            values = []
            for part in range(per_block):
                at = (group * per_block + part) * TILE_ROWS
                values.append(recv_ref[piece, at : at + TILE_ROWS, :])
            up = [edges(piece, group)]
            up += [pltpu.roll(one, 1, 1) for one in values]
            down = [pltpu.roll(one, LANES - 1, 1) for one in values]
            down.append(edges(piece, group + 1))
            for part in range(per_block):
                here = values[part]
                behind = jnp.where(first, up[part], up[part + 1])
                ahead = jnp.where(last, down[part + 1], down[part])
                plus, minus, back_plus, back_minus = rates[part]
                outflow = plus * here + minus * ahead
                inflow = back_plus * behind + back_minus * here
                store(field, row, part * LANES, here - (outflow - inflow))


def energy_kernel(field, recv_ref, speed_ref, back_ref, inverse_ref, moved_ref, ends_ref):
    levels, radii, _ = speed_ref.shape
    known = {}
    for level in range(levels):

        def store(_, row, cell, values, level=level):
            moved_ref[level, row : row + TILE_ROWS, cell : cell + LANES] = values

        carry_level([field], level, recv_ref, speed_ref, back_ref, known, store)
        outer = jnp.concatenate([inverse_ref[level, :TILE_ROWS], inverse_ref[level, radii - TILE_ROWS :]])
        ends = exact_product(outer, moved_ref[level])
        ends_ref[0, level : level + 1, :] = ends[:1]
        ends_ref[1, level : level + 1, :] = ends[-1:]


def exact_product(left, right):
    return jnp.dot(left, right, precision=lax.Precision.HIGHEST, preferred_element_type=jnp.float32)


def energy_part(field, received, speed, back_speed, inverse):
    levels, radii, width = speed.shape
    return pl.pallas_call(
        functools.partial(energy_kernel, field),
        out_shape=[
            jax.ShapeDtypeStruct(speed.shape, jnp.float32),
            jax.ShapeDtypeStruct((2, levels, width), jnp.float32),
        ],
        in_specs=[IN_VMEM] * 4,
        out_specs=[IN_VMEM] * 2,
        compiler_params=ROOMY,
        cost_estimate=cost(60 * speed.size, 4 * speed.size),
    )(received, speed, back_speed, inverse)


def product_kernel(inverse_ref, moved_ref, local_ref):
    for level in range(moved_ref.shape[0]):
        local_ref[level] = exact_product(inverse_ref[level], moved_ref[level])


def product(inverse, moved):
    return pl.pallas_call(
        product_kernel,
        out_shape=jax.ShapeDtypeStruct(moved.shape, jnp.float32),
        in_specs=[IN_VMEM] * 2,
        out_specs=IN_VMEM,
        compiler_params=ROOMY,
        cost_estimate=cost(2 * moved.size * moved.shape[1], 2 * moved.size),
    )(inverse, moved)


def carry_kernel(recv_ref, speed_ref, back_ref, out_ref, held, sems):
    nf, levels = held.shape[:2]
    copies = []
    known = {}
    for level in range(levels):

        def store(field, row, cell, values, level=level):
            held[field, level, row : row + TILE_ROWS, cell : cell + LANES] = values

        carry_level(range(nf), level, recv_ref, speed_ref, back_ref, known, store)
        copies.append(
            pltpu.make_async_copy(held.at[:, level], out_ref.at[pl.ds(0, nf), level], sems.at[level])
        )
        copies[-1].start()
    for copy in copies:
        copy.wait()


def carry(nf, count, received, speed, back_speed):
    levels, radii, width = speed.shape
    return pl.pallas_call(
        carry_kernel,
        out_shape=jax.ShapeDtypeStruct((nf,) + speed.shape, jnp.float32),
        in_specs=[IN_VMEM] * 3,
        out_specs=IN_HBM,
        scratch_shapes=[
            pltpu.VMEM((count,) + speed.shape, jnp.float32),
            pltpu.SemaphoreType.DMA((levels,)),
        ],
        compiler_params=ROOMY,
        cost_estimate=cost(10 * count * speed.size, 2 * count * speed.size),
    )(received, speed, back_speed)


def solve_interfaces(first_row, last_row, corner):
    bands = len(first_row)
    crossings = bands - 1
    nothing = jnp.zeros_like(first_row[0])
    carry_base = nothing
    carry_slope = jnp.zeros_like(corner[0][0])
    records = []
    for crossing in range(crossings):
        link = corner[crossing][4]
        steepness = link * corner[crossing][3]
        offset = last_row[crossing]
        if crossing > 0:
            back_link = corner[crossing - 1][4] * corner[crossing][2]
            steepness = back_link * carry_slope + steepness
            offset = offset + back_link * carry_base
        fore_link = link * corner[crossing + 1][0]
        next_link = jnp.zeros_like(link)
        if crossing + 1 < crossings:
            next_link = corner[crossing + 1][4] * corner[crossing + 1][1]
        denominator = 1.0 - fore_link * steepness
        upper_base = (first_row[crossing + 1] + fore_link * offset) / denominator
        upper_slope = next_link / denominator
        carry_base = offset + steepness * upper_base
        carry_slope = steepness * upper_slope
        records.append((carry_base, carry_slope, upper_base, upper_slope))
    lower_values = [nothing] * crossings
    upper_values = [nothing] * crossings
    follow = nothing
    for crossing in reversed(range(crossings)):
        carry_base, carry_slope, upper_base, upper_slope = records[crossing]
        lower_values[crossing] = carry_base + carry_slope * follow
        upper_values[crossing] = upper_base + upper_slope * follow
        follow = upper_values[crossing]
    return [nothing] + lower_values, upper_values + [nothing]


def finish_kernel(band_ref, corner_ref, local_ref, low_ref, high_ref, *refs):
    end_refs, (_, out_ref, held, sems) = refs[:-4], refs[-4:]
    levels, _, width = local_ref.shape
    bands = corner_ref.shape[1] // 5
    band = band_ref[0]
    if len(end_refs) == 2:
        own, other = end_refs
        ends = [
            [jnp.where(band == j, own[side], other[side]) for j in range(bands)] for side in range(2)
        ]
    else:
        ends = [[end_refs[0][j, side] for j in range(bands)] for side in range(2)]
    corner = [[corner_ref[:, j * 5 + c : j * 5 + c + 1] for c in range(5)] for j in range(bands)]
    all_before, all_beyond = solve_interfaces(ends[0], ends[1], corner)
    before = beyond = jnp.zeros_like(ends[0][0])
    for j in range(bands):
        before = jnp.where(band == j, all_before[j], before)
        beyond = jnp.where(band == j, all_beyond[j], beyond)
    copies = []
    for level in range(levels):
        for cell in range(0, width, LANES):
            cut = slice(cell, cell + LANES)
            held[level, :, cut] = (
                local_ref[level, :, cut]
                + low_ref[level] * before[level : level + 1, cut]
                + high_ref[level] * beyond[level : level + 1, cut]
            )
        copies.append(
            pltpu.make_async_copy(held.at[level], out_ref.at[out_ref.shape[0] - 1, level], sems.at[level])
        )
        copies[-1].start()
    for copy in copies:
        copy.wait()


def finish(band, corners, local_part, low, high, ends, result):
    levels = local_part.shape[0]
    return pl.pallas_call(
        finish_kernel,
        out_shape=jax.ShapeDtypeStruct(result.shape, jnp.float32),
        in_specs=[IN_SMEM] + [IN_VMEM] * (4 + len(ends)) + [IN_HBM],
        out_specs=IN_HBM,
        scratch_shapes=[pltpu.VMEM(local_part.shape, jnp.float32), pltpu.SemaphoreType.DMA((levels,))],
        input_output_aliases={5 + len(ends): 0},
        compiler_params=ROOMY,
        cost_estimate=cost(4 * local_part.size, 2 * local_part.size),
    )(band, corners, local_part, low, high, *ends, result)


def exchange(blocks):
    n = blocks.shape[0]
    order = sorted(range(n), key=lambda device: place_of(device, n))
    return lax.all_to_all(blocks, "az", split_axis=0, concat_axis=0, tiled=True, axis_index_groups=[order])


def per_device(fields, velocity, shifts, block_inverse, coupling):
    n = lax.axis_size("az")
    bands = lax.axis_size("rad")
    nf, levels, radii, width = fields.shape
    rows = nf * levels * radii // n
    me = lax.axis_index("az")
    band = lax.axis_index("rad")

    gathered = exchange(fields.reshape(n, rows, width))

    all_shifts = jnp.tile(shifts, rows // radii + 2)
    own_shifts = lax.dynamic_slice_in_dim(all_shifts, (place_of(me, n) * rows) % radii, rows)
    shift_rows = jnp.broadcast_to(own_shifts[:, None], (rows, LANES))
    edge_speed = lax.ppermute(velocity[:, :, -1], "az", [(i, (i + 1) % n) for i in range(n)])
    back_speed = jnp.concatenate([edge_speed[:, :, None], velocity[:, :, :-1]], axis=2)
    corners = jnp.stack(
        [
            block_inverse[:, 0, 0],
            block_inverse[:, 0, -1],
            block_inverse[:, -1, 0],
            block_inverse[:, -1, -1],
            coupling[:, 0],
        ],
        axis=1,
    )
    all_corners = lax.all_gather(corners, "rad", axis=1, tiled=True)
    links = all_corners.reshape(levels, bands, 5)[:, :, 4]
    links_below = jnp.concatenate([jnp.zeros_like(links[:, :1]), links[:, :-1]], axis=1)
    link_below = lax.dynamic_index_in_dim(links_below, band, 1, keepdims=True)
    low, high = spread(
        (link_below * block_inverse[:, :, 0])[:, :, None], (coupling * block_inverse[:, :, -1])[:, :, None]
    )
    band_scalar = band[None].astype(jnp.int32)
    gathered, back_speed, all_corners, low, high, band_scalar, shift_rows = lax.optimization_barrier(
        (gathered, back_speed, all_corners, low, high, band_scalar, shift_rows)
    )

    received = exchange(turn(shift_rows, gathered))

    moved, ends = energy_part(nf - 1, received, velocity, back_speed, block_inverse)
    if bands == 2:
        all_ends = [ends, lax.ppermute(ends, "rad", [(0, 1), (1, 0)])]
    else:
        all_ends = [lax.all_gather(ends, "rad", axis=0)]
    local_part = product(block_inverse, moved)
    result = carry(nf, nf - 1, received, velocity, back_speed)
    return finish(band_scalar, all_corners, local_part, low, high, all_ends, result)


def solution(mesh):
    placed = (
        P(None, None, "rad", "az"),
        P(None, "rad", "az"),
        P("rad"),
        P(None, "rad", None),
        P(None, "rad"),
    )
    return jax.shard_map(
        per_device,
        mesh=mesh,
        in_specs=placed,
        out_specs=P(None, None, "rad", "az"),
        check_vma=False,
    )
```

```python
import functools

import jax
import jax.numpy as jnp
from jax import lax
from jax.experimental import pallas as pl
from jax.experimental.pallas import tpu as pltpu
from jax.sharding import PartitionSpec as P

LANES = 128
TILE_ROWS = 8
IN_VMEM = pl.BlockSpec(memory_space=pltpu.VMEM)
IN_HBM = pl.BlockSpec(memory_space=pltpu.HBM)
IN_SMEM = pl.BlockSpec(memory_space=pltpu.SMEM)
ROOMY = pltpu.CompilerParams(vmem_limit_bytes=24 * 1024 * 1024)


def cost(flops, moved):
    return pl.CostEstimate(flops=flops, bytes_accessed=4 * moved, transcendentals=0)


def place_of(device, n):
    return (device + n - n // 4) % n


def turn_kernel(shift_ref, in_ref, out_ref):
    n, rows, width = in_ref.shape
    places = [place_of(block, n) for block in range(n)]
    per_block = width // LANES
    tiles = n * per_block
    groups = rows // TILE_ROWS
    halo_row = per_block * rows
    lane = lax.broadcasted_iota(jnp.int32, (TILE_ROWS, LANES), 1)
    for block in range(n):
        out_ref[block, halo_row : halo_row + TILE_ROWS, :] = jnp.zeros((TILE_ROWS, LANES), jnp.float32)

    def one_group(group):
        here = pl.ds(group * TILE_ROWS, TILE_ROWS)
        shift = shift_ref[here, :]
        cells = shift & (LANES - 1)
        whole = shift >> 7
        source = (lane - cells) & (LANES - 1)
        own = lane >= cells
        turned = []
        for tile in range(tiles):
            block, part = divmod(tile, per_block)
            values = in_ref[places[block], here, part * LANES : (part + 1) * LANES]
            turned.append(jnp.take_along_axis(values, source, axis=1, mode="promise_in_bounds"))
        circle = [jnp.where(own, turned[tile], turned[tile - 1]) for tile in range(tiles)]
        step = 1
        while step < tiles:
            wanted = (whole & step) != 0
            circle = [jnp.where(wanted, circle[(tile - step) % tiles], circle[tile]) for tile in range(tiles)]
            step *= 2
        for tile in range(tiles):
            block, part = divmod(tile, per_block)
            row = (group * per_block + part) * TILE_ROWS
            out_ref[places[block], pl.ds(row, TILE_ROWS), :] = circle[tile]
        place = group * 2
        edge = (lane == place) | (lane == place + 1)
        for block in range(n):
            left = circle[(block * per_block - 1) % tiles]
            right = circle[((block + 1) * per_block) % tiles]
            both = pltpu.roll(jnp.where(lane == 0, right, left), place + 1, 1)
            target = out_ref.at[places[block], halo_row : halo_row + TILE_ROWS, :]
            target[...] = jnp.where(edge, both, target[...])

    for group in range(groups):
        one_group(group)


def turn(shift_rows, gathered):
    n, rows, width = gathered.shape
    shape = (n, (width // LANES) * rows + TILE_ROWS, LANES)
    return pl.pallas_call(
        turn_kernel,
        out_shape=jax.ShapeDtypeStruct(shape, jnp.float32),
        in_specs=[IN_VMEM] * 2,
        out_specs=IN_VMEM,
        compiler_params=ROOMY,
        cost_estimate=cost(10 * gathered.size, 2 * gathered.size),
    )(shift_rows, gathered)


def prepare_kernel(low_ref, high_ref, speed_ref, back_ref, low_out, high_out, weights_out):
    low_out[...] = jnp.broadcast_to(low_ref[...], low_out.shape)
    high_out[...] = jnp.broadcast_to(high_ref[...], high_out.shape)
    speed = speed_ref[...]
    back = back_ref[...]
    weights_out[0] = 1.0 - jnp.maximum(speed, 0.0) + jnp.minimum(back, 0.0)
    weights_out[1] = jnp.maximum(back, 0.0)
    weights_out[2] = -jnp.minimum(speed, 0.0)


def prepare(low, high, speed, back_speed):
    column = jax.ShapeDtypeStruct(low.shape[:-1] + (LANES,), jnp.float32)
    return pl.pallas_call(
        prepare_kernel,
        out_shape=[column, column, jax.ShapeDtypeStruct((3,) + speed.shape, jnp.float32)],
        in_specs=[IN_VMEM] * 4,
        out_specs=[IN_VMEM] * 3,
        compiler_params=ROOMY,
        cost_estimate=cost(6 * speed.size, 6 * speed.size),
    )(low, high, speed, back_speed)


def carry_level(fields, level, recv_ref, weights_ref, known, store):
    _, levels, radii, width = weights_ref.shape
    per_block = width // LANES
    in_rows = recv_ref.shape[1]
    halo_row = in_rows - TILE_ROWS
    groups = halo_row // (per_block * TILE_ROWS)
    lane = lax.broadcasted_iota(jnp.int32, (TILE_ROWS, LANES), 1)
    first = lane == 0
    last = lane == LANES - 1

    def edges(piece, group):
        key = (piece, group)
        if key not in known:
            known[key] = pltpu.roll(recv_ref[piece, halo_row:in_rows, :], (LANES - 2 * group) % LANES, 1)
        return known[key]

    for row in range(0, radii, TILE_ROWS):
        weights = [
            [
                weights_ref[side, level, row : row + TILE_ROWS, part * LANES : (part + 1) * LANES]
                for side in range(3)
            ]
            for part in range(per_block)
        ]
        for field in fields:
            piece, group = divmod(((field * levels + level) * radii + row) // TILE_ROWS, groups)
            values = []
            for part in range(per_block):
                at = (group * per_block + part) * TILE_ROWS
                values.append(recv_ref[piece, at : at + TILE_ROWS, :])
            up = [edges(piece, group)]
            up += [pltpu.roll(one, 1, 1) for one in values]
            down = [pltpu.roll(one, LANES - 1, 1) for one in values]
            down.append(edges(piece, group + 1))
            for part in range(per_block):
                here = values[part]
                behind = jnp.where(first, up[part], up[part + 1])
                ahead = jnp.where(last, down[part + 1], down[part])
                keep, from_behind, from_ahead = weights[part]
                result = keep * here + from_behind * behind + from_ahead * ahead
                store(field, row, part * LANES, result)


def energy_kernel(field, recv_ref, weights_ref, inverse_ref, moved_ref, ends_ref):
    levels, radii, _ = moved_ref.shape
    known = {}
    for level in range(levels):

        def store(_, row, cell, values, level=level):
            moved_ref[level, row : row + TILE_ROWS, cell : cell + LANES] = values

        carry_level([field], level, recv_ref, weights_ref, known, store)
        outer = jnp.concatenate([inverse_ref[level, :TILE_ROWS], inverse_ref[level, radii - TILE_ROWS :]])
        ends = exact_product(outer, moved_ref[level])
        ends_ref[0, level : level + 1, :] = ends[:1]
        ends_ref[1, level : level + 1, :] = ends[-1:]


def exact_product(left, right):
    return jnp.dot(left, right, precision=lax.Precision.HIGHEST, preferred_element_type=jnp.float32)


def energy_part(field, received, weights, inverse):
    _, levels, radii, width = weights.shape
    shape = (levels, radii, width)
    return pl.pallas_call(
        functools.partial(energy_kernel, field),
        out_shape=[
            jax.ShapeDtypeStruct(shape, jnp.float32),
            jax.ShapeDtypeStruct((2, levels, width), jnp.float32),
        ],
        in_specs=[IN_VMEM] * 3,
        out_specs=[IN_VMEM] * 2,
        compiler_params=ROOMY,
        cost_estimate=cost(20 * weights.size, 2 * weights.size),
    )(received, weights, inverse)


def product_kernel(inverse_ref, moved_ref, local_ref):
    for level in range(moved_ref.shape[0]):
        local_ref[level] = exact_product(inverse_ref[level], moved_ref[level])


def product(inverse, moved):
    return pl.pallas_call(
        product_kernel,
        out_shape=jax.ShapeDtypeStruct(moved.shape, jnp.float32),
        in_specs=[IN_VMEM] * 2,
        out_specs=IN_VMEM,
        compiler_params=ROOMY,
        cost_estimate=cost(2 * moved.size * moved.shape[1], 2 * moved.size),
    )(inverse, moved)


def carry_kernel(recv_ref, weights_ref, out_ref, held, sems):
    nf, levels = held.shape[:2]
    copies = []
    known = {}
    for level in range(levels):

        def store(field, row, cell, values, level=level):
            held[field, level, row : row + TILE_ROWS, cell : cell + LANES] = values

        carry_level(range(nf), level, recv_ref, weights_ref, known, store)
        copies.append(
            pltpu.make_async_copy(held.at[:, level], out_ref.at[pl.ds(0, nf), level], sems.at[level])
        )
        copies[-1].start()
    for copy in copies:
        copy.wait()


def carry(nf, count, received, weights):
    shape = weights.shape[1:]
    return pl.pallas_call(
        carry_kernel,
        out_shape=jax.ShapeDtypeStruct((nf,) + shape, jnp.float32),
        in_specs=[IN_VMEM] * 2,
        out_specs=IN_HBM,
        scratch_shapes=[
            pltpu.VMEM((count,) + shape, jnp.float32),
            pltpu.SemaphoreType.DMA((shape[0],)),
        ],
        compiler_params=ROOMY,
        cost_estimate=cost(2 * count * weights.size, count * weights.size),
    )(received, weights)


def solve_interfaces(first_row, last_row, corner):
    bands = len(first_row)
    crossings = bands - 1
    nothing = jnp.zeros_like(first_row[0])
    carry_base = nothing
    carry_slope = jnp.zeros_like(corner[0][0])
    records = []
    for crossing in range(crossings):
        link = corner[crossing][4]
        steepness = link * corner[crossing][3]
        offset = last_row[crossing]
        if crossing > 0:
            back_link = corner[crossing - 1][4] * corner[crossing][2]
            steepness = back_link * carry_slope + steepness
            offset = offset + back_link * carry_base
        fore_link = link * corner[crossing + 1][0]
        next_link = jnp.zeros_like(link)
        if crossing + 1 < crossings:
            next_link = corner[crossing + 1][4] * corner[crossing + 1][1]
        denominator = 1.0 - fore_link * steepness
        upper_base = (first_row[crossing + 1] + fore_link * offset) / denominator
        upper_slope = next_link / denominator
        carry_base = offset + steepness * upper_base
        carry_slope = steepness * upper_slope
        records.append((carry_base, carry_slope, upper_base, upper_slope))
    lower_values = [nothing] * crossings
    upper_values = [nothing] * crossings
    follow = nothing
    for crossing in reversed(range(crossings)):
        carry_base, carry_slope, upper_base, upper_slope = records[crossing]
        lower_values[crossing] = carry_base + carry_slope * follow
        upper_values[crossing] = upper_base + upper_slope * follow
        follow = upper_values[crossing]
    return [nothing] + lower_values, upper_values + [nothing]


def finish_kernel(band_ref, corner_ref, local_ref, low_ref, high_ref, *refs):
    end_refs, (_, out_ref, held, sems) = refs[:-4], refs[-4:]
    levels, _, width = local_ref.shape
    bands = corner_ref.shape[1] // 5
    band = band_ref[0]
    if len(end_refs) == 2:
        own, other = end_refs
        ends = [
            [jnp.where(band == j, own[side], other[side]) for j in range(bands)] for side in range(2)
        ]
    else:
        ends = [[end_refs[0][j, side] for j in range(bands)] for side in range(2)]
    corner = [[corner_ref[:, j * 5 + c : j * 5 + c + 1] for c in range(5)] for j in range(bands)]
    all_before, all_beyond = solve_interfaces(ends[0], ends[1], corner)
    before = beyond = jnp.zeros_like(ends[0][0])
    for j in range(bands):
        before = jnp.where(band == j, all_before[j], before)
        beyond = jnp.where(band == j, all_beyond[j], beyond)
    copies = []
    for level in range(levels):
        for cell in range(0, width, LANES):
            cut = slice(cell, cell + LANES)
            held[level, :, cut] = (
                local_ref[level, :, cut]
                + low_ref[level] * before[level : level + 1, cut]
                + high_ref[level] * beyond[level : level + 1, cut]
            )
        copies.append(
            pltpu.make_async_copy(held.at[level], out_ref.at[out_ref.shape[0] - 1, level], sems.at[level])
        )
        copies[-1].start()
    for copy in copies:
        copy.wait()


def finish(band, corners, local_part, low, high, ends, result):
    levels = local_part.shape[0]
    return pl.pallas_call(
        finish_kernel,
        out_shape=jax.ShapeDtypeStruct(result.shape, jnp.float32),
        in_specs=[IN_SMEM] + [IN_VMEM] * (4 + len(ends)) + [IN_HBM],
        out_specs=IN_HBM,
        scratch_shapes=[pltpu.VMEM(local_part.shape, jnp.float32), pltpu.SemaphoreType.DMA((levels,))],
        input_output_aliases={5 + len(ends): 0},
        compiler_params=ROOMY,
        cost_estimate=cost(4 * local_part.size, 2 * local_part.size),
    )(band, corners, local_part, low, high, *ends, result)


def exchange(blocks):
    n = blocks.shape[0]
    order = sorted(range(n), key=lambda device: place_of(device, n))
    return lax.all_to_all(blocks, "az", split_axis=0, concat_axis=0, tiled=True, axis_index_groups=[order])


def per_device(fields, velocity, shifts, block_inverse, coupling):
    n = lax.axis_size("az")
    bands = lax.axis_size("rad")
    nf, levels, radii, width = fields.shape
    rows = nf * levels * radii // n
    me = lax.axis_index("az")
    band = lax.axis_index("rad")

    gathered = exchange(fields.reshape(n, rows, width))

    all_shifts = jnp.tile(shifts, rows // radii + 2)
    own_shifts = lax.dynamic_slice_in_dim(all_shifts, (place_of(me, n) * rows) % radii, rows)
    shift_rows = jnp.broadcast_to(own_shifts[:, None], (rows, LANES))
    edge_speed = lax.ppermute(velocity[:, :, -1], "az", [(i, (i + 1) % n) for i in range(n)])
    back_speed = jnp.concatenate([edge_speed[:, :, None], velocity[:, :, :-1]], axis=2)
    corners = jnp.stack(
        [
            block_inverse[:, 0, 0],
            block_inverse[:, 0, -1],
            block_inverse[:, -1, 0],
            block_inverse[:, -1, -1],
            coupling[:, 0],
        ],
        axis=1,
    )
    all_corners = lax.all_gather(corners, "rad", axis=1, tiled=True)
    links = all_corners.reshape(levels, bands, 5)[:, :, 4]
    links_below = jnp.concatenate([jnp.zeros_like(links[:, :1]), links[:, :-1]], axis=1)
    link_below = lax.dynamic_index_in_dim(links_below, band, 1, keepdims=True)
    low, high, weights = prepare(
        (link_below * block_inverse[:, :, 0])[:, :, None],
        (coupling * block_inverse[:, :, -1])[:, :, None],
        velocity,
        back_speed,
    )
    band_scalar = band[None].astype(jnp.int32)
    gathered, weights, all_corners, low, high, band_scalar, shift_rows = lax.optimization_barrier(
        (gathered, weights, all_corners, low, high, band_scalar, shift_rows)
    )

    received = exchange(turn(shift_rows, gathered))

    moved, ends = energy_part(nf - 1, received, weights, block_inverse)
    if bands == 2:
        all_ends = [ends, lax.ppermute(ends, "rad", [(0, 1), (1, 0)])]
    else:
        all_ends = [lax.all_gather(ends, "rad", axis=0)]
    local_part = product(block_inverse, moved)
    result = carry(nf, nf - 1, received, weights)
    return finish(band_scalar, all_corners, local_part, low, high, all_ends, result)


def solution(mesh):
    placed = (
        P(None, None, "rad", "az"),
        P(None, "rad", "az"),
        P("rad"),
        P(None, "rad", None),
        P(None, "rad"),
    )
    return jax.shard_map(
        per_device,
        mesh=mesh,
        in_specs=placed,
        out_specs=P(None, None, "rad", "az"),
        check_vma=False,
    )
```

```python
import functools

import jax
import jax.numpy as jnp
from jax import lax
from jax.experimental import pallas as pl
from jax.experimental.pallas import tpu as pltpu
from jax.sharding import PartitionSpec as P

LANES = 128
TILE_ROWS = 8
IN_VMEM = pl.BlockSpec(memory_space=pltpu.VMEM)
IN_HBM = pl.BlockSpec(memory_space=pltpu.HBM)
IN_SMEM = pl.BlockSpec(memory_space=pltpu.SMEM)
ROOMY = pltpu.CompilerParams(vmem_limit_bytes=24 * 1024 * 1024)


def cost(flops, moved):
    return pl.CostEstimate(flops=flops, bytes_accessed=4 * moved, transcendentals=0)


def place_of(device, n):
    return (device + n - n // 4) % n


def turn_kernel(shift_ref, edge_ref, in_ref, out_ref):
    n, rows, width = in_ref.shape
    places = [place_of(block, n) for block in range(n)]
    per_block = width // LANES
    tiles = n * per_block
    groups = rows // TILE_ROWS
    halo_row = per_block * rows
    lane = lax.broadcasted_iota(jnp.int32, (TILE_ROWS, LANES), 1)
    for block in range(n):
        out_ref[block, halo_row : halo_row + TILE_ROWS, :] = edge_ref[...]

    def one_group(group):
        here = pl.ds(group * TILE_ROWS, TILE_ROWS)
        shift = shift_ref[here, :]
        cells = shift & (LANES - 1)
        whole = shift >> 7
        source = (lane - cells) & (LANES - 1)
        own = lane >= cells
        turned = []
        for tile in range(tiles):
            block, part = divmod(tile, per_block)
            values = in_ref[places[block], here, part * LANES : (part + 1) * LANES]
            turned.append(jnp.take_along_axis(values, source, axis=1, mode="promise_in_bounds"))
        circle = [jnp.where(own, turned[tile], turned[tile - 1]) for tile in range(tiles)]
        step = 1
        while step < tiles:
            wanted = (whole & step) != 0
            circle = [jnp.where(wanted, circle[(tile - step) % tiles], circle[tile]) for tile in range(tiles)]
            step *= 2
        for tile in range(tiles):
            block, part = divmod(tile, per_block)
            row = (group * per_block + part) * TILE_ROWS
            out_ref[places[block], pl.ds(row, TILE_ROWS), :] = circle[tile]
        place = group * 2
        edge = (lane == place) | (lane == place + 1)
        for block in range(n):
            left = circle[(block * per_block - 1) % tiles]
            right = circle[((block + 1) * per_block) % tiles]
            both = pltpu.roll(jnp.where(lane == 0, right, left), place + 1, 1)
            target = out_ref.at[places[block], halo_row : halo_row + TILE_ROWS, :]
            target[...] = jnp.where(edge, both, target[...])

    for group in range(groups):
        one_group(group)


def turn(shift_rows, edge_tile, gathered):
    n, rows, width = gathered.shape
    shape = (n, (width // LANES) * rows + TILE_ROWS, LANES)
    return pl.pallas_call(
        turn_kernel,
        out_shape=jax.ShapeDtypeStruct(shape, jnp.float32),
        in_specs=[IN_VMEM] * 3,
        out_specs=IN_VMEM,
        compiler_params=ROOMY,
        cost_estimate=cost(10 * gathered.size, 2 * gathered.size),
    )(shift_rows, edge_tile, gathered)


def spread_kernel(low_ref, high_ref, low_out, high_out):
    low_out[...] = jnp.broadcast_to(low_ref[...], low_out.shape)
    high_out[...] = jnp.broadcast_to(high_ref[...], high_out.shape)


def spread(low, high):
    shape = low.shape[:-1] + (LANES,)
    return pl.pallas_call(
        spread_kernel,
        out_shape=[jax.ShapeDtypeStruct(shape, jnp.float32)] * 2,
        in_specs=[IN_VMEM] * 2,
        out_specs=[IN_VMEM] * 2,
        compiler_params=ROOMY,
        cost_estimate=cost(low.size, 2 * low.size * LANES),
    )(low, high)


def carry_level(fields, level, recv_ref, speed_ref, back_ref, known, store):
    levels, radii, width = speed_ref.shape
    per_block = width // LANES
    in_rows = recv_ref.shape[1]
    halo_row = in_rows - TILE_ROWS
    groups = halo_row // (per_block * TILE_ROWS)
    lane = lax.broadcasted_iota(jnp.int32, (TILE_ROWS, LANES), 1)
    first = lane == 0
    last = lane == LANES - 1

    def edges(piece, group):
        key = (piece, group)
        if key not in known:
            known[key] = pltpu.roll(recv_ref[piece, halo_row:in_rows, :], (LANES - 2 * group) % LANES, 1)
        return known[key]

    for row in range(0, radii, TILE_ROWS):
        rates = []
        for part in range(per_block):
            cut = (level, slice(row, row + TILE_ROWS), slice(part * LANES, (part + 1) * LANES))
            speed = speed_ref[cut]
            back = back_ref[cut]
            rates.append(
                (
                    jnp.maximum(speed, 0.0),
                    jnp.minimum(speed, 0.0),
                    jnp.maximum(back, 0.0),
                    jnp.minimum(back, 0.0),
                )
            )
        for field in fields:
            piece, group = divmod(((field * levels + level) * radii + row) // TILE_ROWS, groups)
            values = []
            for part in range(per_block):
                at = (group * per_block + part) * TILE_ROWS
                values.append(recv_ref[piece, at : at + TILE_ROWS, :])
            up = [edges(piece, group)]
            up += [pltpu.roll(one, 1, 1) for one in values]
            down = [pltpu.roll(one, LANES - 1, 1) for one in values]
            down.append(edges(piece, group + 1))
            for part in range(per_block):
                here = values[part]
                behind = jnp.where(first, up[part], up[part + 1])
                ahead = jnp.where(last, down[part + 1], down[part])
                plus, minus, back_plus, back_minus = rates[part]
                outflow = plus * here + minus * ahead
                inflow = back_plus * behind + back_minus * here
                store(field, row, part * LANES, here - (outflow - inflow))


def energy_kernel(
    field, left_ref, recv_ref, speed_ref, inverse_ref, moved_ref, ends_ref, back_ref, columns
):
    levels, radii, width = speed_ref.shape
    in_rows = recv_ref.shape[1]
    tile = recv_ref[left_ref[0], in_rows - TILE_ROWS :, :]
    columns[...] = jnp.transpose(jnp.concatenate([tile] * (LANES // TILE_ROWS), axis=0))
    first = lax.broadcasted_iota(jnp.int32, (TILE_ROWS, LANES), 1) == 0
    known = {}
    for level in range(levels):
        for row in range(0, radii, TILE_ROWS):
            here = slice(row, row + TILE_ROWS)
            column = columns[LANES - radii + row : LANES - radii + row + TILE_ROWS, level : level + 1]
            before = jnp.broadcast_to(column, (TILE_ROWS, LANES))
            for cell in range(0, width, LANES):
                behind = pltpu.roll(speed_ref[level, here, cell : cell + LANES], 1, 1)
                back_ref[level, here, cell : cell + LANES] = jnp.where(first, before, behind)
                before = behind

        def store(_, row, cell, values, level=level):
            moved_ref[level, row : row + TILE_ROWS, cell : cell + LANES] = values

        carry_level([field], level, recv_ref, speed_ref, back_ref, known, store)
        outer = jnp.concatenate([inverse_ref[level, :TILE_ROWS], inverse_ref[level, radii - TILE_ROWS :]])
        ends = exact_product(outer, moved_ref[level])
        ends_ref[0, level : level + 1, :] = ends[:1]
        ends_ref[1, level : level + 1, :] = ends[-1:]


def exact_product(left, right):
    return jnp.dot(left, right, precision=lax.Precision.HIGHEST, preferred_element_type=jnp.float32)


def energy_part(field, left, received, speed, inverse):
    levels, radii, width = speed.shape
    plane = jax.ShapeDtypeStruct(speed.shape, jnp.float32)
    return pl.pallas_call(
        functools.partial(energy_kernel, field),
        out_shape=[plane, jax.ShapeDtypeStruct((2, levels, width), jnp.float32), plane],
        in_specs=[IN_SMEM] + [IN_VMEM] * 3,
        out_specs=[IN_VMEM] * 3,
        scratch_shapes=[pltpu.VMEM((LANES, LANES), jnp.float32)],
        compiler_params=ROOMY,
        cost_estimate=cost(60 * speed.size, 5 * speed.size),
    )(left, received, speed, inverse)


def product_kernel(inverse_ref, moved_ref, local_ref):
    for level in range(moved_ref.shape[0]):
        local_ref[level] = exact_product(inverse_ref[level], moved_ref[level])


def product(inverse, moved):
    return pl.pallas_call(
        product_kernel,
        out_shape=jax.ShapeDtypeStruct(moved.shape, jnp.float32),
        in_specs=[IN_VMEM] * 2,
        out_specs=IN_VMEM,
        compiler_params=ROOMY,
        cost_estimate=cost(2 * moved.size * moved.shape[1], 2 * moved.size),
    )(inverse, moved)


def carry_kernel(recv_ref, speed_ref, back_ref, out_ref, held, sems):
    nf, levels = held.shape[:2]
    copies = []
    known = {}
    for level in range(levels):

        def store(field, row, cell, values, level=level):
            held[field, level, row : row + TILE_ROWS, cell : cell + LANES] = values

        carry_level(range(nf), level, recv_ref, speed_ref, back_ref, known, store)
        copies.append(
            pltpu.make_async_copy(held.at[:, level], out_ref.at[pl.ds(0, nf), level], sems.at[level])
        )
        copies[-1].start()
    for copy in copies:
        copy.wait()


def carry(nf, count, received, speed, back_speed):
    levels, radii, width = speed.shape
    return pl.pallas_call(
        carry_kernel,
        out_shape=jax.ShapeDtypeStruct((nf,) + speed.shape, jnp.float32),
        in_specs=[IN_VMEM] * 3,
        out_specs=IN_HBM,
        scratch_shapes=[
            pltpu.VMEM((count,) + speed.shape, jnp.float32),
            pltpu.SemaphoreType.DMA((levels,)),
        ],
        compiler_params=ROOMY,
        cost_estimate=cost(10 * count * speed.size, 2 * count * speed.size),
    )(received, speed, back_speed)


def solve_interfaces(first_row, last_row, corner):
    bands = len(first_row)
    crossings = bands - 1
    nothing = jnp.zeros_like(first_row[0])
    carry_base = nothing
    carry_slope = jnp.zeros_like(corner[0][0])
    records = []
    for crossing in range(crossings):
        link = corner[crossing][4]
        steepness = link * corner[crossing][3]
        offset = last_row[crossing]
        if crossing > 0:
            back_link = corner[crossing - 1][4] * corner[crossing][2]
            steepness = back_link * carry_slope + steepness
            offset = offset + back_link * carry_base
        fore_link = link * corner[crossing + 1][0]
        next_link = jnp.zeros_like(link)
        if crossing + 1 < crossings:
            next_link = corner[crossing + 1][4] * corner[crossing + 1][1]
        denominator = 1.0 - fore_link * steepness
        upper_base = (first_row[crossing + 1] + fore_link * offset) / denominator
        upper_slope = next_link / denominator
        carry_base = offset + steepness * upper_base
        carry_slope = steepness * upper_slope
        records.append((carry_base, carry_slope, upper_base, upper_slope))
    lower_values = [nothing] * crossings
    upper_values = [nothing] * crossings
    follow = nothing
    for crossing in reversed(range(crossings)):
        carry_base, carry_slope, upper_base, upper_slope = records[crossing]
        lower_values[crossing] = carry_base + carry_slope * follow
        upper_values[crossing] = upper_base + upper_slope * follow
        follow = upper_values[crossing]
    return [nothing] + lower_values, upper_values + [nothing]


def finish_kernel(band_ref, corner_ref, local_ref, low_ref, high_ref, *refs):
    end_refs, (_, out_ref, held, sems) = refs[:-4], refs[-4:]
    levels, _, width = local_ref.shape
    bands = corner_ref.shape[1] // 5
    band = band_ref[0]
    if len(end_refs) == 2:
        own, other = end_refs
        ends = [
            [jnp.where(band == j, own[side], other[side]) for j in range(bands)] for side in range(2)
        ]
    else:
        ends = [[end_refs[0][j, side] for j in range(bands)] for side in range(2)]
    corner = [[corner_ref[:, j * 5 + c : j * 5 + c + 1] for c in range(5)] for j in range(bands)]
    all_before, all_beyond = solve_interfaces(ends[0], ends[1], corner)
    before = beyond = jnp.zeros_like(ends[0][0])
    for j in range(bands):
        before = jnp.where(band == j, all_before[j], before)
        beyond = jnp.where(band == j, all_beyond[j], beyond)
    copies = []
    for level in range(levels):
        for cell in range(0, width, LANES):
            cut = slice(cell, cell + LANES)
            held[level, :, cut] = (
                local_ref[level, :, cut]
                + low_ref[level] * before[level : level + 1, cut]
                + high_ref[level] * beyond[level : level + 1, cut]
            )
        copies.append(
            pltpu.make_async_copy(held.at[level], out_ref.at[out_ref.shape[0] - 1, level], sems.at[level])
        )
        copies[-1].start()
    for copy in copies:
        copy.wait()


def finish(band, corners, local_part, low, high, ends, result):
    levels = local_part.shape[0]
    return pl.pallas_call(
        finish_kernel,
        out_shape=jax.ShapeDtypeStruct(result.shape, jnp.float32),
        in_specs=[IN_SMEM] + [IN_VMEM] * (4 + len(ends)) + [IN_HBM],
        out_specs=IN_HBM,
        scratch_shapes=[pltpu.VMEM(local_part.shape, jnp.float32), pltpu.SemaphoreType.DMA((levels,))],
        input_output_aliases={5 + len(ends): 0},
        compiler_params=ROOMY,
        cost_estimate=cost(4 * local_part.size, 2 * local_part.size),
    )(band, corners, local_part, low, high, *ends, result)


def exchange(blocks):
    n = blocks.shape[0]
    order = sorted(range(n), key=lambda device: place_of(device, n))
    return lax.all_to_all(blocks, "az", split_axis=0, concat_axis=0, tiled=True, axis_index_groups=[order])


def per_device(fields, velocity, shifts, block_inverse, coupling):
    n = lax.axis_size("az")
    bands = lax.axis_size("rad")
    nf, levels, radii, width = fields.shape
    rows = nf * levels * radii // n
    me = lax.axis_index("az")
    band = lax.axis_index("rad")

    gathered = exchange(fields.reshape(n, rows, width))

    all_shifts = jnp.tile(shifts, rows // radii + 2)
    own_shifts = lax.dynamic_slice_in_dim(all_shifts, (place_of(me, n) * rows) % radii, rows)
    shift_rows = jnp.broadcast_to(own_shifts[:, None], (rows, LANES))
    edge_tile = jnp.pad(velocity[:, :, -1], ((0, 0), (LANES - radii, 0)))
    left_scalar = place_of((me + n - 1) % n, n)[None].astype(jnp.int32)
    corners = jnp.stack(
        [
            block_inverse[:, 0, 0],
            block_inverse[:, 0, -1],
            block_inverse[:, -1, 0],
            block_inverse[:, -1, -1],
            coupling[:, 0],
        ],
        axis=1,
    )
    all_corners = lax.all_gather(corners, "rad", axis=1, tiled=True)
    links = all_corners.reshape(levels, bands, 5)[:, :, 4]
    links_below = jnp.concatenate([jnp.zeros_like(links[:, :1]), links[:, :-1]], axis=1)
    link_below = lax.dynamic_index_in_dim(links_below, band, 1, keepdims=True)
    low, high = spread(
        (link_below * block_inverse[:, :, 0])[:, :, None], (coupling * block_inverse[:, :, -1])[:, :, None]
    )
    band_scalar = band[None].astype(jnp.int32)
    gathered, edge_tile, all_corners, low, high, band_scalar, left_scalar, shift_rows = lax.optimization_barrier(
        (gathered, edge_tile, all_corners, low, high, band_scalar, left_scalar, shift_rows)
    )

    received = exchange(turn(shift_rows, edge_tile, gathered))

    moved, ends, back_speed = energy_part(nf - 1, left_scalar, received, velocity, block_inverse)
    if bands == 2:
        all_ends = [ends, lax.ppermute(ends, "rad", [(0, 1), (1, 0)])]
    else:
        all_ends = [lax.all_gather(ends, "rad", axis=0)]
    local_part = product(block_inverse, moved)
    result = carry(nf, nf - 1, received, velocity, back_speed)
    return finish(band_scalar, all_corners, local_part, low, high, all_ends, result)


def solution(mesh):
    placed = (
        P(None, None, "rad", "az"),
        P(None, "rad", "az"),
        P("rad"),
        P(None, "rad", None),
        P(None, "rad"),
    )
    return jax.shard_map(
        per_device,
        mesh=mesh,
        in_specs=placed,
        out_specs=P(None, None, "rad", "az"),
        check_vma=False,
    )
```

```python
import functools

import jax
import jax.numpy as jnp
from jax import lax
from jax.experimental import pallas as pl
from jax.experimental.pallas import tpu as pltpu
from jax.sharding import PartitionSpec as P

LANES = 128
TILE_ROWS = 8
IN_VMEM = pl.BlockSpec(memory_space=pltpu.VMEM)
IN_HBM = pl.BlockSpec(memory_space=pltpu.HBM)
IN_SMEM = pl.BlockSpec(memory_space=pltpu.SMEM)
ROOMY = pltpu.CompilerParams(vmem_limit_bytes=24 * 1024 * 1024)


def cost(flops, moved):
    return pl.CostEstimate(flops=flops, bytes_accessed=4 * moved, transcendentals=0)


def place_of(device, n):
    return (device + n // 2) % n


def turn_kernel(shift_ref, edge_ref, in_ref, out_ref):
    n, rows, width = in_ref.shape
    places = [place_of(block, n) for block in range(n)]
    per_block = width // LANES
    tiles = n * per_block
    groups = rows // TILE_ROWS
    halo_row = per_block * rows
    lane = lax.broadcasted_iota(jnp.int32, (TILE_ROWS, LANES), 1)
    for block in range(n):
        out_ref[block, halo_row : halo_row + TILE_ROWS, :] = edge_ref[...]

    def one_group(group):
        here = pl.ds(group * TILE_ROWS, TILE_ROWS)
        shift = shift_ref[here, :]
        cells = shift & (LANES - 1)
        whole = shift >> 7
        source = (lane - cells) & (LANES - 1)
        own = lane >= cells
        turned = []
        for tile in range(tiles):
            block, part = divmod(tile, per_block)
            values = in_ref[places[block], here, part * LANES : (part + 1) * LANES]
            turned.append(jnp.take_along_axis(values, source, axis=1, mode="promise_in_bounds"))
        circle = [jnp.where(own, turned[tile], turned[tile - 1]) for tile in range(tiles)]
        step = 1
        while step < tiles:
            wanted = (whole & step) != 0
            circle = [jnp.where(wanted, circle[(tile - step) % tiles], circle[tile]) for tile in range(tiles)]
            step *= 2
        for tile in range(tiles):
            block, part = divmod(tile, per_block)
            row = (group * per_block + part) * TILE_ROWS
            out_ref[places[block], pl.ds(row, TILE_ROWS), :] = circle[tile]
        place = group * 2
        edge = (lane == place) | (lane == place + 1)
        for block in range(n):
            left = circle[(block * per_block - 1) % tiles]
            right = circle[((block + 1) * per_block) % tiles]
            both = pltpu.roll(jnp.where(lane == 0, right, left), place + 1, 1)
            target = out_ref.at[places[block], halo_row : halo_row + TILE_ROWS, :]
            target[...] = jnp.where(edge, both, target[...])

    for group in range(groups):
        one_group(group)


def turn(shift_rows, edge_tile, gathered):
    n, rows, width = gathered.shape
    shape = (n, (width // LANES) * rows + TILE_ROWS, LANES)
    return pl.pallas_call(
        turn_kernel,
        out_shape=jax.ShapeDtypeStruct(shape, jnp.float32),
        in_specs=[IN_VMEM] * 3,
        out_specs=IN_VMEM,
        compiler_params=ROOMY,
        cost_estimate=cost(10 * gathered.size, 2 * gathered.size),
    )(shift_rows, edge_tile, gathered)


def spread_kernel(low_ref, high_ref, low_out, high_out):
    low_out[...] = jnp.broadcast_to(low_ref[...], low_out.shape)
    high_out[...] = jnp.broadcast_to(high_ref[...], high_out.shape)


def spread(low, high):
    shape = low.shape[:-1] + (LANES,)
    return pl.pallas_call(
        spread_kernel,
        out_shape=[jax.ShapeDtypeStruct(shape, jnp.float32)] * 2,
        in_specs=[IN_VMEM] * 2,
        out_specs=[IN_VMEM] * 2,
        compiler_params=ROOMY,
        cost_estimate=cost(low.size, 2 * low.size * LANES),
    )(low, high)


def carry_level(fields, level, recv_ref, speed_ref, back_ref, known, store):
    levels, radii, width = speed_ref.shape
    per_block = width // LANES
    in_rows = recv_ref.shape[1]
    halo_row = in_rows - TILE_ROWS
    groups = halo_row // (per_block * TILE_ROWS)
    lane = lax.broadcasted_iota(jnp.int32, (TILE_ROWS, LANES), 1)
    first = lane == 0
    last = lane == LANES - 1

    def edges(piece, group):
        key = (piece, group)
        if key not in known:
            known[key] = pltpu.roll(recv_ref[piece, halo_row:in_rows, :], (LANES - 2 * group) % LANES, 1)
        return known[key]

    for row in range(0, radii, TILE_ROWS):
        rates = []
        for part in range(per_block):
            cut = (level, slice(row, row + TILE_ROWS), slice(part * LANES, (part + 1) * LANES))
            speed = speed_ref[cut]
            back = back_ref[cut]
            rates.append(
                (
                    jnp.maximum(speed, 0.0),
                    jnp.minimum(speed, 0.0),
                    jnp.maximum(back, 0.0),
                    jnp.minimum(back, 0.0),
                )
            )
        for field in fields:
            piece, group = divmod(((field * levels + level) * radii + row) // TILE_ROWS, groups)
            values = []
            for part in range(per_block):
                at = (group * per_block + part) * TILE_ROWS
                values.append(recv_ref[piece, at : at + TILE_ROWS, :])
            up = [edges(piece, group)]
            up += [pltpu.roll(one, 1, 1) for one in values]
            down = [pltpu.roll(one, LANES - 1, 1) for one in values]
            down.append(edges(piece, group + 1))
            for part in range(per_block):
                here = values[part]
                behind = jnp.where(first, up[part], up[part + 1])
                ahead = jnp.where(last, down[part + 1], down[part])
                plus, minus, back_plus, back_minus = rates[part]
                outflow = plus * here + minus * ahead
                inflow = back_plus * behind + back_minus * here
                store(field, row, part * LANES, here - (outflow - inflow))


def energy_kernel(
    field, left_ref, recv_ref, speed_ref, inverse_ref, moved_ref, ends_ref, back_ref, columns
):
    levels, radii, width = speed_ref.shape
    in_rows = recv_ref.shape[1]
    tile = recv_ref[left_ref[0], in_rows - TILE_ROWS :, :]
    columns[...] = jnp.transpose(jnp.concatenate([tile] * (LANES // TILE_ROWS), axis=0))
    first = lax.broadcasted_iota(jnp.int32, (TILE_ROWS, LANES), 1) == 0
    known = {}
    for level in range(levels):
        for row in range(0, radii, TILE_ROWS):
            here = slice(row, row + TILE_ROWS)
            column = columns[LANES - radii + row : LANES - radii + row + TILE_ROWS, level : level + 1]
            before = jnp.broadcast_to(column, (TILE_ROWS, LANES))
            for cell in range(0, width, LANES):
                behind = pltpu.roll(speed_ref[level, here, cell : cell + LANES], 1, 1)
                back_ref[level, here, cell : cell + LANES] = jnp.where(first, before, behind)
                before = behind

        def store(_, row, cell, values, level=level):
            moved_ref[level, row : row + TILE_ROWS, cell : cell + LANES] = values

        carry_level([field], level, recv_ref, speed_ref, back_ref, known, store)
        outer = jnp.concatenate([inverse_ref[level, :TILE_ROWS], inverse_ref[level, radii - TILE_ROWS :]])
        ends = exact_product(outer, moved_ref[level])
        ends_ref[0, level : level + 1, :] = ends[:1]
        ends_ref[1, level : level + 1, :] = ends[-1:]


def exact_product(left, right):
    return jnp.dot(left, right, precision=lax.Precision.HIGHEST, preferred_element_type=jnp.float32)


def energy_part(field, left, received, speed, inverse):
    levels, radii, width = speed.shape
    plane = jax.ShapeDtypeStruct(speed.shape, jnp.float32)
    return pl.pallas_call(
        functools.partial(energy_kernel, field),
        out_shape=[plane, jax.ShapeDtypeStruct((2, levels, width), jnp.float32), plane],
        in_specs=[IN_SMEM] + [IN_VMEM] * 3,
        out_specs=[IN_VMEM] * 3,
        scratch_shapes=[pltpu.VMEM((LANES, LANES), jnp.float32)],
        compiler_params=ROOMY,
        cost_estimate=cost(60 * speed.size, 5 * speed.size),
    )(left, received, speed, inverse)


def carry_kernel(recv_ref, speed_ref, back_ref, inverse_ref, moved_ref, out_ref, local_ref, held, sems):
    nf, levels = held.shape[:2]
    copies = []
    known = {}
    for level in range(levels):
        local_ref[level] = exact_product(inverse_ref[level], moved_ref[level])

        def store(field, row, cell, values, level=level):
            held[field, level, row : row + TILE_ROWS, cell : cell + LANES] = values

        carry_level(range(nf), level, recv_ref, speed_ref, back_ref, known, store)
        copies.append(
            pltpu.make_async_copy(held.at[:, level], out_ref.at[pl.ds(0, nf), level], sems.at[level])
        )
        copies[-1].start()
    for copy in copies:
        copy.wait()


def carry(nf, count, received, speed, back_speed, inverse, moved):
    levels, radii, width = speed.shape
    return pl.pallas_call(
        carry_kernel,
        out_shape=[
            jax.ShapeDtypeStruct((nf,) + speed.shape, jnp.float32),
            jax.ShapeDtypeStruct(speed.shape, jnp.float32),
        ],
        in_specs=[IN_VMEM] * 5,
        out_specs=[IN_HBM, IN_VMEM],
        scratch_shapes=[
            pltpu.VMEM((count,) + speed.shape, jnp.float32),
            pltpu.SemaphoreType.DMA((levels,)),
        ],
        compiler_params=ROOMY,
        cost_estimate=cost(10 * count * speed.size, 2 * count * speed.size),
    )(received, speed, back_speed, inverse, moved)


def solve_interfaces(first_row, last_row, corner):
    bands = len(first_row)
    crossings = bands - 1
    nothing = jnp.zeros_like(first_row[0])
    carry_base = nothing
    carry_slope = jnp.zeros_like(corner[0][0])
    records = []
    for crossing in range(crossings):
        link = corner[crossing][4]
        steepness = link * corner[crossing][3]
        offset = last_row[crossing]
        if crossing > 0:
            back_link = corner[crossing - 1][4] * corner[crossing][2]
            steepness = back_link * carry_slope + steepness
            offset = offset + back_link * carry_base
        fore_link = link * corner[crossing + 1][0]
        next_link = jnp.zeros_like(link)
        if crossing + 1 < crossings:
            next_link = corner[crossing + 1][4] * corner[crossing + 1][1]
        denominator = 1.0 - fore_link * steepness
        upper_base = (first_row[crossing + 1] + fore_link * offset) / denominator
        upper_slope = next_link / denominator
        carry_base = offset + steepness * upper_base
        carry_slope = steepness * upper_slope
        records.append((carry_base, carry_slope, upper_base, upper_slope))
    lower_values = [nothing] * crossings
    upper_values = [nothing] * crossings
    follow = nothing
    for crossing in reversed(range(crossings)):
        carry_base, carry_slope, upper_base, upper_slope = records[crossing]
        lower_values[crossing] = carry_base + carry_slope * follow
        upper_values[crossing] = upper_base + upper_slope * follow
        follow = upper_values[crossing]
    return [nothing] + lower_values, upper_values + [nothing]


def finish_kernel(band_ref, corner_ref, local_ref, low_ref, high_ref, *refs):
    end_refs, (_, out_ref, held, sems) = refs[:-4], refs[-4:]
    levels, _, width = local_ref.shape
    bands = corner_ref.shape[1] // 5
    band = band_ref[0]
    if len(end_refs) == 2:
        own, other = end_refs
        ends = [
            [jnp.where(band == j, own[side], other[side]) for j in range(bands)] for side in range(2)
        ]
    else:
        ends = [[end_refs[0][j, side] for j in range(bands)] for side in range(2)]
    corner = [[corner_ref[:, j * 5 + c : j * 5 + c + 1] for c in range(5)] for j in range(bands)]
    all_before, all_beyond = solve_interfaces(ends[0], ends[1], corner)
    before = beyond = jnp.zeros_like(ends[0][0])
    for j in range(bands):
        before = jnp.where(band == j, all_before[j], before)
        beyond = jnp.where(band == j, all_beyond[j], beyond)
    copies = []
    for level in range(levels):
        for cell in range(0, width, LANES):
            cut = slice(cell, cell + LANES)
            held[level, :, cut] = (
                local_ref[level, :, cut]
                + low_ref[level] * before[level : level + 1, cut]
                + high_ref[level] * beyond[level : level + 1, cut]
            )
        copies.append(
            pltpu.make_async_copy(held.at[level], out_ref.at[out_ref.shape[0] - 1, level], sems.at[level])
        )
        copies[-1].start()
    for copy in copies:
        copy.wait()


def finish(band, corners, local_part, low, high, ends, result):
    levels = local_part.shape[0]
    return pl.pallas_call(
        finish_kernel,
        out_shape=jax.ShapeDtypeStruct(result.shape, jnp.float32),
        in_specs=[IN_SMEM] + [IN_VMEM] * (4 + len(ends)) + [IN_HBM],
        out_specs=IN_HBM,
        scratch_shapes=[pltpu.VMEM(local_part.shape, jnp.float32), pltpu.SemaphoreType.DMA((levels,))],
        input_output_aliases={5 + len(ends): 0},
        compiler_params=ROOMY,
        cost_estimate=cost(4 * local_part.size, 2 * local_part.size),
    )(band, corners, local_part, low, high, *ends, result)


def exchange(blocks):
    n = blocks.shape[0]
    order = sorted(range(n), key=lambda device: place_of(device, n))
    return lax.all_to_all(blocks, "az", split_axis=0, concat_axis=0, tiled=True, axis_index_groups=[order])


def per_device(fields, velocity, shifts, block_inverse, coupling):
    n = lax.axis_size("az")
    bands = lax.axis_size("rad")
    nf, levels, radii, width = fields.shape
    rows = nf * levels * radii // n
    me = lax.axis_index("az")
    band = lax.axis_index("rad")

    gathered = exchange(fields.reshape(n, rows, width))

    all_shifts = jnp.tile(shifts, rows // radii + 2)
    own_shifts = lax.dynamic_slice_in_dim(all_shifts, (place_of(me, n) * rows) % radii, rows)
    shift_rows = jnp.broadcast_to(own_shifts[:, None], (rows, LANES))
    edge_tile = jnp.pad(velocity[:, :, -1], ((0, 0), (LANES - radii, 0)))
    left_scalar = place_of((me + n - 1) % n, n)[None].astype(jnp.int32)
    corners = jnp.stack(
        [
            block_inverse[:, 0, 0],
            block_inverse[:, 0, -1],
            block_inverse[:, -1, 0],
            block_inverse[:, -1, -1],
            coupling[:, 0],
        ],
        axis=1,
    )
    all_corners = lax.all_gather(corners, "rad", axis=1, tiled=True)
    links = all_corners.reshape(levels, bands, 5)[:, :, 4]
    links_below = jnp.concatenate([jnp.zeros_like(links[:, :1]), links[:, :-1]], axis=1)
    link_below = lax.dynamic_index_in_dim(links_below, band, 1, keepdims=True)
    low, high = spread(
        (link_below * block_inverse[:, :, 0])[:, :, None], (coupling * block_inverse[:, :, -1])[:, :, None]
    )
    band_scalar = band[None].astype(jnp.int32)
    gathered, edge_tile, all_corners, low, high, band_scalar, left_scalar, shift_rows = lax.optimization_barrier(
        (gathered, edge_tile, all_corners, low, high, band_scalar, left_scalar, shift_rows)
    )

    received = exchange(turn(shift_rows, edge_tile, gathered))

    moved, ends, back_speed = energy_part(nf - 1, left_scalar, received, velocity, block_inverse)
    if bands == 2:
        all_ends = [ends, lax.ppermute(ends, "rad", [(0, 1), (1, 0)])]
    else:
        all_ends = [lax.all_gather(ends, "rad", axis=0)]
    result, local_part = carry(nf, nf - 1, received, velocity, back_speed, block_inverse, moved)
    return finish(band_scalar, all_corners, local_part, low, high, all_ends, result)


def solution(mesh):
    placed = (
        P(None, None, "rad", "az"),
        P(None, "rad", "az"),
        P("rad"),
        P(None, "rad", None),
        P(None, "rad"),
    )
    return jax.shard_map(
        per_device,
        mesh=mesh,
        in_specs=placed,
        out_specs=P(None, None, "rad", "az"),
        check_vma=False,
    )
```

```python
import functools

import jax
import jax.numpy as jnp
from jax import lax
from jax.experimental import pallas as pl
from jax.experimental.pallas import tpu as pltpu
from jax.sharding import PartitionSpec as P

LANES = 128
TILE_ROWS = 8
IN_VMEM = pl.BlockSpec(memory_space=pltpu.VMEM)
IN_HBM = pl.BlockSpec(memory_space=pltpu.HBM)
IN_SMEM = pl.BlockSpec(memory_space=pltpu.SMEM)
ROOMY = pltpu.CompilerParams(vmem_limit_bytes=24 * 1024 * 1024)


def cost(flops, moved):
    return pl.CostEstimate(flops=flops, bytes_accessed=4 * moved, transcendentals=0)


def place_of(device, n):
    blocks = n // 4
    return (device % 4) * blocks + (device // 4 + blocks // 2) % blocks


def turn_kernel(shift_ref, edge_ref, in_ref, out_ref):
    n, rows, width = in_ref.shape
    places = [place_of(block, n) for block in range(n)]
    per_block = width // LANES
    tiles = n * per_block
    groups = rows // TILE_ROWS
    halo_row = per_block * rows
    lane = lax.broadcasted_iota(jnp.int32, (TILE_ROWS, LANES), 1)
    for block in range(n):
        out_ref[block, halo_row : halo_row + TILE_ROWS, :] = edge_ref[...]

    def one_group(group):
        here = pl.ds(group * TILE_ROWS, TILE_ROWS)
        shift = shift_ref[here, :]
        cells = shift & (LANES - 1)
        whole = shift >> 7
        source = (lane - cells) & (LANES - 1)
        own = lane >= cells
        turned = []
        for tile in range(tiles):
            block, part = divmod(tile, per_block)
            values = in_ref[places[block], here, part * LANES : (part + 1) * LANES]
            turned.append(jnp.take_along_axis(values, source, axis=1, mode="promise_in_bounds"))
        circle = [jnp.where(own, turned[tile], turned[tile - 1]) for tile in range(tiles)]
        step = 1
        while step < tiles:
            wanted = (whole & step) != 0
            circle = [jnp.where(wanted, circle[(tile - step) % tiles], circle[tile]) for tile in range(tiles)]
            step *= 2
        for tile in range(tiles):
            block, part = divmod(tile, per_block)
            row = (group * per_block + part) * TILE_ROWS
            out_ref[places[block], pl.ds(row, TILE_ROWS), :] = circle[tile]
        place = group * 2
        edge = (lane == place) | (lane == place + 1)
        for block in range(n):
            left = circle[(block * per_block - 1) % tiles]
            right = circle[((block + 1) * per_block) % tiles]
            both = pltpu.roll(jnp.where(lane == 0, right, left), place + 1, 1)
            target = out_ref.at[places[block], halo_row : halo_row + TILE_ROWS, :]
            target[...] = jnp.where(edge, both, target[...])

    for group in range(groups):
        one_group(group)


def turn(shift_rows, edge_tile, gathered):
    n, rows, width = gathered.shape
    shape = (n, (width // LANES) * rows + TILE_ROWS, LANES)
    return pl.pallas_call(
        turn_kernel,
        out_shape=jax.ShapeDtypeStruct(shape, jnp.float32),
        in_specs=[IN_VMEM] * 3,
        out_specs=IN_VMEM,
        compiler_params=ROOMY,
        cost_estimate=cost(10 * gathered.size, 2 * gathered.size),
    )(shift_rows, edge_tile, gathered)


def spread_kernel(low_ref, high_ref, low_out, high_out):
    low_out[...] = jnp.broadcast_to(low_ref[...], low_out.shape)
    high_out[...] = jnp.broadcast_to(high_ref[...], high_out.shape)


def spread(low, high):
    shape = low.shape[:-1] + (LANES,)
    return pl.pallas_call(
        spread_kernel,
        out_shape=[jax.ShapeDtypeStruct(shape, jnp.float32)] * 2,
        in_specs=[IN_VMEM] * 2,
        out_specs=[IN_VMEM] * 2,
        compiler_params=ROOMY,
        cost_estimate=cost(low.size, 2 * low.size * LANES),
    )(low, high)


def carry_level(fields, level, recv_ref, speed_ref, back_ref, known, store):
    levels, radii, width = speed_ref.shape
    per_block = width // LANES
    in_rows = recv_ref.shape[1]
    halo_row = in_rows - TILE_ROWS
    groups = halo_row // (per_block * TILE_ROWS)
    lane = lax.broadcasted_iota(jnp.int32, (TILE_ROWS, LANES), 1)
    first = lane == 0
    last = lane == LANES - 1

    def edges(piece, group):
        key = (piece, group)
        if key not in known:
            known[key] = pltpu.roll(recv_ref[piece, halo_row:in_rows, :], (LANES - 2 * group) % LANES, 1)
        return known[key]

    for row in range(0, radii, TILE_ROWS):
        rates = []
        for part in range(per_block):
            cut = (level, slice(row, row + TILE_ROWS), slice(part * LANES, (part + 1) * LANES))
            speed = speed_ref[cut]
            back = back_ref[cut]
            rates.append(
                (
                    jnp.maximum(speed, 0.0),
                    jnp.minimum(speed, 0.0),
                    jnp.maximum(back, 0.0),
                    jnp.minimum(back, 0.0),
                )
            )
        for field in fields:
            piece, group = divmod(((field * levels + level) * radii + row) // TILE_ROWS, groups)
            values = []
            for part in range(per_block):
                at = (group * per_block + part) * TILE_ROWS
                values.append(recv_ref[piece, at : at + TILE_ROWS, :])
            up = [edges(piece, group)]
            up += [pltpu.roll(one, 1, 1) for one in values]
            down = [pltpu.roll(one, LANES - 1, 1) for one in values]
            down.append(edges(piece, group + 1))
            for part in range(per_block):
                here = values[part]
                behind = jnp.where(first, up[part], up[part + 1])
                ahead = jnp.where(last, down[part + 1], down[part])
                plus, minus, back_plus, back_minus = rates[part]
                outflow = plus * here + minus * ahead
                inflow = back_plus * behind + back_minus * here
                store(field, row, part * LANES, here - (outflow - inflow))


def energy_kernel(
    field, left_ref, recv_ref, speed_ref, inverse_ref, moved_ref, ends_ref, back_ref, columns
):
    levels, radii, width = speed_ref.shape
    in_rows = recv_ref.shape[1]
    tile = recv_ref[left_ref[0], in_rows - TILE_ROWS :, :]
    columns[...] = jnp.transpose(jnp.concatenate([tile] * (LANES // TILE_ROWS), axis=0))
    first = lax.broadcasted_iota(jnp.int32, (TILE_ROWS, LANES), 1) == 0
    known = {}
    for level in range(levels):
        for row in range(0, radii, TILE_ROWS):
            here = slice(row, row + TILE_ROWS)
            column = columns[LANES - radii + row : LANES - radii + row + TILE_ROWS, level : level + 1]
            before = jnp.broadcast_to(column, (TILE_ROWS, LANES))
            for cell in range(0, width, LANES):
                behind = pltpu.roll(speed_ref[level, here, cell : cell + LANES], 1, 1)
                back_ref[level, here, cell : cell + LANES] = jnp.where(first, before, behind)
                before = behind

        def store(_, row, cell, values, level=level):
            moved_ref[level, row : row + TILE_ROWS, cell : cell + LANES] = values

        carry_level([field], level, recv_ref, speed_ref, back_ref, known, store)
        outer = jnp.concatenate([inverse_ref[level, :TILE_ROWS], inverse_ref[level, radii - TILE_ROWS :]])
        ends = exact_product(outer, moved_ref[level])
        ends_ref[0, level : level + 1, :] = ends[:1]
        ends_ref[1, level : level + 1, :] = ends[-1:]


def exact_product(left, right):
    return jnp.dot(left, right, precision=lax.Precision.HIGHEST, preferred_element_type=jnp.float32)


def energy_part(field, left, received, speed, inverse):
    levels, radii, width = speed.shape
    plane = jax.ShapeDtypeStruct(speed.shape, jnp.float32)
    return pl.pallas_call(
        functools.partial(energy_kernel, field),
        out_shape=[plane, jax.ShapeDtypeStruct((2, levels, width), jnp.float32), plane],
        in_specs=[IN_SMEM] + [IN_VMEM] * 3,
        out_specs=[IN_VMEM] * 3,
        scratch_shapes=[pltpu.VMEM((LANES, LANES), jnp.float32)],
        compiler_params=ROOMY,
        cost_estimate=cost(60 * speed.size, 5 * speed.size),
    )(left, received, speed, inverse)


def carry_kernel(recv_ref, speed_ref, back_ref, inverse_ref, moved_ref, out_ref, local_ref, held, sems):
    nf, levels = held.shape[:2]
    copies = []
    known = {}
    for level in range(levels):
        local_ref[level] = exact_product(inverse_ref[level], moved_ref[level])

        def store(field, row, cell, values, level=level):
            held[field, level, row : row + TILE_ROWS, cell : cell + LANES] = values

        carry_level(range(nf), level, recv_ref, speed_ref, back_ref, known, store)
        copies.append(
            pltpu.make_async_copy(held.at[:, level], out_ref.at[pl.ds(0, nf), level], sems.at[level])
        )
        copies[-1].start()
    for copy in copies:
        copy.wait()


def carry(nf, count, received, speed, back_speed, inverse, moved):
    levels, radii, width = speed.shape
    return pl.pallas_call(
        carry_kernel,
        out_shape=[
            jax.ShapeDtypeStruct((nf,) + speed.shape, jnp.float32),
            jax.ShapeDtypeStruct(speed.shape, jnp.float32),
        ],
        in_specs=[IN_VMEM] * 5,
        out_specs=[IN_HBM, IN_VMEM],
        scratch_shapes=[
            pltpu.VMEM((count,) + speed.shape, jnp.float32),
            pltpu.SemaphoreType.DMA((levels,)),
        ],
        compiler_params=ROOMY,
        cost_estimate=cost(10 * count * speed.size, 2 * count * speed.size),
    )(received, speed, back_speed, inverse, moved)


def solve_interfaces(first_row, last_row, corner):
    bands = len(first_row)
    crossings = bands - 1
    nothing = jnp.zeros_like(first_row[0])
    carry_base = nothing
    carry_slope = jnp.zeros_like(corner[0][0])
    records = []
    for crossing in range(crossings):
        link = corner[crossing][4]
        steepness = link * corner[crossing][3]
        offset = last_row[crossing]
        if crossing > 0:
            back_link = corner[crossing - 1][4] * corner[crossing][2]
            steepness = back_link * carry_slope + steepness
            offset = offset + back_link * carry_base
        fore_link = link * corner[crossing + 1][0]
        next_link = jnp.zeros_like(link)
        if crossing + 1 < crossings:
            next_link = corner[crossing + 1][4] * corner[crossing + 1][1]
        denominator = 1.0 - fore_link * steepness
        upper_base = (first_row[crossing + 1] + fore_link * offset) / denominator
        upper_slope = next_link / denominator
        carry_base = offset + steepness * upper_base
        carry_slope = steepness * upper_slope
        records.append((carry_base, carry_slope, upper_base, upper_slope))
    lower_values = [nothing] * crossings
    upper_values = [nothing] * crossings
    follow = nothing
    for crossing in reversed(range(crossings)):
        carry_base, carry_slope, upper_base, upper_slope = records[crossing]
        lower_values[crossing] = carry_base + carry_slope * follow
        upper_values[crossing] = upper_base + upper_slope * follow
        follow = upper_values[crossing]
    return [nothing] + lower_values, upper_values + [nothing]


def finish_kernel(band_ref, corner_ref, local_ref, low_ref, high_ref, *refs):
    end_refs, (_, out_ref, held, sems) = refs[:-4], refs[-4:]
    levels, _, width = local_ref.shape
    bands = corner_ref.shape[1] // 5
    band = band_ref[0]
    if len(end_refs) == 2:
        own, other = end_refs
        ends = [
            [jnp.where(band == j, own[side], other[side]) for j in range(bands)] for side in range(2)
        ]
    else:
        ends = [[end_refs[0][j, side] for j in range(bands)] for side in range(2)]
    corner = [[corner_ref[:, j * 5 + c : j * 5 + c + 1] for c in range(5)] for j in range(bands)]
    all_before, all_beyond = solve_interfaces(ends[0], ends[1], corner)
    before = beyond = jnp.zeros_like(ends[0][0])
    for j in range(bands):
        before = jnp.where(band == j, all_before[j], before)
        beyond = jnp.where(band == j, all_beyond[j], beyond)
    copies = []
    for level in range(levels):
        for cell in range(0, width, LANES):
            cut = slice(cell, cell + LANES)
            held[level, :, cut] = (
                local_ref[level, :, cut]
                + low_ref[level] * before[level : level + 1, cut]
                + high_ref[level] * beyond[level : level + 1, cut]
            )
        copies.append(
            pltpu.make_async_copy(held.at[level], out_ref.at[out_ref.shape[0] - 1, level], sems.at[level])
        )
        copies[-1].start()
    for copy in copies:
        copy.wait()


def finish(band, corners, local_part, low, high, ends, result):
    levels = local_part.shape[0]
    return pl.pallas_call(
        finish_kernel,
        out_shape=jax.ShapeDtypeStruct(result.shape, jnp.float32),
        in_specs=[IN_SMEM] + [IN_VMEM] * (4 + len(ends)) + [IN_HBM],
        out_specs=IN_HBM,
        scratch_shapes=[pltpu.VMEM(local_part.shape, jnp.float32), pltpu.SemaphoreType.DMA((levels,))],
        input_output_aliases={5 + len(ends): 0},
        compiler_params=ROOMY,
        cost_estimate=cost(4 * local_part.size, 2 * local_part.size),
    )(band, corners, local_part, low, high, *ends, result)


def exchange(blocks):
    n = blocks.shape[0]
    order = sorted(range(n), key=lambda device: place_of(device, n))
    return lax.all_to_all(blocks, "az", split_axis=0, concat_axis=0, tiled=True, axis_index_groups=[order])


def per_device(fields, velocity, shifts, block_inverse, coupling):
    n = lax.axis_size("az")
    bands = lax.axis_size("rad")
    nf, levels, radii, width = fields.shape
    rows = nf * levels * radii // n
    me = lax.axis_index("az")
    band = lax.axis_index("rad")

    gathered = exchange(fields.reshape(n, rows, width))

    all_shifts = jnp.tile(shifts, rows // radii + 2)
    own_shifts = lax.dynamic_slice_in_dim(all_shifts, (place_of(me, n) * rows) % radii, rows)
    shift_rows = jnp.broadcast_to(own_shifts[:, None], (rows, LANES))
    edge_tile = jnp.pad(velocity[:, :, -1], ((0, 0), (LANES - radii, 0)))
    left_scalar = place_of((me + n - 1) % n, n)[None].astype(jnp.int32)
    corners = jnp.stack(
        [
            block_inverse[:, 0, 0],
            block_inverse[:, 0, -1],
            block_inverse[:, -1, 0],
            block_inverse[:, -1, -1],
            coupling[:, 0],
        ],
        axis=1,
    )
    all_corners = lax.all_gather(corners, "rad", axis=1, tiled=True)
    links = all_corners.reshape(levels, bands, 5)[:, :, 4]
    links_below = jnp.concatenate([jnp.zeros_like(links[:, :1]), links[:, :-1]], axis=1)
    link_below = lax.dynamic_index_in_dim(links_below, band, 1, keepdims=True)
    low, high = spread(
        (link_below * block_inverse[:, :, 0])[:, :, None], (coupling * block_inverse[:, :, -1])[:, :, None]
    )
    band_scalar = band[None].astype(jnp.int32)
    gathered, edge_tile, all_corners, low, high, band_scalar, left_scalar, shift_rows = lax.optimization_barrier(
        (gathered, edge_tile, all_corners, low, high, band_scalar, left_scalar, shift_rows)
    )

    received = exchange(turn(shift_rows, edge_tile, gathered))

    moved, ends, back_speed = energy_part(nf - 1, left_scalar, received, velocity, block_inverse)
    if bands == 2:
        all_ends = [ends, lax.ppermute(ends, "rad", [(0, 1), (1, 0)])]
    else:
        all_ends = [lax.all_gather(ends, "rad", axis=0)]
    result, local_part = carry(nf, nf - 1, received, velocity, back_speed, block_inverse, moved)
    return finish(band_scalar, all_corners, local_part, low, high, all_ends, result)


def solution(mesh):
    placed = (
        P(None, None, "rad", "az"),
        P(None, "rad", "az"),
        P("rad"),
        P(None, "rad", None),
        P(None, "rad"),
    )
    return jax.shard_map(
        per_device,
        mesh=mesh,
        in_specs=placed,
        out_specs=P(None, None, "rad", "az"),
        check_vma=False,
    )
```

```python
import functools

import jax
import jax.numpy as jnp
from jax import lax
from jax.experimental import pallas as pl
from jax.experimental.pallas import tpu as pltpu
from jax.sharding import PartitionSpec as P

LANES = 128
TILE_ROWS = 8
IN_VMEM = pl.BlockSpec(memory_space=pltpu.VMEM)
IN_HBM = pl.BlockSpec(memory_space=pltpu.HBM)
IN_SMEM = pl.BlockSpec(memory_space=pltpu.SMEM)
ROOMY = pltpu.CompilerParams(vmem_limit_bytes=24 * 1024 * 1024)


def cost(flops, moved):
    return pl.CostEstimate(flops=flops, bytes_accessed=4 * moved, transcendentals=0)


def place_of(device, n):
    return (device + n // 2) % n


def turn_kernel(shift_ref, edge_ref, in_ref, out_ref):
    n, rows, width = in_ref.shape
    places = [place_of(block, n) for block in range(n)]
    per_block = width // LANES
    tiles = n * per_block
    groups = rows // TILE_ROWS
    halo_row = per_block * rows
    lane = lax.broadcasted_iota(jnp.int32, (TILE_ROWS, LANES), 1)
    for block in range(n):
        out_ref[block, halo_row : halo_row + TILE_ROWS, :] = edge_ref[...]

    def one_group(group):
        here = pl.ds(group * TILE_ROWS, TILE_ROWS)
        shift = shift_ref[here, :]
        cells = shift & (LANES - 1)
        whole = shift >> 7
        source = (lane - cells) & (LANES - 1)
        own = lane >= cells
        turned = []
        for tile in range(tiles):
            block, part = divmod(tile, per_block)
            values = in_ref[places[block], here, part * LANES : (part + 1) * LANES]
            turned.append(jnp.take_along_axis(values, source, axis=1, mode="promise_in_bounds"))
        circle = [jnp.where(own, turned[tile], turned[tile - 1]) for tile in range(tiles)]
        step = 1
        while step < tiles:
            wanted = (whole & step) != 0
            circle = [jnp.where(wanted, circle[(tile - step) % tiles], circle[tile]) for tile in range(tiles)]
            step *= 2
        for tile in range(tiles):
            block, part = divmod(tile, per_block)
            row = (group * per_block + part) * TILE_ROWS
            out_ref[places[block], pl.ds(row, TILE_ROWS), :] = circle[tile]
        place = group * 2
        edge = (lane == place) | (lane == place + 1)
        for block in range(n):
            left = circle[(block * per_block - 1) % tiles]
            right = circle[((block + 1) * per_block) % tiles]
            both = pltpu.roll(jnp.where(lane == 0, right, left), place + 1, 1)
            target = out_ref.at[places[block], halo_row : halo_row + TILE_ROWS, :]
            target[...] = jnp.where(edge, both, target[...])

    for group in range(groups):
        one_group(group)


def turn(shift_rows, edge_tile, gathered):
    n, rows, width = gathered.shape
    shape = (n, (width // LANES) * rows + TILE_ROWS, LANES)
    return pl.pallas_call(
        turn_kernel,
        out_shape=jax.ShapeDtypeStruct(shape, jnp.float32),
        in_specs=[IN_VMEM] * 3,
        out_specs=IN_VMEM,
        compiler_params=ROOMY,
        cost_estimate=cost(10 * gathered.size, 2 * gathered.size),
    )(shift_rows, edge_tile, gathered)


def spread_kernel(low_ref, high_ref, speed_ref, low_out, high_out, back_out):
    low_out[...] = jnp.broadcast_to(low_ref[...], low_out.shape)
    high_out[...] = jnp.broadcast_to(high_ref[...], high_out.shape)
    levels, radii, width = speed_ref.shape
    first = lax.broadcasted_iota(jnp.int32, (TILE_ROWS, LANES), 1) == 0

    def one_level(level, _):
        for row in range(0, radii, TILE_ROWS):
            here = slice(row, row + TILE_ROWS)
            before = None
            for cell in range(0, width, LANES):
                behind = pltpu.roll(speed_ref[level, here, cell : cell + LANES], 1, 1)
                back_out[level, here, cell : cell + LANES] = (
                    behind if before is None else jnp.where(first, before, behind)
                )
                before = behind
        return 0

    lax.fori_loop(0, levels, one_level, 0)


def spread(low, high, speed):
    column = jax.ShapeDtypeStruct(low.shape[:-1] + (LANES,), jnp.float32)
    return pl.pallas_call(
        spread_kernel,
        out_shape=[column, column, jax.ShapeDtypeStruct(speed.shape, jnp.float32)],
        in_specs=[IN_VMEM] * 3,
        out_specs=[IN_VMEM] * 3,
        compiler_params=ROOMY,
        cost_estimate=cost(2 * speed.size, 3 * speed.size),
    )(low, high, speed)


def carry_level(fields, level, recv_ref, speed_ref, back_ref, known, store):
    levels, radii, width = speed_ref.shape
    per_block = width // LANES
    in_rows = recv_ref.shape[1]
    halo_row = in_rows - TILE_ROWS
    groups = halo_row // (per_block * TILE_ROWS)
    lane = lax.broadcasted_iota(jnp.int32, (TILE_ROWS, LANES), 1)
    first = lane == 0
    last = lane == LANES - 1

    def edges(piece, group):
        key = (piece, group)
        if key not in known:
            known[key] = pltpu.roll(recv_ref[piece, halo_row:in_rows, :], (LANES - 2 * group) % LANES, 1)
        return known[key]

    for row in range(0, radii, TILE_ROWS):
        rates = []
        for part in range(per_block):
            cut = (level, slice(row, row + TILE_ROWS), slice(part * LANES, (part + 1) * LANES))
            speed = speed_ref[cut]
            back = back_ref[cut]
            rates.append(
                (
                    jnp.maximum(speed, 0.0),
                    jnp.minimum(speed, 0.0),
                    jnp.maximum(back, 0.0),
                    jnp.minimum(back, 0.0),
                )
            )
        for field in fields:
            piece, group = divmod(((field * levels + level) * radii + row) // TILE_ROWS, groups)
            values = []
            for part in range(per_block):
                at = (group * per_block + part) * TILE_ROWS
                values.append(recv_ref[piece, at : at + TILE_ROWS, :])
            up = [edges(piece, group)]
            up += [pltpu.roll(one, 1, 1) for one in values]
            down = [pltpu.roll(one, LANES - 1, 1) for one in values]
            down.append(edges(piece, group + 1))
            for part in range(per_block):
                here = values[part]
                behind = jnp.where(first, up[part], up[part + 1])
                ahead = jnp.where(last, down[part + 1], down[part])
                plus, minus, back_plus, back_minus = rates[part]
                outflow = plus * here + minus * ahead
                inflow = back_plus * behind + back_minus * here
                store(field, row, part * LANES, here - (outflow - inflow))


def energy_kernel(
    field, left_ref, recv_ref, speed_ref, shifted_ref, inverse_ref, moved_ref, ends_ref, back_ref, columns
):
    levels, radii, width = speed_ref.shape
    in_rows = recv_ref.shape[1]
    tile = recv_ref[left_ref[0], in_rows - TILE_ROWS :, :]
    columns[...] = jnp.transpose(jnp.concatenate([tile] * (LANES // TILE_ROWS), axis=0))
    first = lax.broadcasted_iota(jnp.int32, (TILE_ROWS, LANES), 1) == 0
    known = {}
    for level in range(levels):
        for row in range(0, radii, TILE_ROWS):
            here = slice(row, row + TILE_ROWS)
            column = columns[LANES - radii + row : LANES - radii + row + TILE_ROWS, level : level + 1]
            before = jnp.broadcast_to(column, (TILE_ROWS, LANES))
            back_ref[level, here, :LANES] = jnp.where(first, before, shifted_ref[level, here, :LANES])
            for cell in range(LANES, width, LANES):
                back_ref[level, here, cell : cell + LANES] = shifted_ref[level, here, cell : cell + LANES]

        def store(_, row, cell, values, level=level):
            moved_ref[level, row : row + TILE_ROWS, cell : cell + LANES] = values

        carry_level([field], level, recv_ref, speed_ref, back_ref, known, store)
        outer = jnp.concatenate([inverse_ref[level, :TILE_ROWS], inverse_ref[level, radii - TILE_ROWS :]])
        ends = exact_product(outer, moved_ref[level])
        ends_ref[0, level : level + 1, :] = ends[:1]
        ends_ref[1, level : level + 1, :] = ends[-1:]


def exact_product(left, right):
    return jnp.dot(left, right, precision=lax.Precision.HIGHEST, preferred_element_type=jnp.float32)


def energy_part(field, left, received, speed, shifted, inverse):
    levels, radii, width = speed.shape
    plane = jax.ShapeDtypeStruct(speed.shape, jnp.float32)
    return pl.pallas_call(
        functools.partial(energy_kernel, field),
        out_shape=[plane, jax.ShapeDtypeStruct((2, levels, width), jnp.float32), plane],
        in_specs=[IN_SMEM] + [IN_VMEM] * 4,
        out_specs=[IN_VMEM] * 3,
        scratch_shapes=[pltpu.VMEM((LANES, LANES), jnp.float32)],
        compiler_params=ROOMY,
        cost_estimate=cost(60 * speed.size, 5 * speed.size),
    )(left, received, speed, shifted, inverse)


def carry_kernel(recv_ref, speed_ref, back_ref, inverse_ref, moved_ref, out_ref, local_ref, held, sems):
    nf, levels = held.shape[:2]
    copies = []
    known = {}
    for level in range(levels):
        local_ref[level] = exact_product(inverse_ref[level], moved_ref[level])

        def store(field, row, cell, values, level=level):
            held[field, level, row : row + TILE_ROWS, cell : cell + LANES] = values

        carry_level(range(nf), level, recv_ref, speed_ref, back_ref, known, store)
        copies.append(
            pltpu.make_async_copy(held.at[:, level], out_ref.at[pl.ds(0, nf), level], sems.at[level])
        )
        copies[-1].start()
    for copy in copies:
        copy.wait()


def carry(nf, count, received, speed, back_speed, inverse, moved):
    levels, radii, width = speed.shape
    return pl.pallas_call(
        carry_kernel,
        out_shape=[
            jax.ShapeDtypeStruct((nf,) + speed.shape, jnp.float32),
            jax.ShapeDtypeStruct(speed.shape, jnp.float32),
        ],
        in_specs=[IN_VMEM] * 5,
        out_specs=[IN_HBM, IN_VMEM],
        scratch_shapes=[
            pltpu.VMEM((count,) + speed.shape, jnp.float32),
            pltpu.SemaphoreType.DMA((levels,)),
        ],
        compiler_params=ROOMY,
        cost_estimate=cost(10 * count * speed.size, 2 * count * speed.size),
    )(received, speed, back_speed, inverse, moved)


def solve_interfaces(first_row, last_row, corner):
    bands = len(first_row)
    crossings = bands - 1
    nothing = jnp.zeros_like(first_row[0])
    carry_base = nothing
    carry_slope = jnp.zeros_like(corner[0][0])
    records = []
    for crossing in range(crossings):
        link = corner[crossing][4]
        steepness = link * corner[crossing][3]
        offset = last_row[crossing]
        if crossing > 0:
            back_link = corner[crossing - 1][4] * corner[crossing][2]
            steepness = back_link * carry_slope + steepness
            offset = offset + back_link * carry_base
        fore_link = link * corner[crossing + 1][0]
        next_link = jnp.zeros_like(link)
        if crossing + 1 < crossings:
            next_link = corner[crossing + 1][4] * corner[crossing + 1][1]
        denominator = 1.0 - fore_link * steepness
        upper_base = (first_row[crossing + 1] + fore_link * offset) / denominator
        upper_slope = next_link / denominator
        carry_base = offset + steepness * upper_base
        carry_slope = steepness * upper_slope
        records.append((carry_base, carry_slope, upper_base, upper_slope))
    lower_values = [nothing] * crossings
    upper_values = [nothing] * crossings
    follow = nothing
    for crossing in reversed(range(crossings)):
        carry_base, carry_slope, upper_base, upper_slope = records[crossing]
        lower_values[crossing] = carry_base + carry_slope * follow
        upper_values[crossing] = upper_base + upper_slope * follow
        follow = upper_values[crossing]
    return [nothing] + lower_values, upper_values + [nothing]


def finish_kernel(band_ref, corner_ref, local_ref, low_ref, high_ref, *refs):
    end_refs, (_, out_ref, held, sems) = refs[:-4], refs[-4:]
    levels, _, width = local_ref.shape
    bands = corner_ref.shape[1] // 5
    band = band_ref[0]
    if len(end_refs) == 2:
        own, other = end_refs
        ends = [
            [jnp.where(band == j, own[side], other[side]) for j in range(bands)] for side in range(2)
        ]
    else:
        ends = [[end_refs[0][j, side] for j in range(bands)] for side in range(2)]
    corner = [[corner_ref[:, j * 5 + c : j * 5 + c + 1] for c in range(5)] for j in range(bands)]
    all_before, all_beyond = solve_interfaces(ends[0], ends[1], corner)
    before = beyond = jnp.zeros_like(ends[0][0])
    for j in range(bands):
        before = jnp.where(band == j, all_before[j], before)
        beyond = jnp.where(band == j, all_beyond[j], beyond)
    copies = []
    for level in range(levels):
        for cell in range(0, width, LANES):
            cut = slice(cell, cell + LANES)
            held[level, :, cut] = (
                local_ref[level, :, cut]
                + low_ref[level] * before[level : level + 1, cut]
                + high_ref[level] * beyond[level : level + 1, cut]
            )
        copies.append(
            pltpu.make_async_copy(held.at[level], out_ref.at[out_ref.shape[0] - 1, level], sems.at[level])
        )
        copies[-1].start()
    for copy in copies:
        copy.wait()


def finish(band, corners, local_part, low, high, ends, result):
    levels = local_part.shape[0]
    return pl.pallas_call(
        finish_kernel,
        out_shape=jax.ShapeDtypeStruct(result.shape, jnp.float32),
        in_specs=[IN_SMEM] + [IN_VMEM] * (4 + len(ends)) + [IN_HBM],
        out_specs=IN_HBM,
        scratch_shapes=[pltpu.VMEM(local_part.shape, jnp.float32), pltpu.SemaphoreType.DMA((levels,))],
        input_output_aliases={5 + len(ends): 0},
        compiler_params=ROOMY,
        cost_estimate=cost(4 * local_part.size, 2 * local_part.size),
    )(band, corners, local_part, low, high, *ends, result)


def exchange(blocks):
    n = blocks.shape[0]
    order = sorted(range(n), key=lambda device: place_of(device, n))
    return lax.all_to_all(blocks, "az", split_axis=0, concat_axis=0, tiled=True, axis_index_groups=[order])


def per_device(fields, velocity, shifts, block_inverse, coupling):
    n = lax.axis_size("az")
    bands = lax.axis_size("rad")
    nf, levels, radii, width = fields.shape
    rows = nf * levels * radii // n
    me = lax.axis_index("az")
    band = lax.axis_index("rad")

    gathered = exchange(fields.reshape(n, rows, width))

    all_shifts = jnp.tile(shifts, rows // radii + 2)
    own_shifts = lax.dynamic_slice_in_dim(all_shifts, (place_of(me, n) * rows) % radii, rows)
    shift_rows = jnp.broadcast_to(own_shifts[:, None], (rows, LANES))
    edge_tile = jnp.pad(velocity[:, :, -1], ((0, 0), (LANES - radii, 0)))
    left_scalar = place_of((me + n - 1) % n, n)[None].astype(jnp.int32)
    corners = jnp.stack(
        [
            block_inverse[:, 0, 0],
            block_inverse[:, 0, -1],
            block_inverse[:, -1, 0],
            block_inverse[:, -1, -1],
            coupling[:, 0],
        ],
        axis=1,
    )
    all_corners = lax.all_gather(corners, "rad", axis=1, tiled=True)
    links = all_corners.reshape(levels, bands, 5)[:, :, 4]
    links_below = jnp.concatenate([jnp.zeros_like(links[:, :1]), links[:, :-1]], axis=1)
    link_below = lax.dynamic_index_in_dim(links_below, band, 1, keepdims=True)
    low, high, shifted = spread(
        (link_below * block_inverse[:, :, 0])[:, :, None],
        (coupling * block_inverse[:, :, -1])[:, :, None],
        velocity,
    )
    band_scalar = band[None].astype(jnp.int32)
    gathered, edge_tile, shifted, all_corners, low, high, band_scalar, left_scalar, shift_rows = (
        lax.optimization_barrier(
            (gathered, edge_tile, shifted, all_corners, low, high, band_scalar, left_scalar, shift_rows)
        )
    )

    received = exchange(turn(shift_rows, edge_tile, gathered))

    moved, ends, back_speed = energy_part(
        nf - 1, left_scalar, received, velocity, shifted, block_inverse
    )
    if bands == 2:
        all_ends = [ends, lax.ppermute(ends, "rad", [(0, 1), (1, 0)])]
    else:
        all_ends = [lax.all_gather(ends, "rad", axis=0)]
    result, local_part = carry(nf, nf - 1, received, velocity, back_speed, block_inverse, moved)
    return finish(band_scalar, all_corners, local_part, low, high, all_ends, result)


def solution(mesh):
    placed = (
        P(None, None, "rad", "az"),
        P(None, "rad", "az"),
        P("rad"),
        P(None, "rad", None),
        P(None, "rad"),
    )
    return jax.shard_map(
        per_device,
        mesh=mesh,
        in_specs=placed,
        out_specs=P(None, None, "rad", "az"),
        check_vma=False,
    )
```

```python
import functools

import jax
import jax.numpy as jnp
from jax import lax
from jax.experimental import pallas as pl
from jax.experimental.pallas import tpu as pltpu
from jax.sharding import PartitionSpec as P

LANES = 128
TILE_ROWS = 8
IN_VMEM = pl.BlockSpec(memory_space=pltpu.VMEM)
IN_HBM = pl.BlockSpec(memory_space=pltpu.HBM)
IN_SMEM = pl.BlockSpec(memory_space=pltpu.SMEM)
ROOMY = pltpu.CompilerParams(vmem_limit_bytes=24 * 1024 * 1024)


def cost(flops, moved):
    return pl.CostEstimate(flops=flops, bytes_accessed=4 * moved, transcendentals=0)


def place_of(device, n):
    return (device + n // 2) % n


def turn_kernel(shift_ref, edge_ref, in_ref, out_ref):
    n, rows, width = in_ref.shape
    places = [place_of(block, n) for block in range(n)]
    per_block = width // LANES
    tiles = n * per_block
    groups = rows // TILE_ROWS
    halo_row = per_block * rows
    lane = lax.broadcasted_iota(jnp.int32, (TILE_ROWS, LANES), 1)
    for block in range(n):
        out_ref[block, halo_row : halo_row + TILE_ROWS, :] = edge_ref[...]

    def one_group(group):
        here = pl.ds(group * TILE_ROWS, TILE_ROWS)
        shift = shift_ref[here, :]
        cells = shift & (LANES - 1)
        whole = shift >> 7
        source = (lane - cells) & (LANES - 1)
        stays = lane < LANES - cells
        circle = []
        for tile in range(tiles):
            block, part = divmod(tile, per_block)
            circle.append(in_ref[places[block], here, part * LANES : (part + 1) * LANES])
        step = 1
        while step < tiles:
            wanted = (whole & step) != 0
            circle = [jnp.where(wanted, circle[(tile - step) % tiles], circle[tile]) for tile in range(tiles)]
            step *= 2
        joined = [jnp.where(stays, circle[tile], circle[tile - 1]) for tile in range(tiles)]
        circle = [jnp.take_along_axis(one, source, axis=1, mode="promise_in_bounds") for one in joined]
        for tile in range(tiles):
            block, part = divmod(tile, per_block)
            row = (group * per_block + part) * TILE_ROWS
            out_ref[places[block], pl.ds(row, TILE_ROWS), :] = circle[tile]
        place = group * 2
        edge = (lane == place) | (lane == place + 1)
        for block in range(n):
            left = circle[(block * per_block - 1) % tiles]
            right = circle[((block + 1) * per_block) % tiles]
            both = pltpu.roll(jnp.where(lane == 0, right, left), place + 1, 1)
            target = out_ref.at[places[block], halo_row : halo_row + TILE_ROWS, :]
            target[...] = jnp.where(edge, both, target[...])

    for group in range(groups):
        one_group(group)


def turn(shift_rows, edge_tile, gathered):
    n, rows, width = gathered.shape
    shape = (n, (width // LANES) * rows + TILE_ROWS, LANES)
    return pl.pallas_call(
        turn_kernel,
        out_shape=jax.ShapeDtypeStruct(shape, jnp.float32),
        in_specs=[IN_VMEM] * 3,
        out_specs=IN_VMEM,
        compiler_params=ROOMY,
        cost_estimate=cost(10 * gathered.size, 2 * gathered.size),
    )(shift_rows, edge_tile, gathered)


def spread_kernel(low_ref, high_ref, speed_ref, low_out, high_out, back_out):
    low_out[...] = jnp.broadcast_to(low_ref[...], low_out.shape)
    high_out[...] = jnp.broadcast_to(high_ref[...], high_out.shape)
    levels, radii, width = speed_ref.shape
    first = lax.broadcasted_iota(jnp.int32, (TILE_ROWS, LANES), 1) == 0

    def one_level(level, _):
        for row in range(0, radii, TILE_ROWS):
            here = slice(row, row + TILE_ROWS)
            before = None
            for cell in range(0, width, LANES):
                behind = pltpu.roll(speed_ref[level, here, cell : cell + LANES], 1, 1)
                back_out[level, here, cell : cell + LANES] = (
                    behind if before is None else jnp.where(first, before, behind)
                )
                before = behind
        return 0

    lax.fori_loop(0, levels, one_level, 0)


def spread(low, high, speed):
    column = jax.ShapeDtypeStruct(low.shape[:-1] + (LANES,), jnp.float32)
    return pl.pallas_call(
        spread_kernel,
        out_shape=[column, column, jax.ShapeDtypeStruct(speed.shape, jnp.float32)],
        in_specs=[IN_VMEM] * 3,
        out_specs=[IN_VMEM] * 3,
        compiler_params=ROOMY,
        cost_estimate=cost(2 * speed.size, 3 * speed.size),
    )(low, high, speed)


def carry_level(fields, level, recv_ref, speed_ref, back_ref, known, store):
    levels, radii, width = speed_ref.shape
    per_block = width // LANES
    in_rows = recv_ref.shape[1]
    halo_row = in_rows - TILE_ROWS
    groups = halo_row // (per_block * TILE_ROWS)
    lane = lax.broadcasted_iota(jnp.int32, (TILE_ROWS, LANES), 1)
    first = lane == 0
    last = lane == LANES - 1

    def edges(piece, group):
        key = (piece, group)
        if key not in known:
            known[key] = pltpu.roll(recv_ref[piece, halo_row:in_rows, :], (LANES - 2 * group) % LANES, 1)
        return known[key]

    for row in range(0, radii, TILE_ROWS):
        rates = []
        for part in range(per_block):
            cut = (level, slice(row, row + TILE_ROWS), slice(part * LANES, (part + 1) * LANES))
            speed = speed_ref[cut]
            back = back_ref[cut]
            rates.append(
                (
                    jnp.maximum(speed, 0.0),
                    jnp.minimum(speed, 0.0),
                    jnp.maximum(back, 0.0),
                    jnp.minimum(back, 0.0),
                )
            )
        for field in fields:
            piece, group = divmod(((field * levels + level) * radii + row) // TILE_ROWS, groups)
            values = []
            for part in range(per_block):
                at = (group * per_block + part) * TILE_ROWS
                values.append(recv_ref[piece, at : at + TILE_ROWS, :])
            up = [edges(piece, group)]
            up += [pltpu.roll(one, 1, 1) for one in values]
            down = [pltpu.roll(one, LANES - 1, 1) for one in values]
            down.append(edges(piece, group + 1))
            for part in range(per_block):
                here = values[part]
                behind = jnp.where(first, up[part], up[part + 1])
                ahead = jnp.where(last, down[part + 1], down[part])
                plus, minus, back_plus, back_minus = rates[part]
                outflow = plus * here + minus * ahead
                inflow = back_plus * behind + back_minus * here
                store(field, row, part * LANES, here - (outflow - inflow))


def energy_kernel(
    field, left_ref, recv_ref, speed_ref, shifted_ref, inverse_ref, moved_ref, ends_ref, back_ref, columns
):
    levels, radii, width = speed_ref.shape
    in_rows = recv_ref.shape[1]
    tile = recv_ref[left_ref[0], in_rows - TILE_ROWS :, :]
    columns[...] = jnp.transpose(jnp.concatenate([tile] * (LANES // TILE_ROWS), axis=0))
    first = lax.broadcasted_iota(jnp.int32, (TILE_ROWS, LANES), 1) == 0
    known = {}
    for level in range(levels):
        for row in range(0, radii, TILE_ROWS):
            here = slice(row, row + TILE_ROWS)
            column = columns[LANES - radii + row : LANES - radii + row + TILE_ROWS, level : level + 1]
            before = jnp.broadcast_to(column, (TILE_ROWS, LANES))
            back_ref[level, here, :LANES] = jnp.where(first, before, shifted_ref[level, here, :LANES])
            for cell in range(LANES, width, LANES):
                back_ref[level, here, cell : cell + LANES] = shifted_ref[level, here, cell : cell + LANES]

        def store(_, row, cell, values, level=level):
            moved_ref[level, row : row + TILE_ROWS, cell : cell + LANES] = values

        carry_level([field], level, recv_ref, speed_ref, back_ref, known, store)
        outer = jnp.concatenate([inverse_ref[level, :TILE_ROWS], inverse_ref[level, radii - TILE_ROWS :]])
        ends = exact_product(outer, moved_ref[level])
        ends_ref[0, level : level + 1, :] = ends[:1]
        ends_ref[1, level : level + 1, :] = ends[-1:]


def exact_product(left, right):
    return jnp.dot(left, right, precision=lax.Precision.HIGHEST, preferred_element_type=jnp.float32)


def energy_part(field, left, received, speed, shifted, inverse):
    levels, radii, width = speed.shape
    plane = jax.ShapeDtypeStruct(speed.shape, jnp.float32)
    return pl.pallas_call(
        functools.partial(energy_kernel, field),
        out_shape=[plane, jax.ShapeDtypeStruct((2, levels, width), jnp.float32), plane],
        in_specs=[IN_SMEM] + [IN_VMEM] * 4,
        out_specs=[IN_VMEM] * 3,
        scratch_shapes=[pltpu.VMEM((LANES, LANES), jnp.float32)],
        compiler_params=ROOMY,
        cost_estimate=cost(60 * speed.size, 5 * speed.size),
    )(left, received, speed, shifted, inverse)


def carry_kernel(recv_ref, speed_ref, back_ref, inverse_ref, moved_ref, out_ref, local_ref, held, sems):
    nf, levels = held.shape[:2]
    copies = []
    known = {}
    for level in range(levels):
        local_ref[level] = exact_product(inverse_ref[level], moved_ref[level])

        def store(field, row, cell, values, level=level):
            held[field, level, row : row + TILE_ROWS, cell : cell + LANES] = values

        carry_level(range(nf), level, recv_ref, speed_ref, back_ref, known, store)
        copies.append(
            pltpu.make_async_copy(held.at[:, level], out_ref.at[pl.ds(0, nf), level], sems.at[level])
        )
        copies[-1].start()
    for copy in copies:
        copy.wait()


def carry(nf, count, received, speed, back_speed, inverse, moved):
    levels, radii, width = speed.shape
    return pl.pallas_call(
        carry_kernel,
        out_shape=[
            jax.ShapeDtypeStruct((nf,) + speed.shape, jnp.float32),
            jax.ShapeDtypeStruct(speed.shape, jnp.float32),
        ],
        in_specs=[IN_VMEM] * 5,
        out_specs=[IN_HBM, IN_VMEM],
        scratch_shapes=[
            pltpu.VMEM((count,) + speed.shape, jnp.float32),
            pltpu.SemaphoreType.DMA((levels,)),
        ],
        compiler_params=ROOMY,
        cost_estimate=cost(10 * count * speed.size, 2 * count * speed.size),
    )(received, speed, back_speed, inverse, moved)


def solve_interfaces(first_row, last_row, corner):
    bands = len(first_row)
    crossings = bands - 1
    nothing = jnp.zeros_like(first_row[0])
    carry_base = nothing
    carry_slope = jnp.zeros_like(corner[0][0])
    records = []
    for crossing in range(crossings):
        link = corner[crossing][4]
        steepness = link * corner[crossing][3]
        offset = last_row[crossing]
        if crossing > 0:
            back_link = corner[crossing - 1][4] * corner[crossing][2]
            steepness = back_link * carry_slope + steepness
            offset = offset + back_link * carry_base
        fore_link = link * corner[crossing + 1][0]
        next_link = jnp.zeros_like(link)
        if crossing + 1 < crossings:
            next_link = corner[crossing + 1][4] * corner[crossing + 1][1]
        denominator = 1.0 - fore_link * steepness
        upper_base = (first_row[crossing + 1] + fore_link * offset) / denominator
        upper_slope = next_link / denominator
        carry_base = offset + steepness * upper_base
        carry_slope = steepness * upper_slope
        records.append((carry_base, carry_slope, upper_base, upper_slope))
    lower_values = [nothing] * crossings
    upper_values = [nothing] * crossings
    follow = nothing
    for crossing in reversed(range(crossings)):
        carry_base, carry_slope, upper_base, upper_slope = records[crossing]
        lower_values[crossing] = carry_base + carry_slope * follow
        upper_values[crossing] = upper_base + upper_slope * follow
        follow = upper_values[crossing]
    return [nothing] + lower_values, upper_values + [nothing]


def finish_kernel(band_ref, corner_ref, local_ref, low_ref, high_ref, *refs):
    end_refs, (_, out_ref, held, sems) = refs[:-4], refs[-4:]
    levels, _, width = local_ref.shape
    bands = corner_ref.shape[1] // 5
    band = band_ref[0]
    if len(end_refs) == 2:
        own, other = end_refs
        ends = [
            [jnp.where(band == j, own[side], other[side]) for j in range(bands)] for side in range(2)
        ]
    else:
        ends = [[end_refs[0][j, side] for j in range(bands)] for side in range(2)]
    corner = [[corner_ref[:, j * 5 + c : j * 5 + c + 1] for c in range(5)] for j in range(bands)]
    all_before, all_beyond = solve_interfaces(ends[0], ends[1], corner)
    before = beyond = jnp.zeros_like(ends[0][0])
    for j in range(bands):
        before = jnp.where(band == j, all_before[j], before)
        beyond = jnp.where(band == j, all_beyond[j], beyond)
    copies = []
    for level in range(levels):
        for cell in range(0, width, LANES):
            cut = slice(cell, cell + LANES)
            held[level, :, cut] = (
                local_ref[level, :, cut]
                + low_ref[level] * before[level : level + 1, cut]
                + high_ref[level] * beyond[level : level + 1, cut]
            )
        copies.append(
            pltpu.make_async_copy(held.at[level], out_ref.at[out_ref.shape[0] - 1, level], sems.at[level])
        )
        copies[-1].start()
    for copy in copies:
        copy.wait()


def finish(band, corners, local_part, low, high, ends, result):
    levels = local_part.shape[0]
    return pl.pallas_call(
        finish_kernel,
        out_shape=jax.ShapeDtypeStruct(result.shape, jnp.float32),
        in_specs=[IN_SMEM] + [IN_VMEM] * (4 + len(ends)) + [IN_HBM],
        out_specs=IN_HBM,
        scratch_shapes=[pltpu.VMEM(local_part.shape, jnp.float32), pltpu.SemaphoreType.DMA((levels,))],
        input_output_aliases={5 + len(ends): 0},
        compiler_params=ROOMY,
        cost_estimate=cost(4 * local_part.size, 2 * local_part.size),
    )(band, corners, local_part, low, high, *ends, result)


def exchange(blocks):
    n = blocks.shape[0]
    order = sorted(range(n), key=lambda device: place_of(device, n))
    return lax.all_to_all(blocks, "az", split_axis=0, concat_axis=0, tiled=True, axis_index_groups=[order])


def per_device(fields, velocity, shifts, block_inverse, coupling):
    n = lax.axis_size("az")
    bands = lax.axis_size("rad")
    nf, levels, radii, width = fields.shape
    rows = nf * levels * radii // n
    me = lax.axis_index("az")
    band = lax.axis_index("rad")

    gathered = exchange(fields.reshape(n, rows, width))

    all_shifts = jnp.tile(shifts, rows // radii + 2)
    own_shifts = lax.dynamic_slice_in_dim(all_shifts, (place_of(me, n) * rows) % radii, rows)
    shift_rows = jnp.broadcast_to(own_shifts[:, None], (rows, LANES))
    edge_tile = jnp.pad(velocity[:, :, -1], ((0, 0), (LANES - radii, 0)))
    left_scalar = place_of((me + n - 1) % n, n)[None].astype(jnp.int32)
    corners = jnp.stack(
        [
            block_inverse[:, 0, 0],
            block_inverse[:, 0, -1],
            block_inverse[:, -1, 0],
            block_inverse[:, -1, -1],
            coupling[:, 0],
        ],
        axis=1,
    )
    all_corners = lax.all_gather(corners, "rad", axis=1, tiled=True)
    links = all_corners.reshape(levels, bands, 5)[:, :, 4]
    links_below = jnp.concatenate([jnp.zeros_like(links[:, :1]), links[:, :-1]], axis=1)
    link_below = lax.dynamic_index_in_dim(links_below, band, 1, keepdims=True)
    low, high, shifted = spread(
        (link_below * block_inverse[:, :, 0])[:, :, None],
        (coupling * block_inverse[:, :, -1])[:, :, None],
        velocity,
    )
    band_scalar = band[None].astype(jnp.int32)
    gathered, edge_tile, shifted, all_corners, low, high, band_scalar, left_scalar, shift_rows = (
        lax.optimization_barrier(
            (gathered, edge_tile, shifted, all_corners, low, high, band_scalar, left_scalar, shift_rows)
        )
    )

    received = exchange(turn(shift_rows, edge_tile, gathered))

    moved, ends, back_speed = energy_part(
        nf - 1, left_scalar, received, velocity, shifted, block_inverse
    )
    if bands == 2:
        all_ends = [ends, lax.ppermute(ends, "rad", [(0, 1), (1, 0)])]
    else:
        all_ends = [lax.all_gather(ends, "rad", axis=0)]
    result, local_part = carry(nf, nf - 1, received, velocity, back_speed, block_inverse, moved)
    return finish(band_scalar, all_corners, local_part, low, high, all_ends, result)


def solution(mesh):
    placed = (
        P(None, None, "rad", "az"),
        P(None, "rad", "az"),
        P("rad"),
        P(None, "rad", None),
        P(None, "rad"),
    )
    return jax.shard_map(
        per_device,
        mesh=mesh,
        in_specs=placed,
        out_specs=P(None, None, "rad", "az"),
        check_vma=False,
    )
```

```python
import functools

import jax
import jax.numpy as jnp
from jax import lax
from jax.experimental import pallas as pl
from jax.experimental.pallas import tpu as pltpu
from jax.sharding import PartitionSpec as P

LANES = 128
TILE_ROWS = 8
IN_VMEM = pl.BlockSpec(memory_space=pltpu.VMEM)
IN_HBM = pl.BlockSpec(memory_space=pltpu.HBM)
IN_SMEM = pl.BlockSpec(memory_space=pltpu.SMEM)
ROOMY = pltpu.CompilerParams(vmem_limit_bytes=24 * 1024 * 1024)


def cost(flops, moved):
    return pl.CostEstimate(flops=flops, bytes_accessed=4 * moved, transcendentals=0)


def place_of(device, n):
    blocks = n // 4
    return (device % 4) * blocks + (device // 4 + blocks // 2) % blocks


def turn_kernel(shift_ref, edge_ref, in_ref, out_ref):
    n, rows, width = in_ref.shape
    places = [place_of(block, n) for block in range(n)]
    per_block = width // LANES
    tiles = n * per_block
    groups = rows // TILE_ROWS
    halo_row = per_block * rows
    lane = lax.broadcasted_iota(jnp.int32, (TILE_ROWS, LANES), 1)
    for block in range(n):
        out_ref[block, halo_row : halo_row + TILE_ROWS, :] = edge_ref[...]

    def one_group(group):
        here = pl.ds(group * TILE_ROWS, TILE_ROWS)
        shift = shift_ref[here, :]
        cells = shift & (LANES - 1)
        whole = shift >> 7
        source = (lane - cells) & (LANES - 1)
        stays = lane < LANES - cells
        circle = []
        for tile in range(tiles):
            block, part = divmod(tile, per_block)
            circle.append(in_ref[places[block], here, part * LANES : (part + 1) * LANES])
        step = 1
        while step < tiles:
            wanted = (whole & step) != 0
            circle = [jnp.where(wanted, circle[(tile - step) % tiles], circle[tile]) for tile in range(tiles)]
            step *= 2
        joined = [jnp.where(stays, circle[tile], circle[tile - 1]) for tile in range(tiles)]
        circle = [jnp.take_along_axis(one, source, axis=1, mode="promise_in_bounds") for one in joined]
        for tile in range(tiles):
            block, part = divmod(tile, per_block)
            row = (group * per_block + part) * TILE_ROWS
            out_ref[places[block], pl.ds(row, TILE_ROWS), :] = circle[tile]
        place = group * 2
        edge = (lane == place) | (lane == place + 1)
        for block in range(n):
            left = circle[(block * per_block - 1) % tiles]
            right = circle[((block + 1) * per_block) % tiles]
            both = pltpu.roll(jnp.where(lane == 0, right, left), place + 1, 1)
            target = out_ref.at[places[block], halo_row : halo_row + TILE_ROWS, :]
            target[...] = jnp.where(edge, both, target[...])

    for group in range(groups):
        one_group(group)


def turn(shift_rows, edge_tile, gathered):
    n, rows, width = gathered.shape
    shape = (n, (width // LANES) * rows + TILE_ROWS, LANES)
    return pl.pallas_call(
        turn_kernel,
        out_shape=jax.ShapeDtypeStruct(shape, jnp.float32),
        in_specs=[IN_VMEM] * 3,
        out_specs=IN_VMEM,
        compiler_params=ROOMY,
        cost_estimate=cost(10 * gathered.size, 2 * gathered.size),
    )(shift_rows, edge_tile, gathered)


def spread_kernel(low_ref, high_ref, speed_ref, low_out, high_out, back_out):
    low_out[...] = jnp.broadcast_to(low_ref[...], low_out.shape)
    high_out[...] = jnp.broadcast_to(high_ref[...], high_out.shape)
    levels, radii, width = speed_ref.shape
    first = lax.broadcasted_iota(jnp.int32, (TILE_ROWS, LANES), 1) == 0

    def one_level(level, _):
        for row in range(0, radii, TILE_ROWS):
            here = slice(row, row + TILE_ROWS)
            before = None
            for cell in range(0, width, LANES):
                behind = pltpu.roll(speed_ref[level, here, cell : cell + LANES], 1, 1)
                back_out[level, here, cell : cell + LANES] = (
                    behind if before is None else jnp.where(first, before, behind)
                )
                before = behind
        return 0

    lax.fori_loop(0, levels, one_level, 0)


def spread(low, high, speed):
    column = jax.ShapeDtypeStruct(low.shape[:-1] + (LANES,), jnp.float32)
    return pl.pallas_call(
        spread_kernel,
        out_shape=[column, column, jax.ShapeDtypeStruct(speed.shape, jnp.float32)],
        in_specs=[IN_VMEM] * 3,
        out_specs=[IN_VMEM] * 3,
        compiler_params=ROOMY,
        cost_estimate=cost(2 * speed.size, 3 * speed.size),
    )(low, high, speed)


def carry_level(fields, level, recv_ref, speed_ref, back_ref, known, store):
    levels, radii, width = speed_ref.shape
    per_block = width // LANES
    in_rows = recv_ref.shape[1]
    halo_row = in_rows - TILE_ROWS
    groups = halo_row // (per_block * TILE_ROWS)
    lane = lax.broadcasted_iota(jnp.int32, (TILE_ROWS, LANES), 1)
    first = lane == 0
    last = lane == LANES - 1

    def edges(piece, group):
        key = (piece, group)
        if key not in known:
            known[key] = pltpu.roll(recv_ref[piece, halo_row:in_rows, :], (LANES - 2 * group) % LANES, 1)
        return known[key]

    for row in range(0, radii, TILE_ROWS):
        rates = []
        for part in range(per_block):
            cut = (level, slice(row, row + TILE_ROWS), slice(part * LANES, (part + 1) * LANES))
            speed = speed_ref[cut]
            back = back_ref[cut]
            rates.append(
                (
                    jnp.maximum(speed, 0.0),
                    jnp.minimum(speed, 0.0),
                    jnp.maximum(back, 0.0),
                    jnp.minimum(back, 0.0),
                )
            )
        for field in fields:
            piece, group = divmod(((field * levels + level) * radii + row) // TILE_ROWS, groups)
            values = []
            for part in range(per_block):
                at = (group * per_block + part) * TILE_ROWS
                values.append(recv_ref[piece, at : at + TILE_ROWS, :])
            up = [edges(piece, group)]
            up += [pltpu.roll(one, 1, 1) for one in values]
            down = [pltpu.roll(one, LANES - 1, 1) for one in values]
            down.append(edges(piece, group + 1))
            for part in range(per_block):
                here = values[part]
                behind = jnp.where(first, up[part], up[part + 1])
                ahead = jnp.where(last, down[part + 1], down[part])
                plus, minus, back_plus, back_minus = rates[part]
                outflow = plus * here + minus * ahead
                inflow = back_plus * behind + back_minus * here
                store(field, row, part * LANES, here - (outflow - inflow))


def energy_kernel(
    field, left_ref, recv_ref, speed_ref, shifted_ref, inverse_ref, moved_ref, ends_ref, back_ref, columns
):
    levels, radii, width = speed_ref.shape
    in_rows = recv_ref.shape[1]
    tile = recv_ref[left_ref[0], in_rows - TILE_ROWS :, :]
    columns[...] = jnp.transpose(jnp.concatenate([tile] * (LANES // TILE_ROWS), axis=0))
    first = lax.broadcasted_iota(jnp.int32, (TILE_ROWS, LANES), 1) == 0
    known = {}
    for level in range(levels):
        for row in range(0, radii, TILE_ROWS):
            here = slice(row, row + TILE_ROWS)
            column = columns[LANES - radii + row : LANES - radii + row + TILE_ROWS, level : level + 1]
            before = jnp.broadcast_to(column, (TILE_ROWS, LANES))
            back_ref[level, here, :LANES] = jnp.where(first, before, shifted_ref[level, here, :LANES])
            for cell in range(LANES, width, LANES):
                back_ref[level, here, cell : cell + LANES] = shifted_ref[level, here, cell : cell + LANES]

        def store(_, row, cell, values, level=level):
            moved_ref[level, row : row + TILE_ROWS, cell : cell + LANES] = values

        carry_level([field], level, recv_ref, speed_ref, back_ref, known, store)
        outer = jnp.concatenate([inverse_ref[level, :TILE_ROWS], inverse_ref[level, radii - TILE_ROWS :]])
        ends = exact_product(outer, moved_ref[level])
        ends_ref[0, level : level + 1, :] = ends[:1]
        ends_ref[1, level : level + 1, :] = ends[-1:]


def exact_product(left, right):
    return jnp.dot(left, right, precision=lax.Precision.HIGHEST, preferred_element_type=jnp.float32)


def energy_part(field, left, received, speed, shifted, inverse):
    levels, radii, width = speed.shape
    plane = jax.ShapeDtypeStruct(speed.shape, jnp.float32)
    return pl.pallas_call(
        functools.partial(energy_kernel, field),
        out_shape=[plane, jax.ShapeDtypeStruct((2, levels, width), jnp.float32), plane],
        in_specs=[IN_SMEM] + [IN_VMEM] * 4,
        out_specs=[IN_VMEM] * 3,
        scratch_shapes=[pltpu.VMEM((LANES, LANES), jnp.float32)],
        compiler_params=ROOMY,
        cost_estimate=cost(60 * speed.size, 5 * speed.size),
    )(left, received, speed, shifted, inverse)


def carry_kernel(recv_ref, speed_ref, back_ref, inverse_ref, moved_ref, out_ref, local_ref, held, sems):
    nf, levels = held.shape[:2]
    copies = []
    known = {}
    for level in range(levels):
        local_ref[level] = exact_product(inverse_ref[level], moved_ref[level])

        def store(field, row, cell, values, level=level):
            held[field, level, row : row + TILE_ROWS, cell : cell + LANES] = values

        carry_level(range(nf), level, recv_ref, speed_ref, back_ref, known, store)
        copies.append(
            pltpu.make_async_copy(held.at[:, level], out_ref.at[pl.ds(0, nf), level], sems.at[level])
        )
        copies[-1].start()
    for copy in copies:
        copy.wait()


def carry(nf, count, received, speed, back_speed, inverse, moved):
    levels, radii, width = speed.shape
    return pl.pallas_call(
        carry_kernel,
        out_shape=[
            jax.ShapeDtypeStruct((nf,) + speed.shape, jnp.float32),
            jax.ShapeDtypeStruct(speed.shape, jnp.float32),
        ],
        in_specs=[IN_VMEM] * 5,
        out_specs=[IN_HBM, IN_VMEM],
        scratch_shapes=[
            pltpu.VMEM((count,) + speed.shape, jnp.float32),
            pltpu.SemaphoreType.DMA((levels,)),
        ],
        compiler_params=ROOMY,
        cost_estimate=cost(10 * count * speed.size, 2 * count * speed.size),
    )(received, speed, back_speed, inverse, moved)


def solve_interfaces(first_row, last_row, corner):
    bands = len(first_row)
    crossings = bands - 1
    nothing = jnp.zeros_like(first_row[0])
    carry_base = nothing
    carry_slope = jnp.zeros_like(corner[0][0])
    records = []
    for crossing in range(crossings):
        link = corner[crossing][4]
        steepness = link * corner[crossing][3]
        offset = last_row[crossing]
        if crossing > 0:
            back_link = corner[crossing - 1][4] * corner[crossing][2]
            steepness = back_link * carry_slope + steepness
            offset = offset + back_link * carry_base
        fore_link = link * corner[crossing + 1][0]
        next_link = jnp.zeros_like(link)
        if crossing + 1 < crossings:
            next_link = corner[crossing + 1][4] * corner[crossing + 1][1]
        denominator = 1.0 - fore_link * steepness
        upper_base = (first_row[crossing + 1] + fore_link * offset) / denominator
        upper_slope = next_link / denominator
        carry_base = offset + steepness * upper_base
        carry_slope = steepness * upper_slope
        records.append((carry_base, carry_slope, upper_base, upper_slope))
    lower_values = [nothing] * crossings
    upper_values = [nothing] * crossings
    follow = nothing
    for crossing in reversed(range(crossings)):
        carry_base, carry_slope, upper_base, upper_slope = records[crossing]
        lower_values[crossing] = carry_base + carry_slope * follow
        upper_values[crossing] = upper_base + upper_slope * follow
        follow = upper_values[crossing]
    return [nothing] + lower_values, upper_values + [nothing]


def finish_kernel(band_ref, corner_ref, local_ref, low_ref, high_ref, *refs):
    end_refs, (_, out_ref, held, sems) = refs[:-4], refs[-4:]
    levels, _, width = local_ref.shape
    bands = corner_ref.shape[1] // 5
    band = band_ref[0]
    if len(end_refs) == 2:
        own, other = end_refs
        ends = [
            [jnp.where(band == j, own[side], other[side]) for j in range(bands)] for side in range(2)
        ]
    else:
        ends = [[end_refs[0][j, side] for j in range(bands)] for side in range(2)]
    corner = [[corner_ref[:, j * 5 + c : j * 5 + c + 1] for c in range(5)] for j in range(bands)]
    all_before, all_beyond = solve_interfaces(ends[0], ends[1], corner)
    before = beyond = jnp.zeros_like(ends[0][0])
    for j in range(bands):
        before = jnp.where(band == j, all_before[j], before)
        beyond = jnp.where(band == j, all_beyond[j], beyond)
    copies = []
    for level in range(levels):
        for cell in range(0, width, LANES):
            cut = slice(cell, cell + LANES)
            held[level, :, cut] = (
                local_ref[level, :, cut]
                + low_ref[level] * before[level : level + 1, cut]
                + high_ref[level] * beyond[level : level + 1, cut]
            )
        copies.append(
            pltpu.make_async_copy(held.at[level], out_ref.at[out_ref.shape[0] - 1, level], sems.at[level])
        )
        copies[-1].start()
    for copy in copies:
        copy.wait()


def finish(band, corners, local_part, low, high, ends, result):
    levels = local_part.shape[0]
    return pl.pallas_call(
        finish_kernel,
        out_shape=jax.ShapeDtypeStruct(result.shape, jnp.float32),
        in_specs=[IN_SMEM] + [IN_VMEM] * (4 + len(ends)) + [IN_HBM],
        out_specs=IN_HBM,
        scratch_shapes=[pltpu.VMEM(local_part.shape, jnp.float32), pltpu.SemaphoreType.DMA((levels,))],
        input_output_aliases={5 + len(ends): 0},
        compiler_params=ROOMY,
        cost_estimate=cost(4 * local_part.size, 2 * local_part.size),
    )(band, corners, local_part, low, high, *ends, result)


def exchange(blocks):
    n = blocks.shape[0]
    order = sorted(range(n), key=lambda device: place_of(device, n))
    return lax.all_to_all(blocks, "az", split_axis=0, concat_axis=0, tiled=True, axis_index_groups=[order])


def per_device(fields, velocity, shifts, block_inverse, coupling):
    n = lax.axis_size("az")
    bands = lax.axis_size("rad")
    nf, levels, radii, width = fields.shape
    rows = nf * levels * radii // n
    me = lax.axis_index("az")
    band = lax.axis_index("rad")

    gathered = exchange(fields.reshape(n, rows, width))

    all_shifts = jnp.tile(shifts, rows // radii + 2)
    own_shifts = lax.dynamic_slice_in_dim(all_shifts, (place_of(me, n) * rows) % radii, rows)
    shift_rows = jnp.broadcast_to(own_shifts[:, None], (rows, LANES))
    edge_tile = jnp.pad(velocity[:, :, -1], ((0, 0), (LANES - radii, 0)))
    left_scalar = place_of((me + n - 1) % n, n)[None].astype(jnp.int32)
    corners = jnp.stack(
        [
            block_inverse[:, 0, 0],
            block_inverse[:, 0, -1],
            block_inverse[:, -1, 0],
            block_inverse[:, -1, -1],
            coupling[:, 0],
        ],
        axis=1,
    )
    all_corners = lax.all_gather(corners, "rad", axis=1, tiled=True)
    links = all_corners.reshape(levels, bands, 5)[:, :, 4]
    links_below = jnp.concatenate([jnp.zeros_like(links[:, :1]), links[:, :-1]], axis=1)
    link_below = lax.dynamic_index_in_dim(links_below, band, 1, keepdims=True)
    low, high, shifted = spread(
        (link_below * block_inverse[:, :, 0])[:, :, None],
        (coupling * block_inverse[:, :, -1])[:, :, None],
        velocity,
    )
    band_scalar = band[None].astype(jnp.int32)
    gathered, edge_tile, shifted, all_corners, low, high, band_scalar, left_scalar, shift_rows = (
        lax.optimization_barrier(
            (gathered, edge_tile, shifted, all_corners, low, high, band_scalar, left_scalar, shift_rows)
        )
    )

    received = exchange(turn(shift_rows, edge_tile, gathered))

    moved, ends, back_speed = energy_part(
        nf - 1, left_scalar, received, velocity, shifted, block_inverse
    )
    if bands == 2:
        all_ends = [ends, lax.ppermute(ends, "rad", [(0, 1), (1, 0)])]
    else:
        all_ends = [lax.all_gather(ends, "rad", axis=0)]
    result, local_part = carry(nf, nf - 1, received, velocity, back_speed, block_inverse, moved)
    return finish(band_scalar, all_corners, local_part, low, high, all_ends, result)


def solution(mesh):
    placed = (
        P(None, None, "rad", "az"),
        P(None, "rad", "az"),
        P("rad"),
        P(None, "rad", None),
        P(None, "rad"),
    )
    return jax.shard_map(
        per_device,
        mesh=mesh,
        in_specs=placed,
        out_specs=P(None, None, "rad", "az"),
        check_vma=False,
    )
```
